32 devices in a mesh: space: 4 (over z), orb: 8 (over y, x, core).
Axes of the slice: x: 2, y: 2, z: 4, core: 2. Of those that a mesh axis runs over, the one named last changes fastest.
Arguments:
- orbitals: bfloat16 [128, 40, 1600], P(('space', 'orb')), may hold values from -6 to 6
- box_offset: int32 [128, 3], replicated, may hold values from 0 to 79, as said below
- send_index: int32 [32, 2, 8], P(('space', 'orb')), may hold values from 0 to 3
- pair_left: int32 [32, 2, 8], P(('space', 'orb')), may hold values from 0 to 3
Outputs:
- exchange_field: float32 [128, 40, 1600], P(('space', 'orb'))
The draws below stay inside these ranges and needn't reach their ends.
Inputs may be any that keep to these rules, and one draw needn't show every extreme that they name: `box_offset`: box corners are cell coordinates on the periodic grid of 80 cells a side.
All inputs are finite; a program needn't handle non-finite values.
Results may differ from the reference program's by a relative error of at most 0.0008.
Values may be sent and summed in bfloat16 or wider, within the bound.
No kernel may reach another device: no remote copies, remote signals or barrier semaphores. Data moves between devices by JAX's collectives and lax.ppermute only.
A program may use at most 128 MiB of HBM per device.

```python
import jax
import jax.numpy as jnp
from jax import lax

B = 40
ORB_DEV = 4
ITERS = 4
G = 80
NORB = 128
N_SPACE = 4
N_ORB = 8
DEVICES = 32


def draw_box_offset(key, part):
    key = jax.random.fold_in(key, 11)
    slab_cells = B // 2
    orbital_count = ORB_DEV * N_SPACE * N_ORB
    flat_key, rise_key = jax.random.split(key)
    owner_space = jnp.arange(orbital_count, dtype=jnp.int32) // (ORB_DEV * N_ORB)
    planar = jax.random.randint(flat_key, (orbital_count, 2), 0, B, dtype=jnp.int32)
    height_jitter = jax.random.randint(rise_key, (orbital_count,), -(slab_cells // 2) + 1, slab_cells // 2 + 1, dtype=jnp.int32)
    height_jitter = height_jitter.at[0].set(-1)
    planar = planar.at[0, 0].set(0)
    height = (owner_space * slab_cells + height_jitter) % (N_SPACE * slab_cells)
    return jnp.concatenate([planar, height[:, None]], axis=1)


def with_ends(entries, stream_key, low, high):
    shape = entries.shape
    place = [jax.random.randint(jax.random.fold_in(stream_key, axis), (), 0, shape[axis]) for axis in range(len(shape))]
    entries = entries.at[tuple(place)].set(low)
    longest = shape.index(max(shape))
    place[longest] = (place[longest] + 1) % shape[longest]
    return entries.at[tuple(place)].set(high)


def steps_of(stream_key, shape, cuts, least, top_value):
    def one(position, blocks):
        draws = jax.random.uniform(jax.random.fold_in(jax.random.fold_in(stream_key, 6), position), (blocks,), jnp.float32, least / len(cuts), top_value / len(cuts))
        return jnp.repeat(jnp.exp(draws), shape[position] // blocks).reshape((-1,) + (1,) * (len(shape) - position - 1))

    level = one(*cuts[0])
    for cut in cuts[1:]:
        level = level * one(*cut)
    return level


def normal_values(rng, dims, width, limit, shards=(), kind=jnp.bfloat16):
    array = width * jax.random.normal(rng, dims, jnp.float32)
    if shards:
        array = array * steps_of(rng, dims, shards, -0.22, 0.18)
    return jnp.clip(array, -limit, limit).astype(kind)


def setup_inputs(seed: int = 0) -> dict:
    key_of = jax.random.split(jax.random.key(seed), 5)
    return {
        "orbitals": normal_values(key_of[0], (NORB, B, B * B), 1.0, 6.0, ((0, 32),)),
        "box_offset": draw_box_offset(jax.random.fold_in(key_of[4], 71), 0),
        "send_index": with_ends(jax.random.randint(key_of[2], (DEVICES, 2, N_ORB), 0, ORB_DEV), jax.random.fold_in(key_of[2], 1), 0, ORB_DEV - 1).astype(jnp.int32),
        "pair_left": with_ends(jax.random.randint(key_of[3], (DEVICES, 2, N_ORB), 0, ORB_DEV), jax.random.fold_in(key_of[3], 1), 0, ORB_DEV - 1).astype(jnp.int32),
    }


screen_shift = 0.25
reference_block = 32


def apply_operator(values, box_side):
    row_pad = jnp.pad(values, ((0, 0), (1, 1), (0, 0)))
    summed = row_pad[:, 2:, :] + row_pad[:, :-2, :]
    flat_pad = jnp.pad(values, ((0, 0), (0, 0), (box_side, box_side)))
    summed = summed + flat_pad[:, :, 2 * box_side:] + flat_pad[:, :, :-2 * box_side]
    inner_pad = jnp.pad(values, ((0, 0), (0, 0), (1, 1)))
    column = lax.broadcasted_iota(jnp.int32, (1, 1, box_side * box_side), 2) % box_side
    next_cell = jnp.where(column < box_side - 1, inner_pad[:, :, 2:], 0.0)
    earlier = jnp.where(column > 0, inner_pad[:, :, :-2], 0.0)
    return (6.0 + screen_shift) * values - summed - next_cell - earlier


def solve_poisson(density, box_side):
    solution = jnp.zeros_like(density)
    residual = density
    direction = density
    norm_now = jnp.sum(residual * residual, axis=(1, 2), keepdims=True)
    for turn_index in range(ITERS):
        applied = apply_operator(direction, box_side)
        step_len = norm_now / jnp.sum(direction * applied, axis=(1, 2), keepdims=True)
        solution = solution + step_len * direction
        residual = residual - step_len * applied
        norm_next = jnp.sum(residual * residual, axis=(1, 2), keepdims=True)
        direction = residual + (norm_next / norm_now) * direction
        norm_now = norm_next
    return solution


def displace(box_values, displacement, box_side):
    half_side = box_side // 2
    flat_reach = half_side * box_side + half_side
    padded = jnp.pad(box_values, ((half_side, half_side), (flat_reach, flat_reach)))
    start_row = (half_side - displacement[0]).astype(jnp.int32)
    start_col = (flat_reach - (displacement[1] * box_side + displacement[2])).astype(jnp.int32)
    moved = lax.dynamic_slice(padded, (start_row, start_col), (box_side, box_side * box_side))
    column = lax.broadcasted_iota(jnp.int32, (1, box_side * box_side), 1) % box_side
    source_col = column - displacement[2].astype(jnp.int32)
    keep = (source_col >= 0) & (source_col < box_side)
    return jnp.where(keep, moved, jnp.zeros((), moved.dtype))


def pair_geometry(left_offset, right_offset, grid_cells, box_side):
    raw_gap = (right_offset - left_offset + grid_cells // 2) % grid_cells - grid_cells // 2
    displacement = jnp.clip(raw_gap, -(box_side // 2), box_side // 2)
    live_flag = jnp.all(raw_gap == displacement, axis=-1).astype(jnp.int32)
    return displacement, live_flag


def pair_terms(left_boxes, right_boxes, displacement, live_flag, box_side):
    shifted = jax.vmap(displace, in_axes=(0, 0, None))(right_boxes, displacement, box_side)
    shifted_wide = shifted.astype(jnp.float32)
    left_wide = left_boxes.astype(jnp.float32)
    potential = solve_poisson(left_wide * shifted_wide, box_side)
    weight = live_flag.astype(jnp.float32)[:, None, None]
    near_term = weight * potential * shifted_wide
    product = potential * left_wide
    far_term = weight * jax.vmap(displace, in_axes=(0, 0, None))(product, -displacement, box_side)
    return near_term, far_term


def reference(orbitals, box_offset, send_index, pair_left):
    box_side = B
    device = jnp.arange(DEVICES, dtype=jnp.int32)
    space_pos = device // N_ORB
    orb_pos = device % N_ORB
    group_offset = jnp.arange(2, dtype=jnp.int32)
    source_orb = jnp.arange(N_ORB, dtype=jnp.int32)
    left_index = device[:, None, None] * ORB_DEV + pair_left
    source = ((space_pos[:, None, None] + group_offset[None, :, None]) % N_SPACE) * N_ORB + source_orb[None, None, :]
    chosen = send_index[source, jnp.broadcast_to(group_offset[None, :, None], source.shape), jnp.broadcast_to(orb_pos[:, None, None], source.shape)]
    right_index = (source * ORB_DEV + chosen).reshape(-1)
    left_index = left_index.reshape(-1)
    displacement, live_flag = pair_geometry(box_offset[left_index], box_offset[right_index], G, box_side)
    block_count = left_index.shape[0] // reference_block
    block_data = (left_index.reshape(block_count, reference_block),
                  right_index.reshape(block_count, reference_block),
                  displacement.reshape(block_count, reference_block, 3),
                  live_flag.reshape(block_count, reference_block))

    def add_block(values, pieces):
        left_rows, right_rows, block_disp, block_live = pieces
        near_term, far_term = pair_terms(orbitals[left_rows], orbitals[right_rows], block_disp, block_live, box_side)
        values = values.at[left_rows].add(near_term).at[right_rows].add(far_term)
        return values, None

    start_values = jnp.zeros(orbitals.shape, jnp.float32)
    exchange_field, unused = lax.scan(add_block, start_values, block_data)
    return exchange_field
```

```python
import functools

import jax
import jax.numpy as jnp
from jax import lax
from jax.experimental import pallas as pl
from jax.experimental.pallas import tpu as pltpu
from jax.sharding import PartitionSpec as P

B = 40
ITERS = 4
SCREEN = 0.25

GROUPS = 3
TILES = 14
LANES = 128
USED = GROUPS * B
BATCH = 8
PLANE = TILES * BATCH
PLANES = B + 2
MARGIN = 24
ROWS = B + 2 * MARGIN
HALF = B // 2
VMEM_BYTES = 44 * 2**20


def lanes_of(shape):
    return lax.broadcasted_iota(jnp.int32, shape, len(shape) - 1)


def overlaps():
    pieces = []
    for b in range(B):
        group = b // TILES
        for flat in range(b * B // LANES, (b * B + B - 1) // LANES + 1):
            pieces.append((b, flat, b * B - flat * LANES - group * B))
    return pieces


def pack_body(box_ref, table_ref, out_ref):
    count = box_ref.shape[0]
    lane = lanes_of((B, LANES))
    for n in range(count):
        tiles = [jnp.zeros((B, LANES), jnp.float32) for _ in range(TILES)]
        loaded = {}
        for b, flat, shift in overlaps():
            if flat not in loaded:
                width = min(LANES, B * B - flat * LANES)
                part = box_ref[n, :, flat * LANES : flat * LANES + width].astype(jnp.float32)
                if width < LANES:
                    part = jnp.concatenate(
                        [part, jnp.zeros((B, LANES - width), jnp.float32)], axis=1
                    )
                loaded[flat] = part
            first = max(b * B, flat * LANES) - b * B + (b // TILES) * B
            last = min(b * B + B, flat * LANES + LANES) - b * B + (b // TILES) * B
            moved = pltpu.roll(loaded[flat], (-shift) % LANES, axis=1)
            keep = (lane >= first) & (lane < last)
            tiles[b % TILES] = jnp.where(keep, moved, tiles[b % TILES])
        if n == 0:
            tiles[0] = tiles[0] + table_ref[...]
        for t in range(TILES):
            out_ref[n, t] = tiles[t].astype(out_ref.dtype)


def pack(orbitals, table):
    count = orbitals.shape[0]
    return pl.pallas_call(
        pack_body,
        out_shape=jax.ShapeDtypeStruct((count, TILES, B, LANES), jnp.bfloat16),
        in_specs=[pl.BlockSpec(memory_space=pltpu.VMEM)] * 2,
        out_specs=pl.BlockSpec(memory_space=pltpu.VMEM),
        compiler_params=pltpu.CompilerParams(vmem_limit_bytes=VMEM_BYTES),
        name="pack",
    )(orbitals, table)


def finish_body(count, slots, field_ref, near_ref, far_ref, row_ref, out_ref, total):
    lane = lanes_of((B, LANES))
    for n in range(count):
        for t in range(TILES):
            total[n, t] = field_ref[n, t] + far_ref[n, t].astype(jnp.float32)

    def add(j, carry):
        row = row_ref[j]
        for t in range(TILES):
            total[row, t] += near_ref[j, t].astype(jnp.float32)
        return carry

    lax.fori_loop(0, slots, add, 0)
    for n in range(count):
        flats = {}
        for b, flat, shift in overlaps():
            first = max(b * B, flat * LANES) - flat * LANES
            last = min(b * B + B, flat * LANES + LANES) - flat * LANES
            moved = pltpu.roll(total[n, b % TILES], shift % LANES, axis=1)
            keep = (lane >= first) & (lane < last)
            before = flats.get(flat)
            flats[flat] = moved if before is None else jnp.where(keep, moved, before)
        for flat, value in flats.items():
            width = min(LANES, B * B - flat * LANES)
            out_ref[n, :, flat * LANES : flat * LANES + width] = value[:, :width]


def finish(field, near, far, rows):
    count, slots = field.shape[0], near.shape[0]
    vmem = pl.BlockSpec(memory_space=pltpu.VMEM)
    return pl.pallas_call(
        functools.partial(finish_body, count, slots),
        out_shape=jax.ShapeDtypeStruct((count, B, B * B), jnp.float32),
        in_specs=[vmem, vmem, vmem, pl.BlockSpec(memory_space=pltpu.SMEM)],
        out_specs=vmem,
        scratch_shapes=[pltpu.VMEM((count, TILES, B, LANES), jnp.float32)],
        compiler_params=pltpu.CompilerParams(vmem_limit_bytes=VMEM_BYTES),
        name="finish",
    )(field, near, far, rows)


def geometry(offset_ref, left, right, grid_cells):
    shift, live = [], jnp.int32(1)
    for axis in range(3):
        gap = offset_ref[3 * right + axis] - offset_ref[3 * left + axis]
        raw = lax.rem(gap + grid_cells // 2 + grid_cells, grid_cells) - grid_cells // 2
        clipped = jnp.clip(raw, -HALF, HALF)
        live = jnp.where(raw == clipped, live, 0)
        shift.append(clipped)
    return shift, live


def displaced(pad_ref, shift):
    lane = lanes_of((1, LANES))
    group = lane // B
    source_col = lane - group * B - shift[2]
    col_ok = (source_col >= 0) & (source_col < B) & (lane < USED)
    for t in range(TILES):
        index = t - shift[1] + 2 * TILES
        turn = index // TILES - 2
        source = index - (turn + 2) * TILES
        row = TILES * group + t
        source_row = row - shift[1]
        keep = col_ok & (source_row >= 0) & (source_row < B) & (row < B)
        block = pad_ref[source, pl.ds(MARGIN - shift[0], B), :]
        amount = lax.rem(shift[2] - B * turn + 2 * LANES, LANES)
        moved = pltpu.roll(block, amount, axis=1)
        yield t, moved * keep.astype(jnp.float32)


def lockstep(ref, plane, tile):
    return ref[pl.ds(pl.multiple_of(plane * PLANE + tile * BATCH, BATCH), BATCH), :]


def put_lockstep(ref, plane, tile, value):
    ref[pl.ds(pl.multiple_of(plane * PLANE + tile * BATCH, BATCH), BATCH), :] = value


def tree_sum(values):
    while len(values) > 1:
        paired = [a + b for a, b in zip(values[::2], values[1::2])]
        values = paired + ([values[-1]] if len(values) % 2 else [])
    return values[0]


def spread(total):
    return jnp.broadcast_to(jnp.sum(total, axis=1, keepdims=True), (BATCH, LANES))


def solve(directions, residual, image):
    lane = lanes_of((BATCH, LANES))
    column = lane % B
    has_before = (column > 0) & (lane < USED)
    has_after = (column < B - 1) & (lane < USED)
    not_first = lane >= B
    not_last = lane < USED - B
    zero = jnp.zeros((BATCH, LANES), jnp.float32)

    def operator(above, here, below):
        result = []
        for t in range(TILES):
            if t == 0:
                before = jnp.where(not_first, pltpu.roll(here[TILES - 1], B, axis=1), 0.0)
            else:
                before = here[t - 1]
            if t == TILES - 1:
                after = jnp.where(not_last, pltpu.roll(here[0], LANES - B, axis=1), 0.0)
            else:
                after = here[t + 1]
            prior = jnp.where(has_before, pltpu.roll(here[t], 1, axis=1), 0.0)
            following = jnp.where(has_after, pltpu.roll(here[t], LANES - 1, axis=1), 0.0)
            around = (above[t] + below[t]) + (before + after) + (prior + following)
            value = (6.0 + SCREEN) * here[t] - around
            if t == B - TILES * (GROUPS - 1):
                value = jnp.where(not_last, value, 0.0)
            result.append(value)
        return result

    norm = None
    ratio = None
    steps = []
    for k in range(ITERS):
        current = directions[k]
        last = k == ITERS - 1

        def fetch(plane, k=k, ratio=ratio):
            if k == 0:
                return [lockstep(directions[0], plane, t) for t in range(TILES)]
            values = []
            for t in range(TILES):
                value = lockstep(residual, plane, t) + ratio * lockstep(
                    directions[k - 1], plane, t
                )
                put_lockstep(directions[k], plane, t, value)
                values.append(value)
            return values

        def stencil(a, carry, k=k, last=last, fetch=fetch):
            products, squares, above, here = carry
            below = fetch(a + 2)
            applied = operator(above, here, below)
            if not last:
                for t in range(TILES):
                    put_lockstep(image, a + 1, t, applied[t])
            products = products + tree_sum([x * y for x, y in zip(here, applied)])
            if k == 0:
                squares = squares + tree_sum([x * x for x in here])
            return products, squares, here, below

        products, squares, _, _ = lax.fori_loop(
            0, B, stencil, (zero, zero, [zero] * TILES, fetch(1))
        )
        if k == 0:
            norm = spread(squares)
        step = norm / spread(products)
        steps.append(step)
        if last:
            break
        source = directions[0] if k == 0 else residual

        def reduce(a, squares, step=step, source=source):
            values = []
            for t in range(TILES):
                value = lockstep(source, a + 1, t) - step * lockstep(image, a + 1, t)
                put_lockstep(residual, a + 1, t, value)
                values.append(value)
            return squares + tree_sum([x * x for x in values])

        new_norm = spread(lax.fori_loop(0, B, reduce, zero))
        ratio = new_norm / norm
        norm = new_norm

    def combine(a, carry):
        for t in range(TILES):
            parts = [s * lockstep(d, a + 1, t) for s, d in zip(steps, directions)]
            put_lockstep(image, a + 1, t, tree_sum(parts))
        return carry

    lax.fori_loop(0, B, combine, 0)


def clear_edges(refs, pad):
    zero = jnp.zeros((PLANE, LANES), jnp.float32)
    for ref in refs:
        ref[0:PLANE, :] = zero
        ref[(PLANES - 1) * PLANE : PLANES * PLANE, :] = zero
    rim = jnp.zeros((TILES, MARGIN, LANES), jnp.float32)
    pad[:, 0:MARGIN, :] = rim
    pad[:, MARGIN + B : ROWS, :] = rim


def run_batch(slot_of, left_at, right_at, near_to, far_to, scratch):
    shifted, pad, residual, image, *directions = scratch

    def load(j, carry):
        shift, live = slot_of(j)

        @pl.when(live == 1)
        def _():
            for t in range(TILES):
                pad[t, MARGIN : MARGIN + B, :] = right_at(j, t)
            for t, moved in displaced(pad, shift):
                shifted[j, t] = moved
                density = moved * left_at(j, t)
                for k in range(B // 8):
                    start = (8 * k + 1) * PLANE + t * BATCH + j
                    directions[0][pl.ds(start, 8, stride=PLANE), :] = density[8 * k : 8 * k + 8]

        return carry

    lax.fori_loop(0, BATCH, load, 0)
    solve(directions, residual, image)

    def unload(j, carry):
        shift, live = slot_of(j)

        @pl.when(live == 1)
        def _():
            for t in range(TILES):
                rows = []
                for k in range(B // 8):
                    start = (8 * k + 1) * PLANE + t * BATCH + j
                    rows.append(image[pl.ds(start, 8, stride=PLANE), :])
                potential = jnp.concatenate(rows, axis=0)
                if near_to is not None:
                    near_to(j, t, potential * shifted[j, t])
                if far_to is not None:
                    pad[t, MARGIN : MARGIN + B, :] = potential * left_at(j, t)
            if far_to is not None:
                for t, moved in displaced(pad, [-s for s in shift]):
                    far_to(j, t, moved)

        if near_to is not None:
            near_to(j, None, live)
        return carry

    lax.fori_loop(0, BATCH, unload, 0)


def batch_scratch():
    lock = pltpu.VMEM((PLANES * PLANE, LANES), jnp.float32)
    return [
        pltpu.VMEM((BATCH, TILES, B, LANES), jnp.float32),
        pltpu.VMEM((TILES, ROWS, LANES), jnp.float32),
    ] + [lock] * (2 + ITERS)


def clear_lockstep(ref):
    def one(a, carry):
        ref[pl.ds(pl.multiple_of(a * PLANE, PLANE), PLANE), :] = jnp.zeros(
            (PLANE, LANES), jnp.float32
        )
        return carry

    lax.fori_loop(0, PLANES, one, 0)


def forward_body(
    count, grid_cells, where_ref, offset_ref, left_ref, right_ref, boxes, incoming,
    near_ref, far_ref, far_sum, *scratch,
):
    slots = near_ref.shape[0]
    first_left, first_right = where_ref[0], where_ref[1]
    clear_edges(scratch[2:], scratch[1])
    clear_lockstep(scratch[4])
    for n in range(count):
        for t in range(TILES):
            far_sum[n, t] = jnp.zeros((B, LANES), jnp.float32)

    def batch(i, carry):
        def rows(j):
            return (i * BATCH + j) * count + left_ref[i * BATCH + j], right_ref[i * BATCH + j]

        def slot_of(j):
            left, right = rows(j)
            return geometry(offset_ref, first_left + left, first_right + right, grid_cells)

        def near_to(j, t, value):
            if t is not None:
                near_ref[i * BATCH + j, t] = value.astype(near_ref.dtype)
            else:

                @pl.when(value == 0)
                def _():
                    near_ref[i * BATCH + j] = jnp.zeros((TILES, B, LANES), near_ref.dtype)

        def far_to(j, t, value):
            far_sum[rows(j)[1], t] += value

        run_batch(
            slot_of,
            lambda j, t: boxes[rows(j)[0], t].astype(jnp.float32),
            lambda j, t: incoming[rows(j)[1], t].astype(jnp.float32),
            near_to, far_to, scratch,
        )
        return carry

    lax.fori_loop(0, slots // BATCH, batch, 0)
    for n in range(count):
        for t in range(TILES):
            far_ref[n, t] = far_sum[n, t].astype(far_ref.dtype)


def forward_pairs(where, offsets, left, right, boxes, incoming, grid_cells):
    slots, count = left.shape[0], incoming.shape[0]
    vmem, smem = (pl.BlockSpec(memory_space=m) for m in (pltpu.VMEM, pltpu.SMEM))
    shape = (TILES, B, LANES)
    return pl.pallas_call(
        functools.partial(forward_body, count, grid_cells),
        out_shape=(
            jax.ShapeDtypeStruct((slots,) + shape, jnp.bfloat16),
            jax.ShapeDtypeStruct((count,) + shape, jnp.bfloat16),
        ),
        in_specs=[smem] * 4 + [vmem] * 2,
        out_specs=(vmem, vmem),
        scratch_shapes=[pltpu.VMEM((count,) + shape, jnp.float32)] + batch_scratch(),
        compiler_params=pltpu.CompilerParams(vmem_limit_bytes=VMEM_BYTES),
        name="forward_pairs",
    )(where, offsets, left, right, boxes, incoming)


def group_body(
    count, grid_cells, where_ref, offset_ref, mine_ref, theirs_ref, sent_ref, lefts_ref,
    boxes, field, *scratch,
):
    slots = mine_ref.shape[0]
    first, mine = where_ref[0], where_ref[1]
    clear_edges(scratch[2:], scratch[1])
    clear_lockstep(scratch[4])
    for n in range(count):
        for t in range(TILES):
            field[n, t] = jnp.zeros((B, LANES), jnp.float32)

    def batch(i, carry):
        def run(left_of, right_of, near, far):
            def slot_of(j):
                return geometry(offset_ref, first + left_of(j), first + right_of(j), grid_cells)

            run_batch(
                slot_of,
                lambda j, t: boxes[left_of(j), t].astype(jnp.float32),
                lambda j, t: boxes[right_of(j), t].astype(jnp.float32),
                near, far, scratch,
            )

        def near_to(j, t, value):
            if t is not None:
                field[mine_ref[i * BATCH + j], t] += value

        def far_to(j, t, value):
            field[sent_ref[i * BATCH + j], t] += value

        run(
            lambda j: mine + mine_ref[i * BATCH + j],
            lambda j: (i * BATCH + j) * count + theirs_ref[i * BATCH + j],
            near_to, None,
        )
        run(
            lambda j: (i * BATCH + j) * count + lefts_ref[i * BATCH + j],
            lambda j: mine + sent_ref[i * BATCH + j],
            None, far_to,
        )
        return carry

    lax.fori_loop(0, slots // BATCH, batch, 0)


def group_pairs(where, offsets, mine, theirs, sent, lefts, boxes, count, grid_cells):
    vmem, smem = (pl.BlockSpec(memory_space=m) for m in (pltpu.VMEM, pltpu.SMEM))
    return pl.pallas_call(
        functools.partial(group_body, count, grid_cells),
        out_shape=jax.ShapeDtypeStruct((count, TILES, B, LANES), jnp.float32),
        in_specs=[smem] * 6 + [vmem],
        out_specs=vmem,
        scratch_shapes=batch_scratch(),
        compiler_params=pltpu.CompilerParams(vmem_limit_bytes=VMEM_BYTES),
        name="group_pairs",
    )(where, offsets, mine, theirs, sent, lefts, boxes)


def along_space(block, distance):
    size = lax.axis_size("space")
    return lax.ppermute(block, "space", [((i - distance) % size, i) for i in range(size)])


def per_device(orbitals, box_offset, send_index, pair_left):
    count = orbitals.shape[0]
    spaces, orbs = lax.axis_size("space"), lax.axis_size("orb")
    grid_cells = spaces * HALF
    space, orb = lax.axis_index("space"), lax.axis_index("orb")
    group_first = space * orbs * count
    offsets = box_offset.reshape(-1)

    free = LANES - USED
    entries = jnp.concatenate([send_index[0].reshape(-1), pair_left[0].reshape(-1)])
    lines = 4 * orbs // free
    table = jnp.pad(
        entries.astype(jnp.float32).reshape(lines, free), ((0, B - lines), (USED, 0))
    )
    packed = pack(orbitals, table)

    incoming = along_space(packed, -1)
    boxes = lax.all_gather(packed, "orb", axis=0, tiled=True)

    def tables(block):
        lead = block.reshape((-1, count) + block.shape[1:])[:, 0, 0, :lines, USED:]
        return lead.astype(jnp.int32).reshape(-1, 2, 2, orbs)

    group = tables(boxes)
    sent_here = jnp.take(group[:, 0, 0, :], orb, axis=1)
    lefts_here = jnp.take(group[:, 1, :, :], orb, axis=2)
    next_sent = tables(incoming)[0, 0, 1]

    next_first = ((space + 1) % spaces * orbs + orb) * count
    near, far = forward_pairs(
        jnp.stack([group_first, next_first]), offsets, lefts_here[:, 1], next_sent,
        boxes, incoming, grid_cells,
    )
    near = lax.all_to_all(near, "orb", split_axis=0, concat_axis=0, tiled=True)
    far = along_space(far, 1)
    field = group_pairs(
        jnp.stack([group_first, orb * count]), offsets, pair_left[0, 0], sent_here,
        send_index[0, 0], lefts_here[:, 0], boxes, count, grid_cells,
    )
    return finish(field, near, far, pair_left[0, 1])


def solution(mesh):
    split = P(("space", "orb"), None, None)
    return jax.shard_map(
        per_device, mesh=mesh, in_specs=(split, P(), split, split), out_specs=split,
        check_vma=False,
    )
```

```python
import functools

import jax
import jax.numpy as jnp
from jax import lax
from jax.experimental import pallas as pl
from jax.experimental.pallas import tpu as pltpu
from jax.sharding import PartitionSpec as P

B = 40
ITERS = 4
SCREEN = 0.25

GROUPS = 3
TILES = 14
LANES = 128
USED = GROUPS * B
SUB = 8
PLANES = B // SUB
CELLS = TILES * PLANES
CELL = 2 * SUB
HALF = B // 2
VMEM_BYTES = 52 * 2**20
FIELDS = 8


def lanes_of(shape):
    return lax.broadcasted_iota(jnp.int32, shape, len(shape) - 1)


def overlaps():
    pieces = []
    for b in range(B):
        group = b // TILES
        for flat in range(b * B // LANES, (b * B + B - 1) // LANES + 1):
            pieces.append((b, flat, b * B - flat * LANES - group * B))
    return pieces


def pack_body(box_ref, table_ref, out_ref, stage):
    count = box_ref.shape[0]
    lane = lanes_of((B, LANES))
    for n in range(count):
        tiles = [jnp.zeros((B, LANES), jnp.float32) for _ in range(TILES)]
        loaded = {}
        for b, flat, shift in overlaps():
            if flat not in loaded:
                width = min(LANES, B * B - flat * LANES)
                part = box_ref[n, :, flat * LANES : flat * LANES + width].astype(jnp.float32)
                if width < LANES:
                    part = jnp.concatenate(
                        [part, jnp.zeros((B, LANES - width), jnp.float32)], axis=1
                    )
                stage[flat] = part
                loaded[flat] = jnp.concatenate(
                    [stage[flat, pl.ds(p, SUB, stride=PLANES), :] for p in range(PLANES)], axis=0
                )
            first = max(b * B, flat * LANES) - b * B + (b // TILES) * B
            last = min(b * B + B, flat * LANES + LANES) - b * B + (b // TILES) * B
            moved = pltpu.roll(loaded[flat], (-shift) % LANES, axis=1)
            keep = (lane >= first) & (lane < last)
            tiles[b % TILES] = jnp.where(keep, moved, tiles[b % TILES])
        if n == 0:
            tiles[0] = tiles[0] + table_ref[...]
        for t in range(TILES):
            out_ref[n, t] = tiles[t].astype(out_ref.dtype)


def pack(orbitals, table):
    count = orbitals.shape[0]
    return pl.pallas_call(
        pack_body,
        out_shape=jax.ShapeDtypeStruct((count, TILES, B, LANES), jnp.bfloat16),
        in_specs=[pl.BlockSpec(memory_space=pltpu.VMEM)] * 2,
        out_specs=pl.BlockSpec(memory_space=pltpu.VMEM),
        scratch_shapes=[pltpu.VMEM((-(-B * B // LANES), B, LANES), jnp.float32)],
        compiler_params=pltpu.CompilerParams(vmem_limit_bytes=VMEM_BYTES),
        name="pack",
    )(orbitals, table)


def finish_body(count, slots, field_ref, near_ref, far_ref, row_ref, out_ref, total, stage):
    lane = lanes_of((B, LANES))
    for n in range(count):
        for t in range(TILES):
            total[n, t] = field_ref[n, t] + far_ref[n, t].astype(jnp.float32)

    def add(j, carry):
        row = row_ref[j]
        for t in range(TILES):
            total[row, t] += near_ref[j, t].astype(jnp.float32)
        return carry

    lax.fori_loop(0, slots, add, 0)
    for n in range(count):
        flats = {}
        for b, flat, shift in overlaps():
            first = max(b * B, flat * LANES) - flat * LANES
            last = min(b * B + B, flat * LANES + LANES) - flat * LANES
            moved = pltpu.roll(total[n, b % TILES], shift % LANES, axis=1)
            keep = (lane >= first) & (lane < last)
            before = flats.get(flat)
            flats[flat] = moved if before is None else jnp.where(keep, moved, before)
        for flat, value in flats.items():
            for p in range(PLANES):
                stage[flat, pl.ds(p, SUB, stride=PLANES), :] = value[p * SUB : p * SUB + SUB]
            width = min(LANES, B * B - flat * LANES)
            out_ref[n, :, flat * LANES : flat * LANES + width] = stage[flat, :, :width]


def finish(field, near, far, rows):
    count, slots = field.shape[0], near.shape[0]
    vmem = pl.BlockSpec(memory_space=pltpu.VMEM)
    return pl.pallas_call(
        functools.partial(finish_body, count, slots),
        out_shape=jax.ShapeDtypeStruct((count, B, B * B), jnp.float32),
        in_specs=[vmem, vmem, vmem, pl.BlockSpec(memory_space=pltpu.SMEM)],
        out_specs=vmem,
        scratch_shapes=[
            pltpu.VMEM((count, TILES, B, LANES), jnp.float32),
            pltpu.VMEM((-(-B * B // LANES), B, LANES), jnp.float32),
        ],
        compiler_params=pltpu.CompilerParams(vmem_limit_bytes=VMEM_BYTES),
        name="finish",
    )(field, near, far, rows)


def geometry(offset_ref, left, right, grid_cells):
    shift, live = [], jnp.int32(1)
    for axis in range(3):
        gap = offset_ref[3 * right + axis] - offset_ref[3 * left + axis] + grid_cells // 2
        gap = jnp.where(gap < 0, gap + grid_cells, gap)
        gap = jnp.where(gap >= grid_cells, gap - grid_cells, gap) - grid_cells // 2
        live = jnp.where((gap > HALF) | (gap < -HALF), 0, live)
        shift.append(gap)
    return shift, live


def wrapped(shift, size):
    start = lax.rem(B * size - shift, size)
    turn = lax.div(B * size - shift, size) - B
    pairs = []
    for i in range(size):
        over = jnp.where(start + i >= size, 1, 0)
        pairs.append((start + i - size * over, turn + over))
    return pairs


def put_padded(pad, t, p, value):
    start = (t * PLANES + p) * CELL + SUB
    pad[start : start + SUB, :] = value


def displaced(pad, shift):
    lane = lanes_of((SUB, LANES))
    group = lane // B
    source_col = lane - group * B - shift[2]
    col_ok = (source_col >= 0) & (source_col < B) & (lane < USED)
    source_row = jnp.where(col_ok, TILES * group - shift[1], -2 * B)
    rows = [p * CELL + SUB + turn for p, turn in wrapped(shift[0], PLANES)]
    for t, (source, turn) in enumerate(wrapped(shift[1], TILES)):
        keep = (source_row + t >= 0) & (source_row + t < B)
        if t >= B - TILES * (GROUPS - 1):
            keep = keep & (lane < USED - B)
        amount = (shift[2] - B * turn + 2 * LANES) & (LANES - 1)
        tile = []
        for p in range(PLANES):
            block = pad[pl.ds(source * (PLANES * CELL) + rows[p], SUB), :]
            tile.append(jnp.where(keep, pltpu.roll(block, amount, axis=1), 0.0))
        yield t, tile


def tree_sum(values):
    while len(values) > 1:
        paired = [a + b for a, b in zip(values[::2], values[1::2])]
        values = paired + ([values[-1]] if len(values) % 2 else [])
    return values[0]


def blocks(value):
    return [value[p * SUB : p * SUB + SUB] for p in range(PLANES)]


def cell(t, p):
    start = (t * PLANES + p) * SUB
    return slice(start, start + SUB)


def make_operator():
    lane = lanes_of((SUB, LANES))
    sublane = lax.broadcasted_iota(jnp.int32, (SUB, LANES), 0)
    column = lane % B
    has_before = (column > 0) & (lane < USED)
    has_after = (column < B - 1) & (lane < USED)
    not_first = lane >= B
    not_last = lane < USED - B
    has_above = sublane > 0
    has_below = sublane < SUB - 1

    def operator(t, before, here, after):
        if t == 0:
            before = [jnp.where(not_first, pltpu.roll(v, B, axis=1), 0.0) for v in before]
        if t == TILES - 1:
            after = [jnp.where(not_last, pltpu.roll(v, LANES - B, axis=1), 0.0) for v in after]
        result = []
        for p in range(PLANES):
            if p == 0:
                above = jnp.where(has_above, pltpu.roll(here[PLANES - 1], 1, axis=0), 0.0)
            else:
                above = here[p - 1]
            if p == PLANES - 1:
                below = jnp.where(has_below, pltpu.roll(here[0], SUB - 1, axis=0), 0.0)
            else:
                below = here[p + 1]
            prior = jnp.where(has_before, pltpu.roll(here[p], 1, axis=1), 0.0)
            following = jnp.where(has_after, pltpu.roll(here[p], LANES - 1, axis=1), 0.0)
            around = (above + below) + (before[p] + after[p]) + (prior + following)
            value = (6.0 + SCREEN) * here[p] - around
            if t == B - TILES * (GROUPS - 1):
                value = jnp.where(not_last, value, 0.0)
            result.append(value)
        return result

    return operator


def solve(used, directions, residual, image, partial, norms, steps, ratios):
    operator = make_operator()

    def totals():
        total = jnp.sum(partial[...], axis=(1, 2), keepdims=True)
        return jnp.broadcast_to(total, partial.shape)

    def norm_of(m, carry):
        parts = []
        for t in range(TILES):
            parts.append(
                tree_sum([directions[0][m, cell(t, p), :] ** 2 for p in range(PLANES)])
            )
        partial[m] = tree_sum(parts)
        return carry

    lax.fori_loop(0, used, norm_of, 0)
    norms[...] = totals()
    for k in range(ITERS):
        last = k == ITERS - 1

        def stencil(m, carry, k=k, last=last):
            ratio = None if k == 0 else ratios[m]

            def fetch(t, keep):
                values = []
                for p in range(PLANES):
                    if k == 0:
                        value = directions[0][m, cell(t, p), :]
                    else:
                        value = residual[m, cell(t, p), :]
                        value = value + ratio * directions[k - 1][m, cell(t, p), :]
                        if keep:
                            directions[k][m, cell(t, p), :] = value
                    values.append(value)
                return values

            before, here = fetch(TILES - 1, False), fetch(0, True)
            total = None
            for t in range(TILES):
                after = fetch((t + 1) % TILES, t < TILES - 1)
                applied = operator(t, before, here, after)
                if not last:
                    for p in range(PLANES):
                        image[m, cell(t, p), :] = applied[p]
                part = tree_sum([x * y for x, y in zip(here, applied)])
                total = part if total is None else total + part
                before, here = here, after
            partial[m] = total
            return carry

        lax.fori_loop(0, used, stencil, 0)
        steps[k] = norms[...] / totals()
        if last:
            break
        source = directions[0] if k == 0 else residual

        def reduce(m, carry, k=k, source=source):
            step = steps[k, m]
            parts = []
            for t in range(TILES):
                squares = []
                for p in range(PLANES):
                    value = source[m, cell(t, p), :] - step * image[m, cell(t, p), :]
                    residual[m, cell(t, p), :] = value
                    squares.append(value * value)
                parts.append(tree_sum(squares))
            partial[m] = tree_sum(parts)
            return carry

        lax.fori_loop(0, used, reduce, 0)
        new = totals()
        ratios[...] = new / norms[...]
        norms[...] = new


def run_slots(used, slot_of, left_at, right_at, near_to, far_to, scratch):
    pad, shifted, partial, norms, steps, ratios, residual, image, *directions = scratch

    def load(m, carry):
        shift, _, _ = slot_of(m)
        for t in range(TILES):
            for p, block in enumerate(blocks(right_at(m, t))):
                put_padded(pad, t, p, block)
        for t, moved in displaced(pad, shift):
            for p, left in enumerate(blocks(left_at(m, t))):
                shifted[m, cell(t, p), :] = moved[p]
                directions[0][m, cell(t, p), :] = moved[p] * left
        return carry

    lax.fori_loop(0, used, load, 0)
    solve(used, directions, residual, image, partial, norms, steps, ratios)

    def unload(m, carry):
        shift, near, far = slot_of(m)
        weights = [steps[k, m] for k in range(ITERS)]
        for t in range(TILES):
            for p in range(PLANES):
                parts = [w * d[m, cell(t, p), :] for w, d in zip(weights, directions)]
                image[m, cell(t, p), :] = tree_sum(parts)

        @pl.when(near == 1)
        def _():
            for t in range(TILES):
                near_to(m, t, image[m, t * B : t * B + B, :] * shifted[m, t * B : t * B + B, :])

        @pl.when(far == 1)
        def _():
            for t in range(TILES):
                for p, left in enumerate(blocks(left_at(m, t))):
                    put_padded(pad, t, p, image[m, cell(t, p), :] * left)
            for t, moved in displaced(pad, [-s for s in shift]):
                far_to(m, t, jnp.concatenate(moved, axis=0))

        return carry

    lax.fori_loop(0, used, unload, 0)


def slot_scratch(batch):
    row = pltpu.VMEM((batch, SUB, LANES), jnp.float32)
    box = pltpu.VMEM((batch, CELLS * SUB, LANES), jnp.float32)
    return [
        pltpu.SMEM((batch * FIELDS,), jnp.int32),
        pltpu.VMEM((CELLS * CELL + SUB, LANES), jnp.float32),
        box, row, row,
        pltpu.VMEM((ITERS, batch, SUB, LANES), jnp.float32),
        row,
    ] + [box] * (2 + ITERS)


def clear(ref):
    for n in range(ref.shape[0]):
        for t in range(TILES):
            ref[n, t] = jnp.zeros((B, LANES), ref.dtype)


def append(listed, used, values):
    for i, value in enumerate(values):
        listed[used * FIELDS + i] = value


def forward_body(
    count, grid_cells, where_ref, offset_ref, left_ref, right_ref, boxes, incoming,
    near_ref, far_ref, far_sum, listed, *scratch,
):
    slots = near_ref.shape[0]
    batch = listed.shape[0] // FIELDS
    first_left, first_right = where_ref[0], where_ref[1]
    scratch[0][...] = jnp.zeros(scratch[0].shape, jnp.float32)
    clear(far_sum)

    def run(i, carry):
        def gather(j, used):
            slot = i * batch + j
            left, right = slot * count + left_ref[slot], right_ref[slot]
            shift, live = geometry(
                offset_ref, first_left + left, first_right + right, grid_cells
            )

            @pl.when(live == 1)
            def _():
                append(listed, used, [left, right, *shift, slot])

            @pl.when(live == 0)
            def _():
                for t in range(TILES):
                    near_ref[slot, t] = jnp.zeros((B, LANES), near_ref.dtype)

            return used + live

        used = lax.fori_loop(0, batch, gather, jnp.int32(0))

        def slot_of(m):
            return [listed[m * FIELDS + 2 + axis] for axis in range(3)], 1, 1

        def near_to(m, t, value):
            near_ref[listed[m * FIELDS + 5], t] = value.astype(near_ref.dtype)

        def far_to(m, t, value):
            far_sum[listed[m * FIELDS + 1], t] += value

        run_slots(
            used, slot_of,
            lambda m, t: boxes[listed[m * FIELDS], t].astype(jnp.float32),
            lambda m, t: incoming[listed[m * FIELDS + 1], t].astype(jnp.float32),
            near_to, far_to, scratch,
        )
        return carry

    lax.fori_loop(0, slots // batch, run, 0)
    for n in range(count):
        for t in range(TILES):
            far_ref[n, t] = far_sum[n, t].astype(far_ref.dtype)


def forward_pairs(where, offsets, left, right, boxes, incoming, grid_cells):
    slots, count = left.shape[0], incoming.shape[0]
    vmem, smem = (pl.BlockSpec(memory_space=m) for m in (pltpu.VMEM, pltpu.SMEM))
    shape = (TILES, B, LANES)
    return pl.pallas_call(
        functools.partial(forward_body, count, grid_cells),
        out_shape=(
            jax.ShapeDtypeStruct((slots,) + shape, jnp.bfloat16),
            jax.ShapeDtypeStruct((count,) + shape, jnp.bfloat16),
        ),
        in_specs=[smem] * 4 + [vmem] * 2,
        out_specs=(vmem, vmem),
        scratch_shapes=[pltpu.VMEM((count,) + shape, jnp.float32)] + slot_scratch(8),
        compiler_params=pltpu.CompilerParams(vmem_limit_bytes=VMEM_BYTES),
        name="forward_pairs",
    )(where, offsets, left, right, boxes, incoming)


def group_body(
    count, grid_cells, where_ref, offset_ref, mine_ref, theirs_ref, sent_ref, lefts_ref,
    boxes, field, listed, *scratch,
):
    slots = mine_ref.shape[0]
    batch = listed.shape[0] // FIELDS
    first, me = where_ref[0], where_ref[1]
    mine = me * count
    scratch[0][...] = jnp.zeros(scratch[0].shape, jnp.float32)
    clear(field)

    def run(i, carry):
        def gather(j, used):
            slot = i * (batch // 2) + j
            near_left, near_right = mine + mine_ref[slot], slot * count + theirs_ref[slot]
            far_left, far_right = slot * count + lefts_ref[slot], mine + sent_ref[slot]
            inside = jnp.where(slot == me, 1, 0)
            shift, live = geometry(offset_ref, first + near_left, first + near_right, grid_cells)

            @pl.when(live == 1)
            def _():
                append(listed, used, [near_left, near_right, *shift, 1, inside])

            used = used + live
            shift, live = geometry(offset_ref, first + far_left, first + far_right, grid_cells)
            live = jnp.where(slot == me, 0, live)

            @pl.when(live == 1)
            def _():
                append(listed, used, [far_left, far_right, *shift, 0, 1])

            return used + live

        used = lax.fori_loop(0, batch // 2, gather, jnp.int32(0))

        def slot_of(m):
            start = m * FIELDS + 2
            return [listed[start + axis] for axis in range(3)], listed[start + 3], listed[start + 4]

        def near_to(m, t, value):
            field[listed[m * FIELDS] - mine, t] += value

        def far_to(m, t, value):
            field[listed[m * FIELDS + 1] - mine, t] += value

        run_slots(
            used, slot_of,
            lambda m, t: boxes[listed[m * FIELDS], t].astype(jnp.float32),
            lambda m, t: boxes[listed[m * FIELDS + 1], t].astype(jnp.float32),
            near_to, far_to, scratch,
        )
        return carry

    lax.fori_loop(0, slots // (batch // 2), run, 0)


def group_pairs(where, offsets, mine, theirs, sent, lefts, boxes, count, grid_cells):
    vmem, smem = (pl.BlockSpec(memory_space=m) for m in (pltpu.VMEM, pltpu.SMEM))
    return pl.pallas_call(
        functools.partial(group_body, count, grid_cells),
        out_shape=jax.ShapeDtypeStruct((count, TILES, B, LANES), jnp.float32),
        in_specs=[smem] * 6 + [vmem],
        out_specs=vmem,
        scratch_shapes=slot_scratch(16),
        compiler_params=pltpu.CompilerParams(vmem_limit_bytes=VMEM_BYTES),
        name="group_pairs",
    )(where, offsets, mine, theirs, sent, lefts, boxes)


def along_space(block, distance):
    size = lax.axis_size("space")
    return lax.ppermute(block, "space", [((i - distance) % size, i) for i in range(size)])


def per_device(orbitals, box_offset, send_index, pair_left):
    count = orbitals.shape[0]
    spaces, orbs = lax.axis_size("space"), lax.axis_size("orb")
    grid_cells = spaces * HALF
    space, orb = lax.axis_index("space"), lax.axis_index("orb")
    group_first = space * orbs * count
    offsets = box_offset.reshape(-1)

    free = LANES - USED
    entries = jnp.concatenate([send_index[0].reshape(-1), pair_left[0].reshape(-1)])
    lines = 4 * orbs // free
    table = jnp.pad(
        entries.astype(jnp.float32).reshape(lines, free), ((0, B - lines), (USED, 0))
    )
    packed = pack(orbitals, table)

    incoming = along_space(packed, -1)
    boxes = lax.all_gather(packed, "orb", axis=0, tiled=True)

    def tables(block):
        lead = block.reshape((-1, count) + block.shape[1:])[:, 0, 0, :lines, USED:]
        return lead.astype(jnp.int32).reshape(-1, 2, 2, orbs)

    group = tables(boxes)
    sent_here = jnp.take(group[:, 0, 0, :], orb, axis=1)
    lefts_here = jnp.take(group[:, 1, :, :], orb, axis=2)
    next_sent = tables(incoming)[0, 0, 1]

    next_first = ((space + 1) % spaces * orbs + orb) * count
    near, far = forward_pairs(
        jnp.stack([group_first, next_first]), offsets, lefts_here[:, 1], next_sent,
        boxes, incoming, grid_cells,
    )
    near = lax.all_to_all(near, "orb", split_axis=0, concat_axis=0, tiled=True)
    far = along_space(far, 1)
    field = group_pairs(
        jnp.stack([group_first, orb]), offsets, pair_left[0, 0], sent_here,
        send_index[0, 0], lefts_here[:, 0], boxes, count, grid_cells,
    )
    return finish(field, near, far, pair_left[0, 1])


def solution(mesh):
    split = P(("space", "orb"), None, None)
    return jax.shard_map(
        per_device, mesh=mesh, in_specs=(split, P(), split, split), out_specs=split,
        check_vma=False,
    )
```

```python
import functools

import jax
import jax.numpy as jnp
from jax import lax
from jax.experimental import pallas as pl
from jax.experimental.pallas import tpu as pltpu
from jax.sharding import PartitionSpec as P

B = 40
ITERS = 4
SCREEN = 0.25

GROUPS = 3
TILES = 14
LANES = 128
USED = GROUPS * B
SUB = 8
PLANES = B // SUB
CELLS = TILES * PLANES
CELL = 2 * SUB
HALF = B // 2
VMEM_BYTES = 52 * 2**20
FIELDS = 8


def lanes_of(shape):
    return lax.broadcasted_iota(jnp.int32, shape, len(shape) - 1)


def overlaps():
    pieces = []
    for b in range(B):
        group = b // TILES
        for flat in range(b * B // LANES, (b * B + B - 1) // LANES + 1):
            pieces.append((b, flat, b * B - flat * LANES - group * B))
    return pieces


def pack_body(box_ref, table_ref, out_ref, stage):
    count = box_ref.shape[0]
    lane = lanes_of((B, LANES))
    for n in range(count):
        tiles = [jnp.zeros((B, LANES), jnp.float32) for _ in range(TILES)]
        loaded = {}
        for b, flat, shift in overlaps():
            if flat not in loaded:
                width = min(LANES, B * B - flat * LANES)
                part = box_ref[n, :, flat * LANES : flat * LANES + width].astype(jnp.float32)
                if width < LANES:
                    part = jnp.concatenate(
                        [part, jnp.zeros((B, LANES - width), jnp.float32)], axis=1
                    )
                stage[flat] = part
                loaded[flat] = jnp.concatenate(
                    [stage[flat, pl.ds(p, SUB, stride=PLANES), :] for p in range(PLANES)], axis=0
                )
            first = max(b * B, flat * LANES) - b * B + (b // TILES) * B
            last = min(b * B + B, flat * LANES + LANES) - b * B + (b // TILES) * B
            moved = pltpu.roll(loaded[flat], (-shift) % LANES, axis=1)
            keep = (lane >= first) & (lane < last)
            tiles[b % TILES] = jnp.where(keep, moved, tiles[b % TILES])
        if n == 0:
            tiles[0] = tiles[0] + table_ref[...]
        for t in range(TILES):
            out_ref[n, t] = tiles[t].astype(out_ref.dtype)


def pack(orbitals, table):
    count = orbitals.shape[0]
    return pl.pallas_call(
        pack_body,
        out_shape=jax.ShapeDtypeStruct((count, TILES, B, LANES), jnp.bfloat16),
        in_specs=[pl.BlockSpec(memory_space=pltpu.VMEM)] * 2,
        out_specs=pl.BlockSpec(memory_space=pltpu.VMEM),
        scratch_shapes=[pltpu.VMEM((-(-B * B // LANES), B, LANES), jnp.float32)],
        compiler_params=pltpu.CompilerParams(vmem_limit_bytes=VMEM_BYTES),
        name="pack",
    )(orbitals, table)


def finish_body(count, slots, field_ref, near_ref, far_ref, row_ref, out_ref, total, stage):
    lane = lanes_of((B, LANES))
    for n in range(count):
        for t in range(TILES):
            total[n, t] = field_ref[n, t] + far_ref[n, t].astype(jnp.float32)

    def add(j, carry):
        row = row_ref[j]
        for t in range(TILES):
            total[row, t] += near_ref[j, t].astype(jnp.float32)
        return carry

    lax.fori_loop(0, slots, add, 0)
    for n in range(count):
        flats = {}
        for b, flat, shift in overlaps():
            first = max(b * B, flat * LANES) - flat * LANES
            last = min(b * B + B, flat * LANES + LANES) - flat * LANES
            moved = pltpu.roll(total[n, b % TILES], shift % LANES, axis=1)
            keep = (lane >= first) & (lane < last)
            before = flats.get(flat)
            flats[flat] = moved if before is None else jnp.where(keep, moved, before)
        for flat, value in flats.items():
            for p in range(PLANES):
                stage[flat, pl.ds(p, SUB, stride=PLANES), :] = value[p * SUB : p * SUB + SUB]
            width = min(LANES, B * B - flat * LANES)
            out_ref[n, :, flat * LANES : flat * LANES + width] = stage[flat, :, :width]


def finish(field, near, far, rows):
    count, slots = field.shape[0], near.shape[0]
    vmem = pl.BlockSpec(memory_space=pltpu.VMEM)
    return pl.pallas_call(
        functools.partial(finish_body, count, slots),
        out_shape=jax.ShapeDtypeStruct((count, B, B * B), jnp.float32),
        in_specs=[vmem, vmem, vmem, pl.BlockSpec(memory_space=pltpu.SMEM)],
        out_specs=vmem,
        scratch_shapes=[
            pltpu.VMEM((count, TILES, B, LANES), jnp.float32),
            pltpu.VMEM((-(-B * B // LANES), B, LANES), jnp.float32),
        ],
        compiler_params=pltpu.CompilerParams(vmem_limit_bytes=VMEM_BYTES),
        name="finish",
    )(field, near, far, rows)


def geometry(offset_ref, left, right, grid_cells):
    shift, live = [], jnp.int32(1)
    for axis in range(3):
        gap = offset_ref[3 * right + axis] - offset_ref[3 * left + axis] + grid_cells // 2
        gap = jnp.where(gap < 0, gap + grid_cells, gap)
        gap = jnp.where(gap >= grid_cells, gap - grid_cells, gap) - grid_cells // 2
        live = jnp.where((gap > HALF) | (gap < -HALF), 0, live)
        shift.append(gap)
    return shift, live


def wrapped(shift, size):
    start = lax.rem(B * size - shift, size)
    turn = lax.div(B * size - shift, size) - B
    pairs = []
    for i in range(size):
        over = jnp.where(start + i >= size, 1, 0)
        pairs.append((start + i - size * over, turn + over))
    return pairs


def put_padded(pad, t, p, value):
    start = (t * PLANES + p) * CELL + SUB
    pad[start : start + SUB, :] = value


def displaced(pad, shift):
    lane = lanes_of((SUB, LANES))
    group = lane // B
    source_col = lane - group * B - shift[2]
    col_ok = (source_col >= 0) & (source_col < B) & (lane < USED)
    source_row = jnp.where(col_ok, TILES * group - shift[1], -2 * B)
    rows = [p * CELL + SUB + turn for p, turn in wrapped(shift[0], PLANES)]
    for t, (source, turn) in enumerate(wrapped(shift[1], TILES)):
        keep = (source_row + t >= 0) & (source_row + t < B)
        if t >= B - TILES * (GROUPS - 1):
            keep = keep & (lane < USED - B)
        amount = (shift[2] - B * turn + 2 * LANES) & (LANES - 1)
        tile = []
        for p in range(PLANES):
            block = pad[pl.ds(source * (PLANES * CELL) + rows[p], SUB), :]
            tile.append(jnp.where(keep, pltpu.roll(block, amount, axis=1), 0.0))
        yield t, tile


def tree_sum(values):
    while len(values) > 1:
        paired = [a + b for a, b in zip(values[::2], values[1::2])]
        values = paired + ([values[-1]] if len(values) % 2 else [])
    return values[0]


def blocks(value):
    return [value[p * SUB : p * SUB + SUB] for p in range(PLANES)]


def cell(t, p):
    start = (t * PLANES + p) * SUB
    return slice(start, start + SUB)


def make_operator():
    lane = lanes_of((SUB, LANES))
    sublane = lax.broadcasted_iota(jnp.int32, (SUB, LANES), 0)
    column = lane % B
    has_before = (column > 0) & (lane < USED)
    has_after = (column < B - 1) & (lane < USED)
    not_first = lane >= B
    not_last = lane < USED - B
    has_above = sublane > 0
    has_below = sublane < SUB - 1

    def operator(t, before, here, after):
        if t == 0:
            before = [jnp.where(not_first, pltpu.roll(v, B, axis=1), 0.0) for v in before]
        if t == TILES - 1:
            after = [jnp.where(not_last, pltpu.roll(v, LANES - B, axis=1), 0.0) for v in after]
        result = []
        for p in range(PLANES):
            if p == 0:
                above = jnp.where(has_above, pltpu.roll(here[PLANES - 1], 1, axis=0), 0.0)
            else:
                above = here[p - 1]
            if p == PLANES - 1:
                below = jnp.where(has_below, pltpu.roll(here[0], SUB - 1, axis=0), 0.0)
            else:
                below = here[p + 1]
            prior = jnp.where(has_before, pltpu.roll(here[p], 1, axis=1), 0.0)
            following = jnp.where(has_after, pltpu.roll(here[p], LANES - 1, axis=1), 0.0)
            around = (above + below) + (before[p] + after[p]) + (prior + following)
            value = (6.0 + SCREEN) * here[p] - around
            if t == B - TILES * (GROUPS - 1):
                value = jnp.where(not_last, value, 0.0)
            result.append(value)
        return result

    return operator


def side_by_side(used, body):
    def pair(i, carry):
        for _ in zip(body(2 * i, 0), body(2 * i + 1, 1)):
            pass
        return carry

    lax.fori_loop(0, lax.div(used, 2), pair, 0)

    @pl.when(lax.rem(used, 2) == 1)
    def _():
        for _ in body(used - 1, 0):
            pass


def solve(used, directions, residual, image, partial, norms, steps, ratios):
    operator = make_operator()

    def totals():
        rows = jnp.sum(partial[...], axis=1)
        return jnp.broadcast_to(jnp.sum(rows, axis=1, keepdims=True), rows.shape)

    norms[...] = totals()
    for k in range(ITERS):
        last = k == ITERS - 1

        def stencil(m, side, k=k, last=last):
            ratio = None if k == 0 else ratios[pl.ds(m, 1), :]

            def fetch(t, keep):
                values = []
                for p in range(PLANES):
                    if k == 0:
                        value = directions[0][m, cell(t, p), :]
                    else:
                        value = residual[m, cell(t, p), :]
                        value = value + ratio * directions[k - 1][m, cell(t, p), :]
                        if keep:
                            directions[k][m, cell(t, p), :] = value
                    values.append(value)
                return values

            before, here = fetch(TILES - 1, False), fetch(0, True)
            total = None
            for t in range(TILES):
                after = fetch((t + 1) % TILES, t < TILES - 1)
                applied = operator(t, before, here, after)
                if not last:
                    for p in range(PLANES):
                        image[m, cell(t, p), :] = applied[p]
                part = tree_sum([x * y for x, y in zip(here, applied)])
                total = part if total is None else total + part
                before, here = here, after
                yield
            partial[m] = total
            yield

        side_by_side(used, stencil)
        steps[k] = norms[...] / totals()
        if last:
            break
        source = directions[0] if k == 0 else residual

        def reduce(m, side, k=k, source=source):
            step = steps[k, pl.ds(m, 1), :]
            total = None
            for t in range(TILES):
                squares = []
                for p in range(PLANES):
                    value = source[m, cell(t, p), :] - step * image[m, cell(t, p), :]
                    residual[m, cell(t, p), :] = value
                    squares.append(value * value)
                part = tree_sum(squares)
                total = part if total is None else total + part
                yield
            partial[m] = total
            yield

        side_by_side(used, reduce)
        new = totals()
        ratios[...] = new / norms[...]
        norms[...] = new


def run_slots(used, nears, fars, shift_of, left_at, right_at, near_to, far_to, scratch):
    pads, shifted, partial, norms, steps, ratios, residual, image, *directions = scratch

    def load(m, side):
        pad = pads.at[side]
        for t in range(TILES):
            for p, block in enumerate(blocks(right_at(m, t))):
                put_padded(pad, t, p, block)
            yield
        total = None
        for t, moved in displaced(pad, shift_of(m)):
            squares = []
            for p, left in enumerate(blocks(left_at(m, t))):
                shifted[m, cell(t, p), :] = moved[p]
                density = moved[p] * left
                directions[0][m, cell(t, p), :] = density
                squares.append(density * density)
            part = tree_sum(squares)
            total = part if total is None else total + part
            yield
        partial[m] = total
        yield

    side_by_side(used, load)
    solve(used, directions, residual, image, partial, norms, steps, ratios)

    def potential(m, t):
        weights = [steps[k, pl.ds(m, 1), :] for k in range(ITERS)]
        return [
            tree_sum([w * d[m, cell(t, p), :] for w, d in zip(weights, directions)])
            for p in range(PLANES)
        ]

    def unload(near, far):
        def one(m, carry):
            pad = pads.at[0]
            for t in range(TILES):
                solved = potential(m, t)
                if near:
                    near_to(
                        m, t,
                        jnp.concatenate(
                            [v * shifted[m, cell(t, p), :] for p, v in enumerate(solved)], axis=0
                        ),
                    )
                if far:
                    for p, left in enumerate(blocks(left_at(m, t))):
                        put_padded(pad, t, p, solved[p] * left)
            if far:
                for t, moved in displaced(pad, [-s for s in shift_of(m)]):
                    far_to(m, t, jnp.concatenate(moved, axis=0))
            return carry

        return one

    if nears is fars:
        lax.fori_loop(*nears, unload(True, True), 0)
    else:
        lax.fori_loop(*nears, unload(True, False), 0)
        lax.fori_loop(*fars, unload(False, True), 0)


def slot_scratch(batch):
    row = pltpu.VMEM((batch, LANES), jnp.float32)
    box = pltpu.VMEM((batch, CELLS * SUB, LANES), jnp.float32)
    return [
        pltpu.SMEM((batch * FIELDS,), jnp.int32),
        pltpu.VMEM((2, CELLS * CELL + SUB, LANES), jnp.float32),
        box,
        pltpu.VMEM((batch, SUB, LANES), jnp.float32),
        row,
        pltpu.VMEM((ITERS, batch, LANES), jnp.float32),
        row,
    ] + [box] * (2 + ITERS)


def clear(ref):
    for n in range(ref.shape[0]):
        for t in range(TILES):
            ref[n, t] = jnp.zeros((B, LANES), ref.dtype)


def append(listed, used, values):
    for i, value in enumerate(values):
        listed[used * FIELDS + i] = value


def forward_body(
    count, grid_cells, where_ref, offset_ref, left_ref, right_ref, boxes, incoming,
    near_ref, far_ref, far_sum, listed, *scratch,
):
    slots = near_ref.shape[0]
    batch = listed.shape[0] // FIELDS
    first_left, first_right = where_ref[0], where_ref[1]
    scratch[0][...] = jnp.zeros(scratch[0].shape, jnp.float32)
    clear(far_sum)

    def run(i, carry):
        def gather(j, used):
            slot = i * batch + j
            left, right = slot * count + left_ref[slot], right_ref[slot]
            shift, live = geometry(
                offset_ref, first_left + left, first_right + right, grid_cells
            )

            @pl.when(live == 1)
            def _():
                append(listed, used, [left, right, *shift, slot])

            @pl.when(live == 0)
            def _():
                for t in range(TILES):
                    near_ref[slot, t] = jnp.zeros((B, LANES), near_ref.dtype)

            return used + live

        used = lax.fori_loop(0, batch, gather, jnp.int32(0))

        def shift_of(m):
            return [listed[m * FIELDS + 2 + axis] for axis in range(3)]

        def near_to(m, t, value):
            near_ref[listed[m * FIELDS + 5], t] = value.astype(near_ref.dtype)

        def far_to(m, t, value):
            far_sum[listed[m * FIELDS + 1], t] += value

        every = (0, used)
        run_slots(
            used, every, every, shift_of,
            lambda m, t: boxes[listed[m * FIELDS], t].astype(jnp.float32),
            lambda m, t: incoming[listed[m * FIELDS + 1], t].astype(jnp.float32),
            near_to, far_to, scratch,
        )
        return carry

    lax.fori_loop(0, slots // batch, run, 0)
    for n in range(count):
        for t in range(TILES):
            far_ref[n, t] = far_sum[n, t].astype(far_ref.dtype)


def forward_pairs(where, offsets, left, right, boxes, incoming, grid_cells):
    slots, count = left.shape[0], incoming.shape[0]
    vmem, smem = (pl.BlockSpec(memory_space=m) for m in (pltpu.VMEM, pltpu.SMEM))
    shape = (TILES, B, LANES)
    return pl.pallas_call(
        functools.partial(forward_body, count, grid_cells),
        out_shape=(
            jax.ShapeDtypeStruct((slots,) + shape, jnp.bfloat16),
            jax.ShapeDtypeStruct((count,) + shape, jnp.bfloat16),
        ),
        in_specs=[smem] * 4 + [vmem] * 2,
        out_specs=(vmem, vmem),
        scratch_shapes=[pltpu.VMEM((count,) + shape, jnp.float32)] + slot_scratch(8),
        compiler_params=pltpu.CompilerParams(vmem_limit_bytes=VMEM_BYTES),
        name="forward_pairs",
    )(where, offsets, left, right, boxes, incoming)


def group_body(
    count, grid_cells, where_ref, offset_ref, mine_ref, theirs_ref, sent_ref, lefts_ref,
    boxes, field, listed, *scratch,
):
    slots = mine_ref.shape[0]
    half = listed.shape[0] // FIELDS // 2
    first, me = where_ref[0], where_ref[1]
    mine = me * count
    scratch[0][...] = jnp.zeros(scratch[0].shape, jnp.float32)
    clear(field)

    def run(i, carry):
        def listing(near):
            def gather(j, used):
                slot = i * half + lax.rem(me + 1 + j, half)
                if near:
                    left, right = mine + mine_ref[slot], slot * count + theirs_ref[slot]
                else:
                    left, right = slot * count + lefts_ref[slot], mine + sent_ref[slot]
                shift, live = geometry(offset_ref, first + left, first + right, grid_cells)
                if not near:
                    live = jnp.where(slot == me, 0, live)

                @pl.when(live == 1)
                def _():
                    append(listed, used, [left, right, *shift])

                return used + live

            return gather

        near_count = lax.fori_loop(0, half, listing(True), jnp.int32(0))
        used = lax.fori_loop(0, half, listing(False), near_count)
        left, right = mine + mine_ref[me], mine + theirs_ref[me]
        inside = geometry(offset_ref, first + left, first + right, grid_cells)[1]
        inside = jnp.where(lax.div(me, half) == i, inside, 0)

        def shift_of(m):
            return [listed[m * FIELDS + 2 + axis] for axis in range(3)]

        def near_to(m, t, value):
            field[listed[m * FIELDS] - mine, t] += value

        def far_to(m, t, value):
            field[listed[m * FIELDS + 1] - mine, t] += value

        run_slots(
            used, (0, near_count), (near_count - inside, used), shift_of,
            lambda m, t: boxes[listed[m * FIELDS], t].astype(jnp.float32),
            lambda m, t: boxes[listed[m * FIELDS + 1], t].astype(jnp.float32),
            near_to, far_to, scratch,
        )
        return carry

    lax.fori_loop(0, slots // half, run, 0)


def group_pairs(where, offsets, mine, theirs, sent, lefts, boxes, count, grid_cells):
    vmem, smem = (pl.BlockSpec(memory_space=m) for m in (pltpu.VMEM, pltpu.SMEM))
    return pl.pallas_call(
        functools.partial(group_body, count, grid_cells),
        out_shape=jax.ShapeDtypeStruct((count, TILES, B, LANES), jnp.float32),
        in_specs=[smem] * 6 + [vmem],
        out_specs=vmem,
        scratch_shapes=slot_scratch(16),
        compiler_params=pltpu.CompilerParams(vmem_limit_bytes=VMEM_BYTES),
        name="group_pairs",
    )(where, offsets, mine, theirs, sent, lefts, boxes)


def along_space(block, distance):
    size = lax.axis_size("space")
    return lax.ppermute(block, "space", [((i - distance) % size, i) for i in range(size)])


def per_device(orbitals, box_offset, send_index, pair_left):
    count = orbitals.shape[0]
    spaces, orbs = lax.axis_size("space"), lax.axis_size("orb")
    grid_cells = spaces * HALF
    space, orb = lax.axis_index("space"), lax.axis_index("orb")
    group_first = space * orbs * count
    offsets = box_offset.reshape(-1)

    free = LANES - USED
    entries = jnp.concatenate([send_index[0].reshape(-1), pair_left[0].reshape(-1)])
    lines = 4 * orbs // free
    table = jnp.pad(
        entries.astype(jnp.float32).reshape(lines, free), ((0, B - lines), (USED, 0))
    )
    packed = pack(orbitals, table)

    incoming = along_space(packed, -1)
    boxes = lax.all_gather(packed, "orb", axis=0, tiled=True)

    def tables(block):
        lead = block.reshape((-1, count) + block.shape[1:])[:, 0, 0, :lines, USED:]
        return lead.astype(jnp.int32).reshape(-1, 2, 2, orbs)

    group = tables(boxes)
    sent_here = jnp.take(group[:, 0, 0, :], orb, axis=1)
    lefts_here = jnp.take(group[:, 1, :, :], orb, axis=2)
    next_sent = tables(incoming)[0, 0, 1]

    next_first = ((space + 1) % spaces * orbs + orb) * count
    near, far = forward_pairs(
        jnp.stack([group_first, next_first]), offsets, lefts_here[:, 1], next_sent,
        boxes, incoming, grid_cells,
    )
    near = lax.all_to_all(near, "orb", split_axis=0, concat_axis=0, tiled=True)
    far = along_space(far, 1)
    field = group_pairs(
        jnp.stack([group_first, orb]), offsets, pair_left[0, 0], sent_here,
        send_index[0, 0], lefts_here[:, 0], boxes, count, grid_cells,
    )
    return finish(field, near, far, pair_left[0, 1])


def solution(mesh):
    split = P(("space", "orb"), None, None)
    return jax.shard_map(
        per_device, mesh=mesh, in_specs=(split, P(), split, split), out_specs=split,
        check_vma=False,
    )
```

```python
import functools

import jax
import jax.numpy as jnp
from jax import lax
from jax.experimental import pallas as pl
from jax.experimental.pallas import tpu as pltpu
from jax.sharding import PartitionSpec as P

B = 40
ITERS = 4
SCREEN = 0.25

GROUPS = 3
TILES = 14
LANES = 128
USED = GROUPS * B
SUB = 8
PLANES = B // SUB
CELLS = TILES * PLANES
CELL = 2 * SUB
HALF = B // 2
VMEM_BYTES = 52 * 2**20
FIELDS = 8


def lanes_of(shape):
    return lax.broadcasted_iota(jnp.int32, shape, len(shape) - 1)


def overlaps():
    pieces = []
    for b in range(B):
        group = b // TILES
        for flat in range(b * B // LANES, (b * B + B - 1) // LANES + 1):
            pieces.append((b, flat, b * B - flat * LANES - group * B))
    return pieces


def pack_body(box_ref, table_ref, first_ref, second_ref, stage):
    count = box_ref.shape[0]
    lane = lanes_of((B, LANES))
    for n in range(count):
        tiles = [jnp.zeros((B, LANES), jnp.float32) for _ in range(TILES)]
        loaded = {}
        for b, flat, shift in overlaps():
            if flat not in loaded:
                width = min(LANES, B * B - flat * LANES)
                part = box_ref[n, :, flat * LANES : flat * LANES + width].astype(jnp.float32)
                if width < LANES:
                    part = jnp.concatenate(
                        [part, jnp.zeros((B, LANES - width), jnp.float32)], axis=1
                    )
                stage[flat] = part
                loaded[flat] = jnp.concatenate(
                    [stage[flat, pl.ds(p, SUB, stride=PLANES), :] for p in range(PLANES)], axis=0
                )
            first = max(b * B, flat * LANES) - b * B + (b // TILES) * B
            last = min(b * B + B, flat * LANES + LANES) - b * B + (b // TILES) * B
            moved = pltpu.roll(loaded[flat], (-shift) % LANES, axis=1)
            keep = (lane >= first) & (lane < last)
            tiles[b % TILES] = jnp.where(keep, moved, tiles[b % TILES])
        if n == 0:
            tiles[0] = tiles[0] + table_ref[...]
        out_ref = first_ref if n < count // 2 else second_ref
        for t in range(TILES):
            out_ref[n % (count // 2), t] = tiles[t].astype(out_ref.dtype)


def pack(orbitals, table):
    count = orbitals.shape[0]
    return pl.pallas_call(
        pack_body,
        out_shape=[jax.ShapeDtypeStruct((count // 2, TILES, B, LANES), jnp.bfloat16)] * 2,
        in_specs=[pl.BlockSpec(memory_space=pltpu.VMEM)] * 2,
        out_specs=[pl.BlockSpec(memory_space=pltpu.VMEM)] * 2,
        scratch_shapes=[pltpu.VMEM((-(-B * B // LANES), B, LANES), jnp.float32)],
        compiler_params=pltpu.CompilerParams(vmem_limit_bytes=VMEM_BYTES),
        name="pack",
    )(orbitals, table)


def finish_body(count, slots, field_ref, near_ref, far_ref, row_ref, out_ref, total, stage):
    lane = lanes_of((B, LANES))
    for n in range(count):
        for t in range(TILES):
            total[n, t] = field_ref[n, t] + far_ref[n, t].astype(jnp.float32)

    def add(j, carry):
        row = row_ref[j]
        for t in range(TILES):
            total[row, t] += near_ref[j, t].astype(jnp.float32)
        return carry

    lax.fori_loop(0, slots, add, 0)
    for n in range(count):
        flats = {}
        for b, flat, shift in overlaps():
            first = max(b * B, flat * LANES) - flat * LANES
            last = min(b * B + B, flat * LANES + LANES) - flat * LANES
            moved = pltpu.roll(total[n, b % TILES], shift % LANES, axis=1)
            keep = (lane >= first) & (lane < last)
            before = flats.get(flat)
            flats[flat] = moved if before is None else jnp.where(keep, moved, before)
        for flat, value in flats.items():
            for p in range(PLANES):
                stage[flat, pl.ds(p, SUB, stride=PLANES), :] = value[p * SUB : p * SUB + SUB]
            width = min(LANES, B * B - flat * LANES)
            out_ref[n, :, flat * LANES : flat * LANES + width] = stage[flat, :, :width]


def finish(field, near, far, rows):
    count, slots = field.shape[0], near.shape[0]
    vmem = pl.BlockSpec(memory_space=pltpu.VMEM)
    return pl.pallas_call(
        functools.partial(finish_body, count, slots),
        out_shape=jax.ShapeDtypeStruct((count, B, B * B), jnp.float32),
        in_specs=[vmem, vmem, vmem, pl.BlockSpec(memory_space=pltpu.SMEM)],
        out_specs=vmem,
        scratch_shapes=[
            pltpu.VMEM((count, TILES, B, LANES), jnp.float32),
            pltpu.VMEM((-(-B * B // LANES), B, LANES), jnp.float32),
        ],
        compiler_params=pltpu.CompilerParams(vmem_limit_bytes=VMEM_BYTES),
        name="finish",
    )(field, near, far, rows)


def geometry(offset_ref, left, right, grid_cells):
    shift, live = [], jnp.int32(1)
    for axis in range(3):
        gap = offset_ref[3 * right + axis] - offset_ref[3 * left + axis] + grid_cells // 2
        gap = jnp.where(gap < 0, gap + grid_cells, gap)
        gap = jnp.where(gap >= grid_cells, gap - grid_cells, gap) - grid_cells // 2
        live = jnp.where((gap > HALF) | (gap < -HALF), 0, live)
        shift.append(gap)
    return shift, live


def wrapped(shift, size):
    start = lax.rem(B * size - shift, size)
    turn = lax.div(B * size - shift, size) - B
    pairs = []
    for i in range(size):
        over = jnp.where(start + i >= size, 1, 0)
        pairs.append((start + i - size * over, turn + over))
    return pairs


def put_padded(pad, t, p, value):
    start = (t * PLANES + p) * CELL + SUB
    pad[start : start + SUB, :] = value


def displaced(pad, shift):
    lane = lanes_of((SUB, LANES))
    group = lane // B
    source_col = lane - group * B - shift[2]
    col_ok = (source_col >= 0) & (source_col < B) & (lane < USED)
    source_row = jnp.where(col_ok, TILES * group - shift[1], -2 * B)
    rows = [p * CELL + SUB + turn for p, turn in wrapped(shift[0], PLANES)]
    for t, (source, turn) in enumerate(wrapped(shift[1], TILES)):
        keep = (source_row + t >= 0) & (source_row + t < B)
        if t >= B - TILES * (GROUPS - 1):
            keep = keep & (lane < USED - B)
        amount = (shift[2] - B * turn + 2 * LANES) & (LANES - 1)
        tile = []
        for p in range(PLANES):
            block = pad[pl.ds(source * (PLANES * CELL) + rows[p], SUB), :]
            tile.append(jnp.where(keep, pltpu.roll(block, amount, axis=1), 0.0))
        yield t, tile


def tree_sum(values):
    while len(values) > 1:
        paired = [a + b for a, b in zip(values[::2], values[1::2])]
        values = paired + ([values[-1]] if len(values) % 2 else [])
    return values[0]


def blocks(value):
    return [value[p * SUB : p * SUB + SUB] for p in range(PLANES)]


def cell(t, p):
    start = (t * PLANES + p) * SUB
    return slice(start, start + SUB)


def make_operator():
    lane = lanes_of((SUB, LANES))
    sublane = lax.broadcasted_iota(jnp.int32, (SUB, LANES), 0)
    column = lane % B
    has_before = (column > 0) & (lane < USED)
    has_after = (column < B - 1) & (lane < USED)
    not_first = lane >= B
    not_last = lane < USED - B
    has_above = sublane > 0
    has_below = sublane < SUB - 1

    def operator(t, before, here, after):
        if t == 0:
            before = [jnp.where(not_first, pltpu.roll(v, B, axis=1), 0.0) for v in before]
        if t == TILES - 1:
            after = [jnp.where(not_last, pltpu.roll(v, LANES - B, axis=1), 0.0) for v in after]
        result = []
        for p in range(PLANES):
            if p == 0:
                above = jnp.where(has_above, pltpu.roll(here[PLANES - 1], 1, axis=0), 0.0)
            else:
                above = here[p - 1]
            if p == PLANES - 1:
                below = jnp.where(has_below, pltpu.roll(here[0], SUB - 1, axis=0), 0.0)
            else:
                below = here[p + 1]
            prior = jnp.where(has_before, pltpu.roll(here[p], 1, axis=1), 0.0)
            following = jnp.where(has_after, pltpu.roll(here[p], LANES - 1, axis=1), 0.0)
            around = (above + below) + (before[p] + after[p]) + (prior + following)
            value = (6.0 + SCREEN) * here[p] - around
            if t == B - TILES * (GROUPS - 1):
                value = jnp.where(not_last, value, 0.0)
            result.append(value)
        return result

    return operator


def side_by_side(used, body):
    def pair(i, carry):
        for _ in zip(body(2 * i, 0), body(2 * i + 1, 1)):
            pass
        return carry

    lax.fori_loop(0, lax.div(used, 2), pair, 0)

    @pl.when(lax.rem(used, 2) == 1)
    def _():
        for _ in body(used - 1, 0):
            pass


def solve(used, directions, residual, image, partial, norms, steps, ratios):
    operator = make_operator()

    def totals():
        rows = jnp.sum(partial[...], axis=1)
        return jnp.broadcast_to(jnp.sum(rows, axis=1, keepdims=True), rows.shape)

    norms[...] = totals()
    for k in range(ITERS):
        last = k == ITERS - 1

        def stencil(m, side, k=k, last=last):
            ratio = None if k == 0 else ratios[pl.ds(m, 1), :]

            def fetch(t, keep):
                values = []
                for p in range(PLANES):
                    if k == 0:
                        value = directions[0][m, cell(t, p), :]
                    else:
                        value = residual[m, cell(t, p), :]
                        value = value + ratio * directions[k - 1][m, cell(t, p), :]
                        if keep:
                            directions[k][m, cell(t, p), :] = value
                    values.append(value)
                return values

            before, here = fetch(TILES - 1, False), fetch(0, True)
            total = None
            for t in range(TILES):
                after = fetch((t + 1) % TILES, t < TILES - 1)
                applied = operator(t, before, here, after)
                if not last:
                    for p in range(PLANES):
                        image[m, cell(t, p), :] = applied[p]
                part = tree_sum([x * y for x, y in zip(here, applied)])
                total = part if total is None else total + part
                before, here = here, after
                yield
            partial[m] = total
            yield

        side_by_side(used, stencil)
        steps[k] = norms[...] / totals()
        if last:
            break
        source = directions[0] if k == 0 else residual

        def reduce(m, side, k=k, source=source):
            step = steps[k, pl.ds(m, 1), :]
            total = None
            for t in range(TILES):
                squares = []
                for p in range(PLANES):
                    value = source[m, cell(t, p), :] - step * image[m, cell(t, p), :]
                    residual[m, cell(t, p), :] = value
                    squares.append(value * value)
                part = tree_sum(squares)
                total = part if total is None else total + part
                yield
            partial[m] = total
            yield

        side_by_side(used, reduce)
        new = totals()
        ratios[...] = new / norms[...]
        norms[...] = new


def run_slots(used, nears, fars, shift_of, left_at, right_at, near_to, far_to, scratch):
    pads, shifted, partial, norms, steps, ratios, residual, image, *directions = scratch

    def load(m, side):
        pad = pads.at[side]
        for t in range(TILES):
            for p, block in enumerate(blocks(right_at(m, t))):
                put_padded(pad, t, p, block)
            yield
        total = None
        for t, moved in displaced(pad, shift_of(m)):
            squares = []
            for p, left in enumerate(blocks(left_at(m, t))):
                shifted[m, cell(t, p), :] = moved[p]
                density = moved[p] * left
                directions[0][m, cell(t, p), :] = density
                squares.append(density * density)
            part = tree_sum(squares)
            total = part if total is None else total + part
            yield
        partial[m] = total
        yield

    side_by_side(used, load)
    solve(used, directions, residual, image, partial, norms, steps, ratios)

    def potential(m, t):
        weights = [steps[k, pl.ds(m, 1), :] for k in range(ITERS)]
        return [
            tree_sum([w * d[m, cell(t, p), :] for w, d in zip(weights, directions)])
            for p in range(PLANES)
        ]

    def unload(near, far):
        def one(m, carry):
            pad = pads.at[0]
            for t in range(TILES):
                solved = potential(m, t)
                if near:
                    near_to(
                        m, t,
                        jnp.concatenate(
                            [v * shifted[m, cell(t, p), :] for p, v in enumerate(solved)], axis=0
                        ),
                    )
                if far:
                    for p, left in enumerate(blocks(left_at(m, t))):
                        put_padded(pad, t, p, solved[p] * left)
            if far:
                for t, moved in displaced(pad, [-s for s in shift_of(m)]):
                    far_to(m, t, jnp.concatenate(moved, axis=0))
            return carry

        return one

    if nears is fars:
        lax.fori_loop(*nears, unload(True, True), 0)
    else:
        lax.fori_loop(*nears, unload(True, False), 0)
        lax.fori_loop(*fars, unload(False, True), 0)


def slot_scratch(batch):
    row = pltpu.VMEM((batch, LANES), jnp.float32)
    box = pltpu.VMEM((batch, CELLS * SUB, LANES), jnp.float32)
    return [
        pltpu.SMEM((batch * FIELDS,), jnp.int32),
        pltpu.VMEM((2, CELLS * CELL + SUB, LANES), jnp.float32),
        box,
        pltpu.VMEM((batch, SUB, LANES), jnp.float32),
        row,
        pltpu.VMEM((ITERS, batch, LANES), jnp.float32),
        row,
    ] + [box] * (2 + ITERS)


def clear(ref):
    for n in range(ref.shape[0]):
        for t in range(TILES):
            ref[n, t] = jnp.zeros((B, LANES), ref.dtype)


def append(listed, used, values):
    for i, value in enumerate(values):
        listed[used * FIELDS + i] = value


def piece_copies(pieces, index, held, slot, sem):
    part = pieces[0].shape[0]
    for h, piece in enumerate(pieces):

        @pl.when(lax.div(index, part) == h)
        def _(h=h, piece=piece):
            pltpu.make_async_copy(piece.at[index - h * part], held.at[slot], sem).start()


def wait_box(pieces, held, slot, sem):
    pltpu.make_async_copy(pieces[0].at[0], held.at[slot], sem).wait()


def read_tables(meta, orbs, me, count, index_ref):
    free = LANES - USED
    lines = orbs // free
    row = lax.broadcasted_iota(jnp.int32, (B, LANES), 0)
    lane = lanes_of((B, LANES)) - USED

    def digits(value, length):
        value = value.astype(jnp.int32)
        for _ in range(length):
            rest = lax.div(value, count)
            yield value - rest * count
            value = rest

    weight = jnp.zeros((B, LANES), jnp.float32)
    for place, kind in enumerate((0, 2, 3)):
        chosen = (row == kind * lines + lax.div(me, free)) & (lane == lax.rem(me, free))
        weight = jnp.where(chosen, float(count**place), weight)
    for k in range(orbs):
        source = jnp.bitwise_xor(me, k)
        total = jnp.sum(meta[k].astype(jnp.float32) * weight)
        for kind, value in enumerate(digits(total, 3)):
            index_ref[kind * orbs + source] = value
    weight = jnp.zeros((B, LANES), jnp.float32)
    for place in range(free):
        weight = jnp.where(lane == place, float(count**place), weight)
    arrived = meta[orbs].astype(jnp.float32) * weight
    for line in range(lines):
        total = jnp.sum(jnp.where(row == lines + line, arrived, 0.0))
        for place, value in enumerate(digits(total, free)):
            index_ref[3 * orbs + line * free + place] = value


def forward_body(orbs, count, grid_cells, where_ref, offset_ref, *refs):
    pieces = [refs[2 * k : 2 * k + 2] for k in range(orbs)]
    incoming = refs[2 * orbs : 2 * orbs + 2]
    near_ref, far_ref, index_ref, meta, held, far_sum, meta_sem, box_sem, listed = refs[
        2 * orbs + 2 : 2 * orbs + 11
    ]
    scratch = refs[2 * orbs + 11 :]
    batch = listed.shape[0] // FIELDS
    part = count // 2
    me = where_ref[2]
    first_left, first_right = where_ref[0], where_ref[1]

    tables = [
        pltpu.make_async_copy(source[0].at[0, 0], meta.at[k], meta_sem.at[k])
        for k, source in enumerate(pieces + [incoming])
    ]
    for copy in tables:
        copy.start()
    rights = [
        pltpu.make_async_copy(
            incoming[n // part].at[n % part], held.at[orbs + n], box_sem.at[orbs + n]
        )
        for n in range(count)
    ]
    for copy in rights:
        copy.start()
    scratch[0][...] = jnp.zeros(scratch[0].shape, jnp.float32)
    clear(far_sum)
    for copy in tables:
        copy.wait()
    read_tables(meta, orbs, me, count, index_ref)
    for k in range(orbs):
        source = jnp.bitwise_xor(me, k)
        piece_copies(pieces[k], index_ref[2 * orbs + source], held, source, box_sem.at[k])
    for k in range(orbs):
        wait_box(pieces[k], held, jnp.bitwise_xor(me, k), box_sem.at[k])
    for copy in rights:
        copy.wait()

    def run(i, carry):
        def gather(j, used):
            slot = i * batch + j
            left, right = slot * count + index_ref[2 * orbs + slot], index_ref[3 * orbs + slot]
            shift, live = geometry(
                offset_ref, first_left + left, first_right + right, grid_cells
            )

            @pl.when(live == 1)
            def _():
                append(listed, used, [slot, orbs + right, *shift])

            @pl.when(live == 0)
            def _():
                for t in range(TILES):
                    near_ref[slot, t] = jnp.zeros((B, LANES), near_ref.dtype)

            return used + live

        used = lax.fori_loop(0, batch, gather, jnp.int32(0))

        def shift_of(m):
            return [listed[m * FIELDS + 2 + axis] for axis in range(3)]

        def near_to(m, t, value):
            near_ref[listed[m * FIELDS], t] = value.astype(near_ref.dtype)

        def far_to(m, t, value):
            far_sum[listed[m * FIELDS + 1] - orbs, t] += value

        every = (0, used)
        run_slots(
            used, every, every, shift_of,
            lambda m, t: held[listed[m * FIELDS], t].astype(jnp.float32),
            lambda m, t: held[listed[m * FIELDS + 1], t].astype(jnp.float32),
            near_to, far_to, scratch,
        )
        return carry

    lax.fori_loop(0, orbs // batch, run, 0)
    for n in range(count):
        for t in range(TILES):
            far_ref[n, t] = far_sum[n, t].astype(far_ref.dtype)


def forward_pairs(where, offsets, pieces, incoming, count, grid_cells):
    orbs = len(pieces)
    vmem, smem, left = (pl.BlockSpec(memory_space=m) for m in (pltpu.VMEM, pltpu.SMEM, pl.ANY))
    shape = (TILES, B, LANES)
    return pl.pallas_call(
        functools.partial(forward_body, orbs, count, grid_cells),
        out_shape=(
            jax.ShapeDtypeStruct((orbs,) + shape, jnp.bfloat16),
            jax.ShapeDtypeStruct((count,) + shape, jnp.bfloat16),
            jax.ShapeDtypeStruct((4 * orbs,), jnp.int32),
        ),
        in_specs=[smem] * 2 + [left] * (2 * orbs + 2),
        out_specs=(vmem, vmem, smem),
        scratch_shapes=[
            pltpu.VMEM((orbs + 1, B, LANES), jnp.bfloat16),
            pltpu.VMEM((orbs + count,) + shape, jnp.bfloat16),
            pltpu.VMEM((count,) + shape, jnp.float32),
            pltpu.SemaphoreType.DMA((orbs + 1,)),
            pltpu.SemaphoreType.DMA((orbs + count,)),
        ] + slot_scratch(8),
        compiler_params=pltpu.CompilerParams(vmem_limit_bytes=VMEM_BYTES),
        name="forward_pairs",
    )(where, offsets, *[half for piece in pieces for half in piece], *incoming)


def group_body(orbs, count, grid_cells, where_ref, offset_ref, mine_ref, sent_ref, index_ref, *refs):
    pieces = [refs[2 * k : 2 * k + 2] for k in range(orbs)]
    field, held, sem, listed = refs[2 * orbs : 2 * orbs + 4]
    scratch = refs[2 * orbs + 4 :]
    half = listed.shape[0] // FIELDS // 2
    part = count // 2
    first, me = where_ref[0], where_ref[2]
    mine = me * count
    own = 2 * orbs

    for k in range(orbs):
        source = jnp.bitwise_xor(me, k)
        piece_copies(pieces[k], index_ref[source], held, source, sem.at[k])
        piece_copies(pieces[k], index_ref[orbs + source], held, orbs + source, sem.at[orbs + k])
    owned = [
        pltpu.make_async_copy(pieces[0][n // part].at[n % part], held.at[own + n], sem.at[own + n])
        for n in range(count)
    ]
    for copy in owned:
        copy.start()
    scratch[0][...] = jnp.zeros(scratch[0].shape, jnp.float32)
    clear(field)
    for k in range(orbs):
        source = jnp.bitwise_xor(me, k)
        wait_box(pieces[k], held, source, sem.at[k])
        wait_box(pieces[k], held, orbs + source, sem.at[orbs + k])
    for copy in owned:
        copy.wait()

    def run(i, carry):
        def listing(near):
            def gather(j, used):
                slot = i * half + lax.rem(me + 1 + j, half)
                if near:
                    left, right = mine + mine_ref[slot], slot * count + index_ref[slot]
                    boxes = [own + mine_ref[slot], slot]
                else:
                    left, right = slot * count + index_ref[orbs + slot], mine + sent_ref[slot]
                    boxes = [orbs + slot, own + sent_ref[slot]]
                shift, live = geometry(offset_ref, first + left, first + right, grid_cells)
                if not near:
                    live = jnp.where(slot == me, 0, live)
                else:
                    boxes[1] = jnp.where(slot == me, own + index_ref[slot], boxes[1])

                @pl.when(live == 1)
                def _():
                    append(listed, used, boxes + [*shift])

                return used + live

            return gather

        near_count = lax.fori_loop(0, half, listing(True), jnp.int32(0))
        used = lax.fori_loop(0, half, listing(False), near_count)
        left, right = mine + mine_ref[me], mine + index_ref[me]
        inside = geometry(offset_ref, first + left, first + right, grid_cells)[1]
        inside = jnp.where(lax.div(me, half) == i, inside, 0)

        def shift_of(m):
            return [listed[m * FIELDS + 2 + axis] for axis in range(3)]

        def near_to(m, t, value):
            field[listed[m * FIELDS] - own, t] += value

        def far_to(m, t, value):
            field[listed[m * FIELDS + 1] - own, t] += value

        run_slots(
            used, (0, near_count), (near_count - inside, used), shift_of,
            lambda m, t: held[listed[m * FIELDS], t].astype(jnp.float32),
            lambda m, t: held[listed[m * FIELDS + 1], t].astype(jnp.float32),
            near_to, far_to, scratch,
        )
        return carry

    lax.fori_loop(0, orbs // half, run, 0)


def group_pairs(where, offsets, mine, sent, index, pieces, count, grid_cells):
    orbs = len(pieces)
    vmem, smem, left = (pl.BlockSpec(memory_space=m) for m in (pltpu.VMEM, pltpu.SMEM, pl.ANY))
    shape = (TILES, B, LANES)
    return pl.pallas_call(
        functools.partial(group_body, orbs, count, grid_cells),
        out_shape=jax.ShapeDtypeStruct((count,) + shape, jnp.float32),
        in_specs=[smem] * 5 + [left] * (2 * orbs),
        out_specs=vmem,
        scratch_shapes=[
            pltpu.VMEM((2 * orbs + count,) + shape, jnp.bfloat16),
            pltpu.SemaphoreType.DMA((2 * orbs + count,)),
        ] + slot_scratch(16),
        compiler_params=pltpu.CompilerParams(vmem_limit_bytes=VMEM_BYTES),
        name="group_pairs",
    )(where, offsets, mine, sent, index, *[half for piece in pieces for half in piece])


def along_space(block, distance):
    size = lax.axis_size("space")
    return lax.ppermute(block, "space", [((i - distance) % size, i) for i in range(size)])


def group_exchange(packed, orbs):
    bits = [1 << i for i in range(orbs.bit_length() - 1)]
    orders = (bits[1:] + bits[:1], bits[:0:-1] + bits[:1])
    halves = []
    for block, order in zip(packed, orders):
        known = {0: block}
        for bit in order:
            route = [(i, i ^ bit) for i in range(orbs)]
            for k in list(known):
                known[k ^ bit] = lax.ppermute(known[k], "orb", route)
        halves.append(known)
    return [[known[k] for known in halves] for k in range(orbs)]


def per_device(orbitals, box_offset, send_index, pair_left):
    count = orbitals.shape[0]
    spaces, orbs = lax.axis_size("space"), lax.axis_size("orb")
    grid_cells = spaces * HALF
    space, orb = lax.axis_index("space"), lax.axis_index("orb")
    group_first = space * orbs * count
    offsets = box_offset.reshape(-1)

    free = LANES - USED
    entries = jnp.concatenate([send_index[0].reshape(-1), pair_left[0].reshape(-1)])
    lines = 4 * orbs // free
    table = jnp.pad(
        entries.astype(jnp.float32).reshape(lines, free), ((0, B - lines), (USED, 0))
    )
    packed = pack(orbitals, table)

    incoming = [along_space(half, -1) for half in packed]
    pieces = group_exchange(packed, orbs)
    where = jnp.stack([group_first, ((space + 1) % spaces * orbs + orb) * count, orb])
    near, far, index = forward_pairs(where, offsets, pieces, incoming, count, grid_cells)
    near = lax.all_to_all(near, "orb", split_axis=0, concat_axis=0, tiled=True)
    far = along_space(far, 1)
    field = group_pairs(
        where, offsets, pair_left[0, 0], send_index[0, 0], index, pieces, count, grid_cells
    )
    return finish(field, near, far, pair_left[0, 1])


def solution(mesh):
    split = P(("space", "orb"), None, None)
    return jax.shard_map(
        per_device, mesh=mesh, in_specs=(split, P(), split, split), out_specs=split,
        check_vma=False,
    )
```

```python
import functools

import jax
import jax.numpy as jnp
from jax import lax
from jax.experimental import pallas as pl
from jax.experimental.pallas import tpu as pltpu
from jax.sharding import PartitionSpec as P

B = 40
ITERS = 4
SCREEN = 0.25

GROUPS = 3
TILES = 14
LANES = 128
USED = GROUPS * B
SUB = 8
PLANES = B // SUB
CELLS = TILES * PLANES
CELL = 2 * SUB
HALF = B // 2
VMEM_BYTES = 52 * 2**20
FIELDS = 8
EARLY_LIMIT = 6
LATE_LIMIT = 2


def lanes_of(shape):
    return lax.broadcasted_iota(jnp.int32, shape, len(shape) - 1)


def overlaps():
    pieces = []
    for b in range(B):
        group = b // TILES
        for flat in range(b * B // LANES, (b * B + B - 1) // LANES + 1):
            pieces.append((b, flat, b * B - flat * LANES - group * B))
    return pieces


def pack_body(box_ref, table_ref, first_ref, second_ref, stage):
    count = box_ref.shape[0]
    lane = lanes_of((B, LANES))
    for n in range(count):
        tiles = [jnp.zeros((B, LANES), jnp.float32) for _ in range(TILES)]
        loaded = {}
        for b, flat, shift in overlaps():
            if flat not in loaded:
                width = min(LANES, B * B - flat * LANES)
                part = box_ref[n, :, flat * LANES : flat * LANES + width].astype(jnp.float32)
                if width < LANES:
                    part = jnp.concatenate(
                        [part, jnp.zeros((B, LANES - width), jnp.float32)], axis=1
                    )
                stage[flat] = part
                loaded[flat] = jnp.concatenate(
                    [stage[flat, pl.ds(p, SUB, stride=PLANES), :] for p in range(PLANES)], axis=0
                )
            first = max(b * B, flat * LANES) - b * B + (b // TILES) * B
            last = min(b * B + B, flat * LANES + LANES) - b * B + (b // TILES) * B
            moved = pltpu.roll(loaded[flat], (-shift) % LANES, axis=1)
            keep = (lane >= first) & (lane < last)
            tiles[b % TILES] = jnp.where(keep, moved, tiles[b % TILES])
        if n == 0:
            tiles[0] = tiles[0] + table_ref[...]
        out_ref = first_ref if n < count // 2 else second_ref
        for t in range(TILES):
            out_ref[n % (count // 2), t] = tiles[t].astype(out_ref.dtype)


def pack(orbitals, table):
    count = orbitals.shape[0]
    return pl.pallas_call(
        pack_body,
        out_shape=[jax.ShapeDtypeStruct((count // 2, TILES, B, LANES), jnp.bfloat16)] * 2,
        in_specs=[pl.BlockSpec(memory_space=pltpu.VMEM)] * 2,
        out_specs=[pl.BlockSpec(memory_space=pltpu.VMEM)] * 2,
        scratch_shapes=[pltpu.VMEM((-(-B * B // LANES), B, LANES), jnp.float32)],
        compiler_params=pltpu.CompilerParams(vmem_limit_bytes=VMEM_BYTES),
        name="pack",
    )(orbitals, table)


def finish_body(count, slots, field_ref, near_ref, far_ref, row_ref, out_ref, total, stage):
    lane = lanes_of((B, LANES))
    for n in range(count):
        for t in range(TILES):
            total[n, t] = field_ref[n, t] + far_ref[n, t].astype(jnp.float32)

    def add(j, carry):
        row = row_ref[j]
        for t in range(TILES):
            total[row, t] += near_ref[j, t].astype(jnp.float32)
        return carry

    lax.fori_loop(0, slots, add, 0)
    for n in range(count):
        flats = {}
        for b, flat, shift in overlaps():
            first = max(b * B, flat * LANES) - flat * LANES
            last = min(b * B + B, flat * LANES + LANES) - flat * LANES
            moved = pltpu.roll(total[n, b % TILES], shift % LANES, axis=1)
            keep = (lane >= first) & (lane < last)
            before = flats.get(flat)
            flats[flat] = moved if before is None else jnp.where(keep, moved, before)
        for flat, value in flats.items():
            for p in range(PLANES):
                stage[flat, pl.ds(p, SUB, stride=PLANES), :] = value[p * SUB : p * SUB + SUB]
            width = min(LANES, B * B - flat * LANES)
            out_ref[n, :, flat * LANES : flat * LANES + width] = stage[flat, :, :width]


def finish(field, near, far, rows):
    count, slots = field.shape[0], near.shape[0]
    vmem = pl.BlockSpec(memory_space=pltpu.VMEM)
    return pl.pallas_call(
        functools.partial(finish_body, count, slots),
        out_shape=jax.ShapeDtypeStruct((count, B, B * B), jnp.float32),
        in_specs=[vmem, vmem, vmem, pl.BlockSpec(memory_space=pltpu.SMEM)],
        out_specs=vmem,
        scratch_shapes=[
            pltpu.VMEM((count, TILES, B, LANES), jnp.float32),
            pltpu.VMEM((-(-B * B // LANES), B, LANES), jnp.float32),
        ],
        compiler_params=pltpu.CompilerParams(vmem_limit_bytes=VMEM_BYTES),
        name="finish",
    )(field, near, far, rows)


def geometry(offset_ref, left, right, grid_cells):
    shift, live = [], jnp.int32(1)
    for axis in range(3):
        gap = offset_ref[3 * right + axis] - offset_ref[3 * left + axis] + grid_cells // 2
        gap = jnp.where(gap < 0, gap + grid_cells, gap)
        gap = jnp.where(gap >= grid_cells, gap - grid_cells, gap) - grid_cells // 2
        live = jnp.where((gap > HALF) | (gap < -HALF), 0, live)
        shift.append(gap)
    return shift, live


def wrapped(shift, size):
    start = lax.rem(B * size - shift, size)
    turn = lax.div(B * size - shift, size) - B
    pairs = []
    for i in range(size):
        over = jnp.where(start + i >= size, 1, 0)
        pairs.append((start + i - size * over, turn + over))
    return pairs


def put_padded(pad, t, p, value):
    start = (t * PLANES + p) * CELL + SUB
    pad[start : start + SUB, :] = value


def displaced(pad, shift):
    lane = lanes_of((SUB, LANES))
    group = lane // B
    source_col = lane - group * B - shift[2]
    col_ok = (source_col >= 0) & (source_col < B) & (lane < USED)
    source_row = jnp.where(col_ok, TILES * group - shift[1], -2 * B)
    rows = [p * CELL + SUB + turn for p, turn in wrapped(shift[0], PLANES)]
    for t, (source, turn) in enumerate(wrapped(shift[1], TILES)):
        keep = (source_row + t >= 0) & (source_row + t < B)
        if t >= B - TILES * (GROUPS - 1):
            keep = keep & (lane < USED - B)
        amount = (shift[2] - B * turn + 2 * LANES) & (LANES - 1)
        tile = []
        for p in range(PLANES):
            block = pad[pl.ds(source * (PLANES * CELL) + rows[p], SUB), :]
            tile.append(jnp.where(keep, pltpu.roll(block, amount, axis=1), 0.0))
        yield t, tile


def tree_sum(values):
    while len(values) > 1:
        paired = [a + b for a, b in zip(values[::2], values[1::2])]
        values = paired + ([values[-1]] if len(values) % 2 else [])
    return values[0]


def blocks(value):
    return [value[p * SUB : p * SUB + SUB] for p in range(PLANES)]


def cell(t, p):
    start = (t * PLANES + p) * SUB
    return slice(start, start + SUB)


def make_operator():
    lane = lanes_of((SUB, LANES))
    sublane = lax.broadcasted_iota(jnp.int32, (SUB, LANES), 0)
    column = lane % B
    has_before = (column > 0) & (lane < USED)
    has_after = (column < B - 1) & (lane < USED)
    not_first = lane >= B
    not_last = lane < USED - B
    has_above = sublane > 0
    has_below = sublane < SUB - 1

    def operator(t, before, here, after):
        if t == 0:
            before = [jnp.where(not_first, pltpu.roll(v, B, axis=1), 0.0) for v in before]
        if t == TILES - 1:
            after = [jnp.where(not_last, pltpu.roll(v, LANES - B, axis=1), 0.0) for v in after]
        result = []
        for p in range(PLANES):
            if p == 0:
                above = jnp.where(has_above, pltpu.roll(here[PLANES - 1], 1, axis=0), 0.0)
            else:
                above = here[p - 1]
            if p == PLANES - 1:
                below = jnp.where(has_below, pltpu.roll(here[0], SUB - 1, axis=0), 0.0)
            else:
                below = here[p + 1]
            prior = jnp.where(has_before, pltpu.roll(here[p], 1, axis=1), 0.0)
            following = jnp.where(has_after, pltpu.roll(here[p], LANES - 1, axis=1), 0.0)
            around = (above + below) + (before[p] + after[p]) + (prior + following)
            value = (6.0 + SCREEN) * here[p] - around
            if t == B - TILES * (GROUPS - 1):
                value = jnp.where(not_last, value, 0.0)
            result.append(value)
        return result

    return operator


def side_by_side(used, body):
    def pair(i, carry):
        for _ in zip(body(2 * i, 0), body(2 * i + 1, 1)):
            pass
        return carry

    lax.fori_loop(0, lax.div(used, 2), pair, 0)

    @pl.when(lax.rem(used, 2) == 1)
    def _():
        for _ in body(used - 1, 0):
            pass


def solve(used, directions, residuals, image, partial, norms, steps, ratios):
    operator = make_operator()

    def totals():
        rows = jnp.sum(partial[...], axis=1)
        return jnp.broadcast_to(jnp.sum(rows, axis=1, keepdims=True), rows.shape)

    norms[...] = totals()
    for k in range(ITERS):
        last = k == ITERS - 1

        residual = residuals[(k - 1) % 2]

        def stencil(m, side, k=k, last=last, residual=residual):
            if k > 0:
                ratio = jnp.broadcast_to(ratios[pl.ds(m, 1), :], (SUB, LANES))

            def fetch(t, keep):
                values = []
                for p in range(PLANES):
                    if k == 0:
                        value = directions[0][m, cell(t, p), :]
                    else:
                        value = residual[m, cell(t, p), :]
                        value = value + ratio * directions[k - 1][m, cell(t, p), :]
                        if keep:
                            directions[k][m, cell(t, p), :] = value
                    values.append(value)
                return values

            before, here = fetch(TILES - 1, False), fetch(0, True)
            total = None
            for t in range(TILES):
                after = fetch((t + 1) % TILES, t < TILES - 1)
                applied = operator(t, before, here, after)
                if not last:
                    for p in range(PLANES):
                        image[m, cell(t, p), :] = applied[p]
                part = tree_sum([x * y for x, y in zip(here, applied)])
                total = part if total is None else total + part
                before, here = here, after
                yield
            partial[m] = total
            yield

        side_by_side(used, stencil)
        steps[k] = norms[...] / totals()
        if last:
            break
        source = directions[0] if k == 0 else residual
        target = residuals[k % 2]

        def reduce(m, side, k=k, source=source, target=target):
            step = jnp.broadcast_to(steps[k, pl.ds(m, 1), :], (SUB, LANES))
            total = None
            for t in range(TILES):
                squares = []
                for p in range(PLANES):
                    value = source[m, cell(t, p), :] - step * image[m, cell(t, p), :]
                    target[m, cell(t, p), :] = value
                    squares.append(value * value)
                part = tree_sum(squares)
                total = part if total is None else total + part
                yield
            partial[m] = total
            yield

        side_by_side(used, reduce)
        new = totals()
        ratios[...] = new / norms[...]
        norms[...] = new


def run_slots(used, forward, near, far, arrived, shift_of, held, sinks, scratch):
    pads, shifted, partial, norms, steps, ratios, odd, even, image, *directions = scratch

    def left_at(m, t):
        return blocks(held[2 * m, t].astype(jnp.float32))

    def load(m, side):
        arrived(m)
        pad = pads.at[side]
        for t in range(TILES):
            for p, block in enumerate(blocks(held[2 * m + 1, t].astype(jnp.float32))):
                put_padded(pad, t, p, block)
            yield
        total = None
        for t, moved in displaced(pad, shift_of(m)):
            squares = []
            for p, left in enumerate(left_at(m, t)):
                shifted[m, cell(t, p), :] = moved[p]
                density = moved[p] * left
                directions[0][m, cell(t, p), :] = density
                squares.append(density * density)
            part = tree_sum(squares)
            total = part if total is None else total + part
            yield
        partial[m] = total
        yield

    side_by_side(used, load)
    solve(used, directions, (odd, even), image, partial, norms, steps, ratios)

    def unload(near_to, far_to):
        def one(m, carry):
            pad = pads.at[0]
            weights = [
                jnp.broadcast_to(steps[k, pl.ds(m, 1), :], (SUB, LANES)) for k in range(ITERS)
            ]
            put_near = near_to(m) if near_to else None
            put_far = far_to(m) if far_to else None
            for t in range(TILES):
                solved = [
                    tree_sum([w * d[m, cell(t, p), :] for w, d in zip(weights, directions)])
                    for p in range(PLANES)
                ]
                if near_to:
                    terms = [v * shifted[m, cell(t, p), :] for p, v in enumerate(solved)]
                    put_near(t, jnp.concatenate(terms, axis=0))
                if far_to:
                    for p, left in enumerate(left_at(m, t)):
                        put_padded(pad, t, p, solved[p] * left)
            if far_to:
                for t, moved in displaced(pad, [-s for s in shift_of(m)]):
                    put_far(t, jnp.concatenate(moved, axis=0))
            return carry

        return one

    if forward is not None:
        lax.fori_loop(*forward, unload(sinks["forward_near"], sinks["forward_far"]), 0)
    lax.fori_loop(*near, unload(sinks["near"], None), 0)
    lax.fori_loop(*far, unload(None, sinks["far"]), 0)


def slot_scratch(batch):
    row = pltpu.VMEM((batch, LANES), jnp.float32)
    box = pltpu.VMEM((batch, CELLS * SUB, LANES), jnp.float32)
    return [
        pltpu.SMEM((batch * FIELDS,), jnp.int32),
        pltpu.VMEM((2, CELLS * CELL + SUB, LANES), jnp.float32),
        box,
        pltpu.VMEM((batch, SUB, LANES), jnp.float32),
        row,
        pltpu.VMEM((ITERS, batch, LANES), jnp.float32),
        row,
    ] + [box] * (3 + ITERS)


def clear(ref):
    for n in range(ref.shape[0]):
        for t in range(TILES):
            ref[n, t] = jnp.zeros((B, LANES), ref.dtype)


def fetch(pieces, index, target, sem):
    part = pieces[0].shape[0]
    for h, piece in enumerate(pieces):

        @pl.when(lax.div(index, part) == h)
        def _(h=h, piece=piece):
            pltpu.make_async_copy(piece.at[index - h * part], target, sem).start()


def read_tables(meta, sources, orbs, me, count, index_ref):
    free = LANES - USED
    lines = orbs // free
    row = lax.broadcasted_iota(jnp.int32, (B, LANES), 0)
    lane = lanes_of((B, LANES)) - USED

    def digits(value, length):
        value = value.astype(jnp.int32)
        for _ in range(length):
            rest = lax.div(value, count)
            yield value - rest * count
            value = rest

    weight = jnp.zeros((B, LANES), jnp.float32)
    for place, kind in enumerate((0, 2, 3)):
        chosen = (row == kind * lines + lax.div(me, free)) & (lane == lax.rem(me, free))
        weight = jnp.where(chosen, float(count**place), weight)
    for i, k in enumerate(sources):
        total = jnp.sum(meta[i].astype(jnp.float32) * weight)
        for kind, value in enumerate(digits(total, 3)):
            index_ref[kind * orbs + k] = value
    if meta.shape[0] > len(sources):
        weight = jnp.zeros((B, LANES), jnp.float32)
        for place in range(free):
            weight = jnp.where(lane == place, float(count**place), weight)
        arrived = meta[len(sources)].astype(jnp.float32) * weight
        for line in range(lines):
            total = jnp.sum(jnp.where(row == lines + line, arrived, 0.0))
            for place, value in enumerate(digits(total, free)):
                index_ref[3 * orbs + line * free + place] = value


def pairs_body(plan, *refs):
    orbs, count, first, last = plan["orbs"], plan["count"], plan["first"], plan["last"]
    fresh, forward, inner = plan["fresh"], plan["forward"], plan["inner"]
    refs = list(refs)

    def take(number):
        taken = refs[:number]
        del refs[:number]
        return taken

    where_ref, offset_ref, mine_ref, sent_ref = take(4)
    index_in, done_in, field_in = (None,) * 3 if first else take(3)
    near_in, far_in = (None,) * 2 if first or last else take(2)
    pieces = {k: take(2) for k in plan["present"]}
    incoming = None if last else take(2)
    (field,) = take(1)
    index_ref, done = (index_in, None) if last else take(2)
    near_ref, far_ref = (None,) * 2 if last else take(2)
    listed, held, sem, flags, state_sem = take(5)
    if not last:
        meta, far_sum = take(2)
    if first:
        far_sum = far_ref
    scratch = refs
    batch = held.shape[0] // 2
    group_first, next_first, me = where_ref[0], where_ref[1], where_ref[2]
    mine = group_first + me * count
    grid_cells = plan["grid_cells"]

    def start(source, target, number):
        copy = pltpu.make_async_copy(source, target, state_sem.at[number])
        copy.start()
        return copy

    waiting, tables = [], []
    if not last:
        sources = [pieces[k] for k in fresh] + ([incoming] if first else [])
        for i, source in enumerate(sources):
            tables.append(start(source[0].at[0, 0], meta.at[i], i))
    if not first:
        waiting.append(start(field_in, field, orbs + 1))
        if not last:
            waiting.append(start(far_in, far_sum, orbs + 2))
            waiting.append(start(near_in, near_ref, orbs + 3))
    scratch[0][...] = jnp.zeros(scratch[0].shape, jnp.float32)
    if first:
        clear(field)
        clear(far_sum)
    for kind in range(3):
        for k in range(orbs):
            flags[kind * orbs + k] = 0 if first else done_in[kind * orbs + k]
    if not first and not last:
        for i in range(4 * orbs):
            index_ref[i] = index_in[i]
    for copy in tables:
        copy.wait()
    if not last:
        read_tables(meta, fresh, orbs, me, count, index_ref)
    for copy in waiting:
        copy.wait()

    def consider(kind, k, used, limit):
        slot = jnp.bitwise_xor(me, k)
        theirs = group_first + slot * count
        if kind == 0:
            boxes = [(pieces[k], index_ref[2 * orbs + k]), (incoming, index_ref[3 * orbs + slot])]
            left, right = theirs + boxes[0][1], next_first + boxes[1][1]
        elif kind == 1:
            boxes = [(pieces[0], mine_ref[slot]), (pieces[k], index_ref[k])]
            left, right = mine + boxes[0][1], theirs + boxes[1][1]
        else:
            boxes = [(pieces[k], index_ref[orbs + k]), (pieces[0], sent_ref[slot])]
            left, right = theirs + boxes[0][1], mine + boxes[1][1]
        shift, live = geometry(offset_ref, left, right, grid_cells)
        if kind == 0:

            @pl.when(live == 0)
            def _():
                for t in range(TILES):
                    near_ref[slot, t] = jnp.zeros((B, LANES), near_ref.dtype)

        chosen = jnp.where((flags[kind * orbs + k] == 0) & (used < limit), live, 0)

        @pl.when(chosen == 1)
        def _():
            flags[kind * orbs + k] = 1
            near_row, far_row = (slot if kind == 0 else boxes[0][1]), boxes[1][1]
            for i, value in enumerate([*shift, near_row, far_row]):
                listed[used * FIELDS + i] = value
            for side, (source, index) in enumerate(boxes):
                fetch(source, index, held.at[2 * used + side], sem.at[2 * used + side])

        return used + chosen

    def arrived(m):
        for side in range(2):
            pltpu.make_async_copy(
                pieces[0][0].at[0], held.at[2 * m + side], sem.at[2 * m + side]
            ).wait()

    def shift_of(m):
        return [listed[m * FIELDS + axis] for axis in range(3)]

    def adding(ref, place):
        def sink(m):
            row = listed[m * FIELDS + place]

            def put(t, value):
                ref[row, t] += value

            return put

        return sink

    def forward_near(m):
        row = listed[m * FIELDS + 3]

        def put(t, value):
            near_ref[row, t] = value.astype(near_ref.dtype)

        return put

    sinks = {"near": adding(field, 3), "far": adding(field, 4)}
    if forward:
        sinks["forward_near"] = forward_near
        sinks["forward_far"] = adding(far_sum, 4)

    def run(i, carry):
        used = jnp.int32(0)
        for k in forward:
            used = consider(0, k, used, batch)
        forwards = used
        for k in inner[1:]:
            used = consider(1, k, used, plan["limit"])
        before = used
        used = consider(1, 0, used, plan["limit"])
        nears, inside = used, used - before
        for k in inner[1:]:
            used = consider(2, k, used, plan["limit"])
        run_slots(
            used, (0, forwards) if forward else None, (forwards, nears), (nears - inside, used),
            arrived, shift_of, held, sinks, scratch,
        )
        return carry

    needed = max(len(forward), 2 * len(inner) - 1 if last else 0)
    lax.fori_loop(0, -(-needed // batch), run, 0)
    if not last:
        for kind in range(3):
            for k in range(orbs):
                done[kind * orbs + k] = flags[kind * orbs + k]
    if not first and not last:
        for n in range(count):
            for t in range(TILES):
                far_ref[n, t] = far_sum[n, t].astype(far_ref.dtype)


def pairs(plan, tables, state, pieces, incoming, batch, name):
    orbs, count, first, last = plan["orbs"], plan["count"], plan["first"], plan["last"]
    vmem, smem, left = (pl.BlockSpec(memory_space=m) for m in (pltpu.VMEM, pltpu.SMEM, pl.ANY))
    shape = (TILES, B, LANES)
    operands, in_specs = list(tables), [smem] * 4
    if not first:
        operands += state
        in_specs += [smem] * 2 + [left] * (len(state) - 2)
    flat = [half for k in plan["present"] for half in pieces[k]] + (incoming or [])
    out_shape = [jax.ShapeDtypeStruct((count,) + shape, jnp.float32)]
    out_specs = [vmem]
    scratch = [
        pltpu.SMEM((batch * FIELDS,), jnp.int32),
        pltpu.VMEM((2 * batch,) + shape, jnp.bfloat16),
        pltpu.SemaphoreType.DMA((2 * batch,)),
        pltpu.SMEM((3 * orbs,), jnp.int32),
        pltpu.SemaphoreType.DMA((orbs + 4,)),
    ]
    if not last:
        out_shape += [
            jax.ShapeDtypeStruct((4 * orbs,), jnp.int32),
            jax.ShapeDtypeStruct((3 * orbs,), jnp.int32),
            jax.ShapeDtypeStruct((orbs,) + shape, jnp.bfloat16),
            jax.ShapeDtypeStruct((count,) + shape, jnp.float32 if first else jnp.bfloat16),
        ]
        out_specs += [smem] * 2 + [vmem] * 2
        far_rows = 1 if first else count
        scratch += [
            pltpu.VMEM((len(plan["fresh"]) + (1 if first else 0), B, LANES), jnp.bfloat16),
            pltpu.VMEM((far_rows,) + shape, jnp.float32),
        ]
    return pl.pallas_call(
        functools.partial(pairs_body, plan),
        out_shape=out_shape,
        in_specs=in_specs + [left] * len(flat),
        out_specs=out_specs,
        scratch_shapes=scratch + slot_scratch(batch)[1:],
        compiler_params=pltpu.CompilerParams(vmem_limit_bytes=VMEM_BYTES),
        cost_estimate=pl.CostEstimate(
            flops=plan["limit"] * 8 * 10**6, bytes_accessed=plan["limit"] * 10**6, transcendentals=0
        ),
        name=name,
    )(*operands, *flat)


def along_space(block, distance):
    size = lax.axis_size("space")
    return lax.ppermute(block, "space", [((i - distance) % size, i) for i in range(size)])


def group_exchange(packed, orbs):
    bits = [1 << i for i in range(orbs.bit_length() - 1)]
    orders = (bits[1:] + bits[:1], bits[:0:-1] + bits[:1])
    halves = []
    for block, order in zip(packed, orders):
        known = {0: block}
        for bit in order:
            route = [(i, i ^ bit) for i in range(orbs)]
            for k in list(known):
                known[k ^ bit] = lax.ppermute(known[k], "orb", route)
        halves.append(known)
    return [[known[k] for known in halves] for k in range(orbs)]


def per_device(orbitals, box_offset, send_index, pair_left):
    count = orbitals.shape[0]
    spaces, orbs = lax.axis_size("space"), lax.axis_size("orb")
    grid_cells = spaces * HALF
    space, orb = lax.axis_index("space"), lax.axis_index("orb")
    group_first = space * orbs * count
    offsets = box_offset.reshape(-1)

    free = LANES - USED
    entries = jnp.concatenate([send_index[0].reshape(-1), pair_left[0].reshape(-1)])
    lines = 4 * orbs // free
    table = jnp.pad(
        entries.astype(jnp.float32).reshape(lines, free), ((0, B - lines), (USED, 0))
    )
    packed = pack(orbitals, table)

    incoming = [along_space(half, -1) for half in packed]
    pieces = group_exchange(packed, orbs)
    where = jnp.stack([group_first, ((space + 1) % spaces * orbs + orb) * count, orb])
    known = (where, offsets, pair_left[0, 0], send_index[0, 0])
    every = list(range(orbs))
    early, late = every[: 3 * orbs // 4], every[3 * orbs // 4 :]
    plan = {"orbs": orbs, "count": count, "grid_cells": grid_cells, "first": False, "last": False}

    begin = plan | {
        "first": True, "present": early, "fresh": early, "forward": early, "inner": early,
        "limit": EARLY_LIMIT,
    }
    field, index, done, near, far = pairs(begin, known, [], pieces, incoming, 8, "early_pairs")
    middle = plan | {
        "present": every, "fresh": late, "forward": late, "inner": every, "limit": LATE_LIMIT,
    }
    field, index, done, near, far = pairs(
        middle, known, [index, done, field, near, far], pieces, incoming, 8, "late_pairs"
    )
    near = lax.all_to_all(near, "orb", split_axis=0, concat_axis=0, tiled=True)
    far = along_space(far, 1)
    end = plan | {
        "last": True, "present": every, "fresh": [], "forward": [], "inner": every, "limit": 16,
    }
    (field,) = pairs(end, known, [index, done, field], pieces, None, 16, "rest_pairs")
    return finish(field, near, far, pair_left[0, 1])


def solution(mesh):
    split = P(("space", "orb"), None, None)
    return jax.shard_map(
        per_device, mesh=mesh, in_specs=(split, P(), split, split), out_specs=split,
        check_vma=False,
    )
```

```python
import functools

import jax
import jax.numpy as jnp
from jax import lax
from jax.experimental import pallas as pl
from jax.experimental.pallas import tpu as pltpu
from jax.sharding import PartitionSpec as P

B = 40
ITERS = 4
SCREEN = 0.25

GROUPS = 3
TILES = 14
LANES = 128
USED = GROUPS * B
SUB = 8
PLANES = B // SUB
CELLS = TILES * PLANES
CELL = 2 * SUB
HALF = B // 2
VMEM_BYTES = 52 * 2**20
FIELDS = 8
FILL = 6


def lanes_of(shape):
    return lax.broadcasted_iota(jnp.int32, shape, len(shape) - 1)


def overlaps():
    pieces = []
    for b in range(B):
        group = b // TILES
        for flat in range(b * B // LANES, (b * B + B - 1) // LANES + 1):
            pieces.append((b, flat, b * B - flat * LANES - group * B))
    return pieces


def flat_width(flat):
    return min(LANES, B * B - flat * LANES)


def pack_body(box_ref, send_ref, left_ref, first_ref, second_ref, boxes, stage, sem):
    count = box_ref.shape[0]
    copies = [pltpu.make_async_copy(box_ref.at[n], boxes.at[n], sem.at[n]) for n in range(count)]
    for copy in copies:
        copy.start()
    lane = lanes_of((B, LANES))
    row = lax.broadcasted_iota(jnp.int32, (B, LANES), 0)
    orbs = send_ref.shape[2]
    place = row * (LANES - USED) + lane - USED
    place = jnp.where(lane >= USED, place, -1)
    table = jnp.zeros((B, LANES), jnp.int32)
    for i, ref in enumerate((send_ref, left_ref)):
        for g in range(2):
            for o in range(orbs):
                table = jnp.where(place == (2 * i + g) * orbs + o, ref[0, g, o], table)
    for n in range(count):
        copies[n].wait()
        tiles = [jnp.zeros((B, LANES), jnp.float32) for _ in range(TILES)]
        loaded = {}
        for b, flat, shift in overlaps():
            if flat not in loaded:
                width = flat_width(flat)
                part = boxes[n, :, flat * LANES : flat * LANES + width].astype(jnp.float32)
                if width < LANES:
                    part = jnp.concatenate(
                        [part, jnp.zeros((B, LANES - width), jnp.float32)], axis=1
                    )
                stage[flat] = part
                loaded[flat] = jnp.concatenate(
                    [stage[flat, pl.ds(p, SUB, stride=PLANES), :] for p in range(PLANES)], axis=0
                )
            first = max(b * B, flat * LANES) - b * B + (b // TILES) * B
            last = min(b * B + B, flat * LANES + LANES) - b * B + (b // TILES) * B
            moved = pltpu.roll(loaded[flat], (-shift) % LANES, axis=1)
            keep = (lane >= first) & (lane < last)
            tiles[b % TILES] = jnp.where(keep, moved, tiles[b % TILES])
        if n == 0:
            tiles[0] = tiles[0] + table.astype(jnp.float32)
        out_ref = first_ref if n < count // 2 else second_ref
        for t in range(TILES):
            out_ref[n % (count // 2), t] = tiles[t].astype(out_ref.dtype)


def pack(orbitals, send_index, pair_left):
    count = orbitals.shape[0]
    smem = pl.BlockSpec(memory_space=pltpu.SMEM)
    return pl.pallas_call(
        pack_body,
        out_shape=[jax.ShapeDtypeStruct((count // 2, TILES, B, LANES), jnp.bfloat16)] * 2,
        in_specs=[pl.BlockSpec(memory_space=pl.ANY), smem, smem],
        out_specs=[pl.BlockSpec(memory_space=pltpu.VMEM)] * 2,
        scratch_shapes=[
            pltpu.VMEM(orbitals.shape, jnp.bfloat16),
            pltpu.VMEM((-(-B * B // LANES), B, LANES), jnp.float32),
            pltpu.SemaphoreType.DMA((count,)),
        ],
        compiler_params=pltpu.CompilerParams(vmem_limit_bytes=VMEM_BYTES),
        name="pack",
    )(orbitals, send_index, pair_left)


def finish_body(field_ref, near_ref, far_ref, left_ref, out_ref, total, near, far, made, stage, *sems):
    count, slots = field_ref.shape[0], near_ref.shape[0]
    field_sem, near_sem, far_sem, out_sem = sems

    def copy(source, target, sem):
        made = pltpu.make_async_copy(source, target, sem)
        made.start()
        return made

    fields = [copy(field_ref.at[n], total.at[n], field_sem.at[n]) for n in range(count)]
    fars = [copy(far_ref.at[n], far.at[n], far_sem.at[n]) for n in range(count)]
    nears = [copy(near_ref.at[j], near.at[j], near_sem.at[j]) for j in range(slots)]
    for n in range(count):
        fields[n].wait()
        fars[n].wait()
        for t in range(TILES):
            total[n, t] += far[n, t].astype(jnp.float32)
    for j in range(slots):
        nears[j].wait()
        row = left_ref[0, 1, j]
        for t in range(TILES):
            total[row, t] += near[j, t].astype(jnp.float32)
    lane = lanes_of((B, LANES))
    sent = []
    for n in range(count):
        flats = {}
        for b, flat, shift in overlaps():
            first = max(b * B, flat * LANES) - flat * LANES
            last = min(b * B + B, flat * LANES + LANES) - flat * LANES
            moved = pltpu.roll(total[n, b % TILES], shift % LANES, axis=1)
            keep = (lane >= first) & (lane < last)
            before = flats.get(flat)
            flats[flat] = moved if before is None else jnp.where(keep, moved, before)
        for flat, value in flats.items():
            for p in range(PLANES):
                stage[flat, pl.ds(p, SUB, stride=PLANES), :] = value[p * SUB : p * SUB + SUB]
            width = flat_width(flat)
            made[n, :, flat * LANES : flat * LANES + width] = stage[flat, :, :width]
        sent.append(copy(made.at[n], out_ref.at[n], out_sem.at[n]))
    for one in sent:
        one.wait()


def finish(field, near, far, pair_left):
    count, slots = field.shape[0], near.shape[0]
    left = pl.BlockSpec(memory_space=pl.ANY)
    shape = (TILES, B, LANES)
    return pl.pallas_call(
        finish_body,
        out_shape=jax.ShapeDtypeStruct((count, B, B * B), jnp.float32),
        in_specs=[left] * 3 + [pl.BlockSpec(memory_space=pltpu.SMEM)],
        out_specs=left,
        scratch_shapes=[
            pltpu.VMEM((count,) + shape, jnp.float32),
            pltpu.VMEM((slots,) + shape, near.dtype),
            pltpu.VMEM((count,) + shape, far.dtype),
            pltpu.VMEM((count, B, B * B), jnp.float32),
            pltpu.VMEM((-(-B * B // LANES), B, LANES), jnp.float32),
        ] + [pltpu.SemaphoreType.DMA((size,)) for size in (count, slots, count, count)],
        compiler_params=pltpu.CompilerParams(vmem_limit_bytes=VMEM_BYTES),
        name="finish",
    )(field, near, far, pair_left)


def geometry(offset_ref, left, right, grid_cells):
    shift, live = [], jnp.int32(1)
    for axis in range(3):
        gap = offset_ref[3 * right + axis] - offset_ref[3 * left + axis] + grid_cells // 2
        gap = jnp.where(gap < 0, gap + grid_cells, gap)
        gap = jnp.where(gap >= grid_cells, gap - grid_cells, gap) - grid_cells // 2
        live = jnp.where((gap > HALF) | (gap < -HALF), 0, live)
        shift.append(gap)
    return shift, live


def wrapped(shift, size):
    start = lax.rem(B * size - shift, size)
    turn = lax.div(B * size - shift, size) - B
    pairs = []
    for i in range(size):
        over = jnp.where(start + i >= size, 1, 0)
        pairs.append((start + i - size * over, turn + over))
    return pairs


def put_padded(pad, t, p, value):
    start = (t * PLANES + p) * CELL + SUB
    pad[start : start + SUB, :] = value


def displaced(pad, shift):
    lane = lanes_of((SUB, LANES))
    group = lane // B
    source_col = lane - group * B - shift[2]
    col_ok = (source_col >= 0) & (source_col < B) & (lane < USED)
    source_row = jnp.where(col_ok, TILES * group - shift[1], -2 * B)
    rows = [p * CELL + SUB + turn for p, turn in wrapped(shift[0], PLANES)]
    for t, (source, turn) in enumerate(wrapped(shift[1], TILES)):
        keep = (source_row + t >= 0) & (source_row + t < B)
        if t >= B - TILES * (GROUPS - 1):
            keep = keep & (lane < USED - B)
        amount = (shift[2] - B * turn + 2 * LANES) & (LANES - 1)
        tile = []
        for p in range(PLANES):
            block = pad[pl.ds(source * (PLANES * CELL) + rows[p], SUB), :]
            tile.append(jnp.where(keep, pltpu.roll(block, amount, axis=1), 0.0))
        yield t, tile


def tree_sum(values):
    while len(values) > 1:
        paired = [a + b for a, b in zip(values[::2], values[1::2])]
        values = paired + ([values[-1]] if len(values) % 2 else [])
    return values[0]


def blocks(value):
    return [value[p * SUB : p * SUB + SUB] for p in range(PLANES)]


def cell(t, p):
    start = (t * PLANES + p) * SUB
    return slice(start, start + SUB)


def make_operator():
    lane = lanes_of((SUB, LANES))
    sublane = lax.broadcasted_iota(jnp.int32, (SUB, LANES), 0)
    column = lane % B
    has_before = (column > 0) & (lane < USED)
    has_after = (column < B - 1) & (lane < USED)
    not_first = lane >= B
    not_last = lane < USED - B
    has_above = sublane > 0
    has_below = sublane < SUB - 1

    def operator(t, before, here, after):
        if t == 0:
            before = [jnp.where(not_first, pltpu.roll(v, B, axis=1), 0.0) for v in before]
        if t == TILES - 1:
            after = [jnp.where(not_last, pltpu.roll(v, LANES - B, axis=1), 0.0) for v in after]
        result = []
        for p in range(PLANES):
            if p == 0:
                above = jnp.where(has_above, pltpu.roll(here[PLANES - 1], 1, axis=0), 0.0)
            else:
                above = here[p - 1]
            if p == PLANES - 1:
                below = jnp.where(has_below, pltpu.roll(here[0], SUB - 1, axis=0), 0.0)
            else:
                below = here[p + 1]
            prior = jnp.where(has_before, pltpu.roll(here[p], 1, axis=1), 0.0)
            following = jnp.where(has_after, pltpu.roll(here[p], LANES - 1, axis=1), 0.0)
            around = (above + below) + (before[p] + after[p]) + (prior + following)
            value = (6.0 + SCREEN) * here[p] - around
            if t == B - TILES * (GROUPS - 1):
                value = jnp.where(not_last, value, 0.0)
            result.append(value)
        return result

    return operator


def side_by_side(used, body):
    def pair(i, carry):
        for _ in zip(body(2 * i, 0), body(2 * i + 1, 1)):
            pass
        return carry

    lax.fori_loop(0, lax.div(used, 2), pair, 0)

    @pl.when(lax.rem(used, 2) == 1)
    def _():
        for _ in body(used - 1, 0):
            pass


def solve(used, directions, residuals, image, partial, norms, steps, ratios):
    operator = make_operator()

    def totals():
        rows = jnp.sum(partial[...], axis=1)
        return jnp.broadcast_to(jnp.sum(rows, axis=1, keepdims=True), rows.shape)

    norms[...] = totals()
    for k in range(ITERS):
        last = k == ITERS - 1

        residual = residuals[(k - 1) % 2]

        def stencil(m, side, k=k, last=last, residual=residual):
            if k > 0:
                ratio = jnp.broadcast_to(ratios[pl.ds(m, 1), :], (SUB, LANES))

            def fetch(t, keep):
                values = []
                for p in range(PLANES):
                    if k == 0:
                        value = directions[0][m, cell(t, p), :]
                    else:
                        value = residual[m, cell(t, p), :]
                        value = value + ratio * directions[k - 1][m, cell(t, p), :]
                        if keep:
                            directions[k][m, cell(t, p), :] = value
                    values.append(value)
                return values

            before, here = fetch(TILES - 1, False), fetch(0, True)
            total = None
            for t in range(TILES):
                after = fetch((t + 1) % TILES, t < TILES - 1)
                applied = operator(t, before, here, after)
                if not last:
                    for p in range(PLANES):
                        image[m, cell(t, p), :] = applied[p]
                part = tree_sum([x * y for x, y in zip(here, applied)])
                total = part if total is None else total + part
                before, here = here, after
                yield
            partial[m] = total
            yield

        side_by_side(used, stencil)
        steps[k] = norms[...] / totals()
        if last:
            break
        source = directions[0] if k == 0 else residual
        target = residuals[k % 2]

        def reduce(m, side, k=k, source=source, target=target):
            step = jnp.broadcast_to(steps[k, pl.ds(m, 1), :], (SUB, LANES))
            total = None
            for t in range(TILES):
                squares = []
                for p in range(PLANES):
                    value = source[m, cell(t, p), :] - step * image[m, cell(t, p), :]
                    target[m, cell(t, p), :] = value
                    squares.append(value * value)
                part = tree_sum(squares)
                total = part if total is None else total + part
                yield
            partial[m] = total
            yield

        side_by_side(used, reduce)
        new = totals()
        ratios[...] = new / norms[...]
        norms[...] = new


def run_slots(used, forward, near, far, arrived, shift_of, held, sinks, scratch):
    pads, shifted, partial, norms, steps, ratios, odd, even, image, *directions = scratch

    def left_at(m, t):
        return blocks(held[2 * m, t].astype(jnp.float32))

    def load(m, side):
        arrived(m)
        pad = pads.at[side]
        for t in range(TILES):
            for p, block in enumerate(blocks(held[2 * m + 1, t].astype(jnp.float32))):
                put_padded(pad, t, p, block)
            yield
        total = None
        for t, moved in displaced(pad, shift_of(m)):
            squares = []
            for p, left in enumerate(left_at(m, t)):
                shifted[m, cell(t, p), :] = moved[p]
                density = moved[p] * left
                directions[0][m, cell(t, p), :] = density
                squares.append(density * density)
            part = tree_sum(squares)
            total = part if total is None else total + part
            yield
        partial[m] = total
        yield

    side_by_side(used, load)
    solve(used, directions, (odd, even), image, partial, norms, steps, ratios)

    def unload(near_to, far_to):
        def one(m, carry):
            pad = pads.at[0]
            weights = [
                jnp.broadcast_to(steps[k, pl.ds(m, 1), :], (SUB, LANES)) for k in range(ITERS)
            ]
            put_near = near_to(m) if near_to else None
            put_far = far_to(m) if far_to else None
            for t in range(TILES):
                solved = [
                    tree_sum([w * d[m, cell(t, p), :] for w, d in zip(weights, directions)])
                    for p in range(PLANES)
                ]
                if near_to:
                    terms = [v * shifted[m, cell(t, p), :] for p, v in enumerate(solved)]
                    put_near(t, jnp.concatenate(terms, axis=0))
                if far_to:
                    for p, left in enumerate(left_at(m, t)):
                        put_padded(pad, t, p, solved[p] * left)
            if far_to:
                for t, moved in displaced(pad, [-s for s in shift_of(m)]):
                    put_far(t, jnp.concatenate(moved, axis=0))
            return carry

        return one

    if forward is not None:
        lax.fori_loop(*forward, unload(sinks["forward_near"], sinks["forward_far"]), 0)
    lax.fori_loop(*near, unload(sinks["near"], None), 0)
    lax.fori_loop(*far, unload(None, sinks["far"]), 0)


def slot_scratch(batch):
    row = pltpu.VMEM((batch, LANES), jnp.float32)
    box = pltpu.VMEM((batch, CELLS * SUB, LANES), jnp.float32)
    return [
        pltpu.SMEM((batch * FIELDS,), jnp.int32),
        pltpu.VMEM((2, CELLS * CELL + SUB, LANES), jnp.float32),
        box,
        pltpu.VMEM((batch, SUB, LANES), jnp.float32),
        row,
        pltpu.VMEM((ITERS, batch, LANES), jnp.float32),
        row,
    ] + [box] * (3 + ITERS)


def clear(ref):
    for n in range(ref.shape[0]):
        for t in range(TILES):
            ref[n, t] = jnp.zeros((B, LANES), ref.dtype)


def fetch(pieces, index, target, sem):
    part = pieces[0].shape[0]
    for h, piece in enumerate(pieces):

        @pl.when(lax.div(index, part) == h)
        def _(h=h, piece=piece):
            pltpu.make_async_copy(piece.at[index - h * part], target, sem).start()


def read_tables(meta, sources, orbs, me, count, index_ref):
    free = LANES - USED
    lines = orbs // free
    row = lax.broadcasted_iota(jnp.int32, (B, LANES), 0)
    lane = lanes_of((B, LANES)) - USED

    def digits(value, length):
        value = value.astype(jnp.int32)
        for _ in range(length):
            rest = lax.div(value, count)
            yield value - rest * count
            value = rest

    weight = jnp.zeros((B, LANES), jnp.float32)
    for place, kind in enumerate((0, 2, 3)):
        chosen = (row == kind * lines + lax.div(me, free)) & (lane == lax.rem(me, free))
        weight = jnp.where(chosen, float(count**place), weight)
    for i, k in enumerate(sources):
        total = jnp.sum(meta[i].astype(jnp.float32) * weight)
        for kind, value in enumerate(digits(total, 3)):
            index_ref[kind * orbs + k] = value
    if meta.shape[0] > len(sources):
        weight = jnp.zeros((B, LANES), jnp.float32)
        for place in range(free):
            weight = jnp.where(lane == place, float(count**place), weight)
        arrived = meta[len(sources)].astype(jnp.float32) * weight
        for line in range(lines):
            total = jnp.sum(jnp.where(row == lines + line, arrived, 0.0))
            for place, value in enumerate(digits(total, free)):
                index_ref[3 * orbs + line * free + place] = value


def pairs_body(forward, limit, grid_cells, *refs):
    orbs = refs[1].shape[2]
    count = refs[3].shape[0] * 2 if forward else refs[5].shape[0]
    refs = list(refs)

    def take(number):
        taken = refs[:number]
        del refs[:number]
        return taken

    offset_ref, send_ref, left_ref = take(3)
    index_ref, done = (None, None) if forward else take(2)
    if forward:
        pieces = [take(2) for k in range(orbs)]
        incoming = take(2)
        field, index_ref, done, near_ref, far_ref = take(5)
        meta, far_sum, meta_sem = take(3)
    else:
        field_in = take(1)[0]
        pieces = [take(2) for k in range(orbs)]
        field, field_sem = take(2)
    listed, held, sem, flags, used = take(5)
    scratch = refs
    batch = held.shape[0] // 2
    space, me = lax.axis_index("space"), lax.axis_index("orb")
    spaces = lax.axis_size("space")
    group_first = space * (orbs * count)
    after = jnp.where(space == spaces - 1, 0, space + 1)
    next_first = (after * orbs + me) * count
    mine = group_first + me * count

    if forward:
        copies = [
            pltpu.make_async_copy(source[0].at[0, 0], meta.at[k], meta_sem.at[k])
            for k, source in enumerate(pieces + [incoming])
        ]
    else:
        copies = [pltpu.make_async_copy(field_in, field, field_sem.at[0])]
    for copy in copies:
        copy.start()
    scratch[0][...] = jnp.zeros(scratch[0].shape, jnp.float32)
    if forward:
        clear(field)
        clear(far_sum)
    for i in range(3 * orbs):
        flags[i] = 0 if forward else done[i]
    if forward:
        for copy in copies:
            copy.wait()
        read_tables(meta, range(orbs), orbs, me, count, index_ref)

    def consider(kind, k, room):
        @pl.when((flags[kind * orbs + k] == 0) & (used[0] < room))
        def _():
            slot = jnp.bitwise_xor(me, k)
            theirs = group_first + slot * count
            if kind == 0:
                sources = pieces[k], incoming
                rows = index_ref[2 * orbs + k], index_ref[3 * orbs + slot]
                first = theirs, next_first
            elif kind == 1:
                sources = pieces[0], pieces[k]
                rows = left_ref[0, 0, slot], index_ref[k]
                first = mine, theirs
            else:
                sources = pieces[k], pieces[0]
                rows = index_ref[orbs + k], send_ref[0, 0, slot]
                first = theirs, mine
            shift, live = geometry(offset_ref, first[0] + rows[0], first[1] + rows[1], grid_cells)
            flags[kind * orbs + k] = 1

            @pl.when(live == 1)
            def _():
                place = used[0]
                near_row = slot if kind == 0 else rows[0]
                for i, value in enumerate([*shift, near_row, rows[1]]):
                    listed[place * FIELDS + i] = value
                for side in range(2):
                    target = 2 * place + side
                    fetch(sources[side], rows[side], held.at[target], sem.at[target])
                used[0] = place + 1

            if kind == 0:

                @pl.when(live == 0)
                def _():
                    for t in range(TILES):
                        near_ref[slot, t] = jnp.zeros((B, LANES), near_ref.dtype)

    def arrived(m):
        for side in range(2):
            pltpu.make_async_copy(
                pieces[0][0].at[0], held.at[2 * m + side], sem.at[2 * m + side]
            ).wait()

    def shift_of(m):
        return [listed[m * FIELDS + axis] for axis in range(3)]

    def adding(ref, place):
        def sink(m):
            row = listed[m * FIELDS + place]

            def put(t, value):
                ref[row, t] += value

            return put

        return sink

    def forward_near(m):
        row = listed[m * FIELDS + 3]

        def put(t, value):
            near_ref[row, t] = value.astype(near_ref.dtype)

        return put

    sinks = {"near": adding(field, 3), "far": adding(field, 4)}
    if forward:
        sinks |= {"forward_near": forward_near, "forward_far": adding(far_sum, 4)}

    def run(i, carry):
        used[0] = 0
        if forward:
            for k in range(orbs):
                consider(0, k, batch)
        forwards = used[0]
        for k in range(1, orbs):
            consider(1, k, limit)
        before = used[0]
        consider(1, 0, limit)
        nears = used[0]
        for k in range(1, orbs):
            consider(2, k, limit)
        if not forward:

            @pl.when(i == 0)
            def _():
                copies[0].wait()

        run_slots(
            used[0], (0, forwards) if forward else None, (forwards, nears), (before, used[0]),
            arrived, shift_of, held, sinks, scratch,
        )
        return carry

    needed = orbs if forward else 2 * orbs - 1
    lax.fori_loop(0, -(-needed // batch), run, 0)
    if forward:
        for i in range(3 * orbs):
            done[i] = flags[i]
        for n in range(count):
            for t in range(TILES):
                far_ref[n, t] = far_sum[n, t].astype(far_ref.dtype)


def pairs(tables, state, pieces, incoming, batch, limit, grid_cells, name):
    forward = incoming is not None
    orbs, count = len(pieces), 2 * pieces[0][0].shape[0]
    vmem, smem, left = (pl.BlockSpec(memory_space=m) for m in (pltpu.VMEM, pltpu.SMEM, pl.ANY))
    shape = (TILES, B, LANES)
    flat = [half for piece in pieces for half in piece] + (incoming or [])
    out_shape, out_specs = [jax.ShapeDtypeStruct((count,) + shape, jnp.float32)], [vmem]
    if forward:
        out_shape += [
            jax.ShapeDtypeStruct((4 * orbs,), jnp.int32),
            jax.ShapeDtypeStruct((3 * orbs,), jnp.int32),
            jax.ShapeDtypeStruct((orbs,) + shape, jnp.bfloat16),
            jax.ShapeDtypeStruct((count,) + shape, jnp.bfloat16),
        ]
        out_specs += [smem] * 2 + [vmem] * 2
        state_specs = []
        scratch = [
            pltpu.VMEM((orbs + 1, B, LANES), jnp.bfloat16),
            pltpu.VMEM((count,) + shape, jnp.float32),
            pltpu.SemaphoreType.DMA((orbs + 1,)),
        ]
    else:
        state_specs = [smem] * 2 + [left]
        scratch = [pltpu.SemaphoreType.DMA((1,))]
    scratch += [
        pltpu.SMEM((batch * FIELDS,), jnp.int32),
        pltpu.VMEM((2 * batch,) + shape, jnp.bfloat16),
        pltpu.SemaphoreType.DMA((2 * batch,)),
        pltpu.SMEM((3 * orbs,), jnp.int32),
        pltpu.SMEM((1,), jnp.int32),
    ]
    return pl.pallas_call(
        functools.partial(pairs_body, forward, limit, grid_cells),
        out_shape=out_shape,
        in_specs=[smem] * 3 + state_specs + [left] * len(flat),
        out_specs=out_specs,
        scratch_shapes=scratch + slot_scratch(batch)[1:],
        compiler_params=pltpu.CompilerParams(vmem_limit_bytes=VMEM_BYTES),
        cost_estimate=pl.CostEstimate(
            flops=limit * 8 * 10**6, bytes_accessed=limit * 10**6, transcendentals=0
        ),
        name=name,
    )(*tables, *state, *flat)


def along_space(block, distance):
    size = lax.axis_size("space")
    return lax.ppermute(block, "space", [((i - distance) % size, i) for i in range(size)])


def group_exchange(packed, orbs):
    bits = [1 << i for i in range(orbs.bit_length() - 1)]
    orders = (bits[1:] + bits[:1], bits[:0:-1] + bits[:1])
    halves = []
    for block, order in zip(packed, orders):
        known = {0: block}
        for bit in order:
            route = [(i, i ^ bit) for i in range(orbs)]
            for k in list(known):
                known[k ^ bit] = lax.ppermute(known[k], "orb", route)
        halves.append(known)
    return [[known[k] for known in halves] for k in range(orbs)]


def per_device(orbitals, box_offset, send_index, pair_left):
    orbs = lax.axis_size("orb")
    grid_cells = lax.axis_size("space") * HALF
    packed = pack(orbitals, send_index, pair_left)
    incoming = [along_space(half, -1) for half in packed]
    pieces = group_exchange(packed, orbs)
    tables = (box_offset.reshape(-1), send_index, pair_left)
    field, index, done, near, far = pairs(
        tables, (), pieces, incoming, 8, FILL, grid_cells, "forward_pairs"
    )
    near = lax.all_to_all(near, "orb", split_axis=0, concat_axis=0, tiled=True)
    far = along_space(far, 1)
    (field,) = pairs(
        tables, (index, done, field), pieces, None, 16, 16, grid_cells, "group_pairs"
    )
    return finish(field, near, far, pair_left)


def solution(mesh):
    split = P(("space", "orb"), None, None)
    return jax.shard_map(
        per_device, mesh=mesh, in_specs=(split, P(), split, split), out_specs=split,
        check_vma=False,
    )
```

```python
import functools

import jax
import jax.numpy as jnp
from jax import lax
from jax.experimental import pallas as pl
from jax.experimental.pallas import tpu as pltpu
from jax.sharding import PartitionSpec as P

B = 40
ITERS = 4
SCREEN = 0.25

GROUPS = 3
TILES = 14
LANES = 128
USED = GROUPS * B
SUB = 8
PLANES = B // SUB
CELLS = TILES * PLANES
CELL = 2 * SUB
HALF = B // 2
VMEM_BYTES = 52 * 2**20
FIELDS = 8
FILL = 4


def lanes_of(shape):
    return lax.broadcasted_iota(jnp.int32, shape, len(shape) - 1)


def overlaps():
    pieces = []
    for b in range(B):
        group = b // TILES
        for flat in range(b * B // LANES, (b * B + B - 1) // LANES + 1):
            pieces.append((b, flat, b * B - flat * LANES - group * B))
    return pieces


def flat_width(flat):
    return min(LANES, B * B - flat * LANES)


def pack_body(late, box_ref, table_ref, known_ref, first_ref, second_ref, *refs):
    direct_refs, stage = refs[:-1], refs[-1]
    count = box_ref.shape[0]
    part = count // 2
    orbs = known_ref.shape[0] // 4
    me = lax.axis_index("orb")
    lane = lanes_of((B, LANES))
    for n in range(count):
        tiles = [jnp.zeros((B, LANES), jnp.float32) for _ in range(TILES)]
        loaded = {}
        for b, flat, shift in overlaps():
            if flat not in loaded:
                width = flat_width(flat)
                part_of = box_ref[n, :, flat * LANES : flat * LANES + width].astype(jnp.float32)
                if width < LANES:
                    part_of = jnp.concatenate(
                        [part_of, jnp.zeros((B, LANES - width), jnp.float32)], axis=1
                    )
                stage[flat] = part_of
                loaded[flat] = jnp.concatenate(
                    [stage[flat, pl.ds(p, SUB, stride=PLANES), :] for p in range(PLANES)], axis=0
                )
            first = max(b * B, flat * LANES) - b * B + (b // TILES) * B
            last = min(b * B + B, flat * LANES + LANES) - b * B + (b // TILES) * B
            moved = pltpu.roll(loaded[flat], (-shift) % LANES, axis=1)
            keep = (lane >= first) & (lane < last)
            tiles[b % TILES] = jnp.where(keep, moved, tiles[b % TILES])
        out_ref = first_ref if n < part else second_ref
        for t in range(TILES):
            value = tiles[t] + table_ref[...] if n == 0 and t == 0 else tiles[t]
            out_ref[n % part, t] = value.astype(out_ref.dtype)
        for k, direct_ref in zip(late, direct_refs):

            @pl.when(known_ref[3 * orbs + jnp.bitwise_xor(me, k)] == n)
            def _(n=n, tiles=tiles, direct_ref=direct_ref):
                for t in range(TILES):
                    value = jnp.where(lane == USED, float(n), tiles[t]) if t == 0 else tiles[t]
                    direct_ref[0, t] = value.astype(direct_ref.dtype)


def pack(orbitals, table, known, late):
    count = orbitals.shape[0]
    vmem, shape = pl.BlockSpec(memory_space=pltpu.VMEM), (TILES, B, LANES)
    sizes = [count // 2] * 2 + [1] * len(late)
    return pl.pallas_call(
        functools.partial(pack_body, late),
        out_shape=[jax.ShapeDtypeStruct((size,) + shape, jnp.bfloat16) for size in sizes],
        in_specs=[vmem, vmem, pl.BlockSpec(memory_space=pltpu.SMEM)],
        out_specs=[vmem] * len(sizes),
        scratch_shapes=[pltpu.VMEM((-(-B * B // LANES), B, LANES), jnp.float32)],
        compiler_params=pltpu.CompilerParams(vmem_limit_bytes=VMEM_BYTES),
        name="pack",
    )(orbitals, table, known)


def finish_body(count, slots, field_ref, near_ref, far_ref, row_ref, out_ref, total, stage):
    lane = lanes_of((B, LANES))
    for n in range(count):
        for t in range(TILES):
            total[n, t] = field_ref[n, t] + far_ref[n, t].astype(jnp.float32)

    def add(j, carry):
        row = row_ref[j]
        for t in range(TILES):
            total[row, t] += near_ref[j, t].astype(jnp.float32)
        return carry

    lax.fori_loop(0, slots, add, 0)
    for n in range(count):
        flats = {}
        for b, flat, shift in overlaps():
            first = max(b * B, flat * LANES) - flat * LANES
            last = min(b * B + B, flat * LANES + LANES) - flat * LANES
            moved = pltpu.roll(total[n, b % TILES], shift % LANES, axis=1)
            keep = (lane >= first) & (lane < last)
            before = flats.get(flat)
            flats[flat] = moved if before is None else jnp.where(keep, moved, before)
        for flat, value in flats.items():
            for p in range(PLANES):
                stage[flat, pl.ds(p, SUB, stride=PLANES), :] = value[p * SUB : p * SUB + SUB]
            width = min(LANES, B * B - flat * LANES)
            out_ref[n, :, flat * LANES : flat * LANES + width] = stage[flat, :, :width]


def finish(field, near, far, rows):
    count, slots = field.shape[0], near.shape[0]
    vmem = pl.BlockSpec(memory_space=pltpu.VMEM)
    return pl.pallas_call(
        functools.partial(finish_body, count, slots),
        out_shape=jax.ShapeDtypeStruct((count, B, B * B), jnp.float32),
        in_specs=[vmem, vmem, vmem, pl.BlockSpec(memory_space=pltpu.SMEM)],
        out_specs=vmem,
        scratch_shapes=[
            pltpu.VMEM((count, TILES, B, LANES), jnp.float32),
            pltpu.VMEM((-(-B * B // LANES), B, LANES), jnp.float32),
        ],
        compiler_params=pltpu.CompilerParams(vmem_limit_bytes=VMEM_BYTES),
        name="finish",
    )(field, near, far, rows)


def geometry(offset_ref, left, right, grid_cells):
    shift, live = [], jnp.int32(1)
    for axis in range(3):
        gap = offset_ref[3 * right + axis] - offset_ref[3 * left + axis] + grid_cells // 2
        gap = jnp.where(gap < 0, gap + grid_cells, gap)
        gap = jnp.where(gap >= grid_cells, gap - grid_cells, gap) - grid_cells // 2
        live = jnp.where((gap > HALF) | (gap < -HALF), 0, live)
        shift.append(gap)
    return shift, live


def wrapped(shift, size):
    start = lax.rem(B * size - shift, size)
    turn = lax.div(B * size - shift, size) - B
    pairs = []
    for i in range(size):
        over = jnp.where(start + i >= size, 1, 0)
        pairs.append((start + i - size * over, turn + over))
    return pairs


def put_padded(pad, t, p, value):
    start = (t * PLANES + p) * CELL + SUB
    pad[start : start + SUB, :] = value


def displaced(pad, shift):
    lane = lanes_of((SUB, LANES))
    group = lane // B
    source_col = lane - group * B - shift[2]
    col_ok = (source_col >= 0) & (source_col < B) & (lane < USED)
    source_row = jnp.where(col_ok, TILES * group - shift[1], -2 * B)
    rows = [p * CELL + SUB + turn for p, turn in wrapped(shift[0], PLANES)]
    for t, (source, turn) in enumerate(wrapped(shift[1], TILES)):
        keep = (source_row + t >= 0) & (source_row + t < B)
        if t >= B - TILES * (GROUPS - 1):
            keep = keep & (lane < USED - B)
        amount = (shift[2] - B * turn + 2 * LANES) & (LANES - 1)
        tile = []
        for p in range(PLANES):
            block = pad[pl.ds(source * (PLANES * CELL) + rows[p], SUB), :]
            tile.append(jnp.where(keep, pltpu.roll(block, amount, axis=1), 0.0))
        yield t, tile


def tree_sum(values):
    while len(values) > 1:
        paired = [a + b for a, b in zip(values[::2], values[1::2])]
        values = paired + ([values[-1]] if len(values) % 2 else [])
    return values[0]


def blocks(value):
    return [value[p * SUB : p * SUB + SUB] for p in range(PLANES)]


def cell(t, p):
    start = (t * PLANES + p) * SUB
    return slice(start, start + SUB)


def make_operator():
    lane = lanes_of((SUB, LANES))
    sublane = lax.broadcasted_iota(jnp.int32, (SUB, LANES), 0)
    column = lane % B
    has_before = (column > 0) & (lane < USED)
    has_after = (column < B - 1) & (lane < USED)
    not_first = lane >= B
    not_last = lane < USED - B
    has_above = sublane > 0
    has_below = sublane < SUB - 1

    def operator(t, before, here, after):
        if t == 0:
            before = [jnp.where(not_first, pltpu.roll(v, B, axis=1), 0.0) for v in before]
        if t == TILES - 1:
            after = [jnp.where(not_last, pltpu.roll(v, LANES - B, axis=1), 0.0) for v in after]
        result = []
        for p in range(PLANES):
            if p == 0:
                above = jnp.where(has_above, pltpu.roll(here[PLANES - 1], 1, axis=0), 0.0)
            else:
                above = here[p - 1]
            if p == PLANES - 1:
                below = jnp.where(has_below, pltpu.roll(here[0], SUB - 1, axis=0), 0.0)
            else:
                below = here[p + 1]
            prior = jnp.where(has_before, pltpu.roll(here[p], 1, axis=1), 0.0)
            following = jnp.where(has_after, pltpu.roll(here[p], LANES - 1, axis=1), 0.0)
            around = (above + below) + (before[p] + after[p]) + (prior + following)
            value = (6.0 + SCREEN) * here[p] - around
            if t == B - TILES * (GROUPS - 1):
                value = jnp.where(not_last, value, 0.0)
            result.append(value)
        return result

    return operator


def side_by_side(used, body):
    def pair(i, carry):
        for _ in zip(body(2 * i, 0), body(2 * i + 1, 1)):
            pass
        return carry

    lax.fori_loop(0, lax.div(used, 2), pair, 0)

    @pl.when(lax.rem(used, 2) == 1)
    def _():
        for _ in body(used - 1, 0):
            pass


def solve(used, directions, residuals, image, partial, norms, steps, ratios):
    operator = make_operator()

    def totals():
        rows = jnp.sum(partial[...], axis=1)
        return jnp.broadcast_to(jnp.sum(rows, axis=1, keepdims=True), rows.shape)

    norms[...] = totals()
    for k in range(ITERS):
        last = k == ITERS - 1

        residual = residuals[(k - 1) % 2]

        def stencil(m, side, k=k, last=last, residual=residual):
            if k > 0:
                ratio = jnp.broadcast_to(ratios[pl.ds(m, 1), :], (SUB, LANES))

            def fetch(t, keep):
                values = []
                for p in range(PLANES):
                    if k == 0:
                        value = directions[0][m, cell(t, p), :]
                    else:
                        value = residual[m, cell(t, p), :]
                        value = value + ratio * directions[k - 1][m, cell(t, p), :]
                        if keep:
                            directions[k][m, cell(t, p), :] = value
                    values.append(value)
                return values

            before, here = fetch(TILES - 1, False), fetch(0, True)
            total = None
            for t in range(TILES):
                after = fetch((t + 1) % TILES, t < TILES - 1)
                applied = operator(t, before, here, after)
                if not last:
                    for p in range(PLANES):
                        image[m, cell(t, p), :] = applied[p]
                part = tree_sum([x * y for x, y in zip(here, applied)])
                total = part if total is None else total + part
                before, here = here, after
                yield
            partial[m] = total
            yield

        side_by_side(used, stencil)
        steps[k] = norms[...] / totals()
        if last:
            break
        source = directions[0] if k == 0 else residual
        target = residuals[k % 2]

        def reduce(m, side, k=k, source=source, target=target):
            step = jnp.broadcast_to(steps[k, pl.ds(m, 1), :], (SUB, LANES))
            total = None
            for t in range(TILES):
                squares = []
                for p in range(PLANES):
                    value = source[m, cell(t, p), :] - step * image[m, cell(t, p), :]
                    target[m, cell(t, p), :] = value
                    squares.append(value * value)
                part = tree_sum(squares)
                total = part if total is None else total + part
                yield
            partial[m] = total
            yield

        side_by_side(used, reduce)
        new = totals()
        ratios[...] = new / norms[...]
        norms[...] = new


def run_slots(used, forward, near, far, arrived, shift_of, held, sinks, scratch):
    pads, shifted, partial, norms, steps, ratios, odd, even, image, *directions = scratch

    def left_at(m, t):
        return blocks(held[2 * m, t].astype(jnp.float32))

    def load(m, side):
        arrived(m)
        pad = pads.at[side]
        for t in range(TILES):
            for p, block in enumerate(blocks(held[2 * m + 1, t].astype(jnp.float32))):
                put_padded(pad, t, p, block)
            yield
        total = None
        for t, moved in displaced(pad, shift_of(m)):
            squares = []
            for p, left in enumerate(left_at(m, t)):
                shifted[m, cell(t, p), :] = moved[p]
                density = moved[p] * left
                directions[0][m, cell(t, p), :] = density
                squares.append(density * density)
            part = tree_sum(squares)
            total = part if total is None else total + part
            yield
        partial[m] = total
        yield

    side_by_side(used, load)
    solve(used, directions, (odd, even), image, partial, norms, steps, ratios)

    def unload(near_to, far_to):
        def one(m, carry):
            pad = pads.at[0]
            weights = [
                jnp.broadcast_to(steps[k, pl.ds(m, 1), :], (SUB, LANES)) for k in range(ITERS)
            ]
            put_near = near_to(m) if near_to else None
            put_far = far_to(m) if far_to else None
            for t in range(TILES):
                solved = [
                    tree_sum([w * d[m, cell(t, p), :] for w, d in zip(weights, directions)])
                    for p in range(PLANES)
                ]
                if near_to:
                    terms = [v * shifted[m, cell(t, p), :] for p, v in enumerate(solved)]
                    put_near(t, jnp.concatenate(terms, axis=0))
                if far_to:
                    for p, left in enumerate(left_at(m, t)):
                        put_padded(pad, t, p, solved[p] * left)
            if far_to:
                for t, moved in displaced(pad, [-s for s in shift_of(m)]):
                    put_far(t, jnp.concatenate(moved, axis=0))
            return carry

        return one

    if forward is not None:
        lax.fori_loop(*forward, unload(sinks["forward_near"], sinks["forward_far"]), 0)
    lax.fori_loop(*near, unload(sinks["near"], None), 0)
    lax.fori_loop(*far, unload(None, sinks["far"]), 0)


def slot_scratch(batch):
    row = pltpu.VMEM((batch, LANES), jnp.float32)
    box = pltpu.VMEM((batch, CELLS * SUB, LANES), jnp.float32)
    return [
        pltpu.SMEM((batch * FIELDS,), jnp.int32),
        pltpu.VMEM((2, CELLS * CELL + SUB, LANES), jnp.float32),
        box,
        pltpu.VMEM((batch, SUB, LANES), jnp.float32),
        row,
        pltpu.VMEM((ITERS, batch, LANES), jnp.float32),
        row,
    ] + [box] * (3 + ITERS)


def clear(ref):
    for n in range(ref.shape[0]):
        for t in range(TILES):
            ref[n, t] = jnp.zeros((B, LANES), ref.dtype)


def fetch(pieces, index, target, sem):
    part = pieces[0].shape[0]
    if len(pieces) == 1:
        pltpu.make_async_copy(pieces[0].at[0], target, sem).start()
        return
    for h, piece in enumerate(pieces):

        @pl.when(lax.div(index, part) == h)
        def _(h=h, piece=piece):
            pltpu.make_async_copy(piece.at[index - h * part], target, sem).start()


def read_tables(meta, sources, orbs, me, count, index_ref):
    free = LANES - USED
    lines = orbs // free
    row = lax.broadcasted_iota(jnp.int32, (B, LANES), 0)
    lane = lanes_of((B, LANES)) - USED

    def digits(value, length):
        for _ in range(length):
            rest = lax.div(value, count)
            yield value - rest * count
            value = rest

    weight = jnp.zeros((B, LANES), jnp.float32)
    for place, kind in enumerate((0, 2, 3)):
        chosen = (row == kind * lines + lax.div(me, free)) & (lane == lax.rem(me, free))
        weight = jnp.where(chosen, float(count**place), weight)
    powers = jnp.zeros((B, LANES), jnp.float32)
    for place in range(free):
        powers = jnp.where(lane == place, float(count**place), powers)
    totals = []
    for i, source in enumerate(sources):
        table = meta[i].astype(jnp.float32)
        if source is None:
            parts = [jnp.where(row == lines + line, powers, 0.0) for line in range(lines)]
        elif isinstance(source, tuple):
            parts = [jnp.where((row == 0) & (lane == 0), 1.0, 0.0)]
        else:
            parts = [weight]
        totals.append([jnp.sum(table * part).astype(jnp.int32) for part in parts])
    for source, values in zip(sources, totals):
        if source is None:
            for line, value in enumerate(values):
                for place, digit in enumerate(digits(value, free)):
                    index_ref[3 * orbs + line * free + place] = digit
        elif isinstance(source, tuple):
            index_ref[2 * orbs + source[0]] = values[0]
        else:
            for kind, digit in enumerate(digits(values[0], 3)):
                index_ref[kind * orbs + source] = digit


def pairs_body(forward, late, limit, grid_cells, *refs):
    refs = list(refs)

    def take(number):
        taken = refs[:number]
        del refs[:number]
        return taken

    offset_ref, known_ref = take(2)
    orbs = known_ref.shape[0] // 4
    inner = [k for k in range(orbs) if not forward or k not in late]
    if forward:
        pieces = {k: take(2) for k in inner}
        direct = {k: take(1) for k in late}
        incoming = take(2)
        field, index_ref, done, near_ref, far_ref = take(5)
        meta, far_sum, meta_sem = take(3)
        sources = inner + [(k, None) for k in late] + [None]
        tables = [pieces[k] for k in inner] + [direct[k] for k in late] + [incoming]
    else:
        index_in, done, field_in = take(3)
        pieces = {k: take(2) for k in inner}
        field, meta, index_ref, field_sem, meta_sem = take(5)
        sources, tables = late, [pieces[k] for k in late]
    count = 2 * pieces[0][0].shape[0]
    listed, held, sem, flags, used = take(5)
    scratch = refs
    batch = held.shape[0] // 2
    space, me = lax.axis_index("space"), lax.axis_index("orb")
    spaces = lax.axis_size("space")
    group_first = space * (orbs * count)
    after = jnp.where(space == spaces - 1, 0, space + 1)
    next_first = (after * orbs + me) * count
    mine = group_first + me * count

    copies = [
        pltpu.make_async_copy(source[0].at[0, 0], meta.at[i], meta_sem.at[i])
        for i, source in enumerate(tables)
    ]
    for copy in copies:
        copy.start()
    if not forward:
        load_field = pltpu.make_async_copy(field_in, field, field_sem.at[0])
        load_field.start()
    scratch[0][...] = jnp.zeros(scratch[0].shape, jnp.float32)
    if forward:
        clear(field)
        clear(far_sum)
    for i in range(3 * orbs):
        flags[i] = 0 if forward else done[i]
    if not forward:
        for i in range(2 * orbs):
            index_ref[i] = index_in[i]
    for copy in copies:
        copy.wait()
    read_tables(meta, sources, orbs, me, count, index_ref)

    def consider(kind, k, room):
        @pl.when((flags[kind * orbs + k] == 0) & (used[0] < room))
        def _():
            slot = jnp.bitwise_xor(me, k)
            theirs = group_first + slot * count
            if kind == 0:
                sources = direct[k] if k in late else pieces[k], incoming
                rows = index_ref[2 * orbs + k], index_ref[3 * orbs + slot]
                first = theirs, next_first
            elif kind == 1:
                sources = pieces[0], pieces[k]
                rows = known_ref[2 * orbs + slot], index_ref[k]
                first = mine, theirs
            else:
                sources = pieces[k], pieces[0]
                rows = index_ref[orbs + k], known_ref[slot]
                first = theirs, mine
            shift, live = geometry(offset_ref, first[0] + rows[0], first[1] + rows[1], grid_cells)
            flags[kind * orbs + k] = 1

            @pl.when(live == 1)
            def _():
                place = used[0]
                near_row = slot if kind == 0 else rows[0]
                for i, value in enumerate([*shift, near_row, rows[1]]):
                    listed[place * FIELDS + i] = value
                for side in range(2):
                    target = 2 * place + side
                    fetch(sources[side], rows[side], held.at[target], sem.at[target])
                used[0] = place + 1

            if kind == 0:

                @pl.when(live == 0)
                def _():
                    for t in range(TILES):
                        near_ref[slot, t] = jnp.zeros((B, LANES), near_ref.dtype)

    def arrived(m):
        for side in range(2):
            pltpu.make_async_copy(
                pieces[0][0].at[0], held.at[2 * m + side], sem.at[2 * m + side]
            ).wait()

    def shift_of(m):
        return [listed[m * FIELDS + axis] for axis in range(3)]

    def adding(ref, place):
        def sink(m):
            row = listed[m * FIELDS + place]

            def put(t, value):
                ref[row, t] += value

            return put

        return sink

    def forward_near(m):
        row = listed[m * FIELDS + 3]

        def put(t, value):
            near_ref[row, t] = value.astype(near_ref.dtype)

        return put

    sinks = {"near": adding(field, 3), "far": adding(field, 4)}
    if forward:
        sinks |= {"forward_near": forward_near, "forward_far": adding(far_sum, 4)}

    def run(i, carry):
        used[0] = 0
        if forward:
            for k in range(orbs):
                consider(0, k, batch)
        forwards = used[0]
        for k in inner[1:]:
            consider(1, k, limit)
        before = used[0]
        consider(1, 0, limit)
        nears = used[0]
        for k in inner[1:]:
            consider(2, k, limit)
        if not forward:

            @pl.when(i == 0)
            def _():
                load_field.wait()

        run_slots(
            used[0], (0, forwards) if forward else None, (forwards, nears), (before, used[0]),
            arrived, shift_of, held, sinks, scratch,
        )
        return carry

    needed = orbs if forward else 2 * orbs - 1
    lax.fori_loop(0, -(-needed // batch), run, 0)
    if forward:
        for i in range(3 * orbs):
            done[i] = flags[i]
        for n in range(count):
            for t in range(TILES):
                far_ref[n, t] = far_sum[n, t].astype(far_ref.dtype)


def pairs(tables, state, pieces, direct, incoming, late, batch, limit, grid_cells, name):
    forward = incoming is not None
    orbs, count = tables[1].shape[0] // 4, 2 * pieces[0][0].shape[0]
    vmem, smem, left = (pl.BlockSpec(memory_space=m) for m in (pltpu.VMEM, pltpu.SMEM, pl.ANY))
    shape = (TILES, B, LANES)
    flat = [half for piece in pieces for half in piece]
    out_shape, out_specs = [jax.ShapeDtypeStruct((count,) + shape, jnp.float32)], [vmem]
    if forward:
        flat += direct + incoming
        out_shape += [
            jax.ShapeDtypeStruct((4 * orbs,), jnp.int32),
            jax.ShapeDtypeStruct((3 * orbs,), jnp.int32),
            jax.ShapeDtypeStruct((orbs,) + shape, jnp.bfloat16),
            jax.ShapeDtypeStruct((count,) + shape, jnp.bfloat16),
        ]
        out_specs += [smem] * 2 + [vmem] * 2
        state_specs = []
        scratch = [
            pltpu.VMEM((orbs + 1, B, LANES), jnp.bfloat16),
            pltpu.VMEM((count,) + shape, jnp.float32),
            pltpu.SemaphoreType.DMA((orbs + 1,)),
        ]
    else:
        state_specs = [smem] * 2 + [left]
        scratch = [
            pltpu.VMEM((len(late), B, LANES), jnp.bfloat16),
            pltpu.SMEM((3 * orbs,), jnp.int32),
            pltpu.SemaphoreType.DMA((1,)),
            pltpu.SemaphoreType.DMA((len(late),)),
        ]
    scratch += [
        pltpu.SMEM((batch * FIELDS,), jnp.int32),
        pltpu.VMEM((2 * batch,) + shape, jnp.bfloat16),
        pltpu.SemaphoreType.DMA((2 * batch,)),
        pltpu.SMEM((3 * orbs,), jnp.int32),
        pltpu.SMEM((1,), jnp.int32),
    ]
    return pl.pallas_call(
        functools.partial(pairs_body, forward, late, limit, grid_cells),
        out_shape=out_shape,
        in_specs=[smem] * 2 + state_specs + [left] * len(flat),
        out_specs=out_specs,
        scratch_shapes=scratch + slot_scratch(batch)[1:],
        compiler_params=pltpu.CompilerParams(vmem_limit_bytes=VMEM_BYTES),
        cost_estimate=pl.CostEstimate(
            flops=limit * 8 * 10**6, bytes_accessed=limit * 10**6, transcendentals=0
        ),
        name=name,
    )(*tables, *state, *flat)


def along_space(block, distance):
    size = lax.axis_size("space")
    return lax.ppermute(block, "space", [((i - distance) % size, i) for i in range(size)])


def across(block, orbs, offset):
    return lax.ppermute(block, "orb", [(i, i ^ offset) for i in range(orbs)])


def per_device(orbitals, box_offset, send_index, pair_left):
    orbs = lax.axis_size("orb")
    grid_cells = lax.axis_size("space") * HALF
    bits = [1 << i for i in range(orbs.bit_length() - 1)]
    far_side = bits[-1] | bits[-2]
    late = [k for k in range(orbs) if k & far_side == far_side]

    known = jnp.concatenate([send_index.reshape(-1), pair_left.reshape(-1)])
    free = LANES - USED
    lines = 4 * orbs // free
    table = known.reshape(lines, free).astype(jnp.float32)
    table = jnp.pad(table, ((0, B - lines), (USED, 0)))
    packed = pack(orbitals, table, known, late)
    halves, direct = packed[:2], packed[2:]

    one, other = bits[-2], bits[-1]
    first = [one, other]
    pieces = {}
    for h, half in enumerate(halves):
        pieces[0, h] = half
        pieces[first[h], h] = across(half, orbs, first[h])
        pieces[first[1 - h], h] = across(half, orbs, first[1 - h])
    direct = [across(block, orbs, k) for k, block in zip(late, direct)]
    incoming = [along_space(half, -1) for half in halves]
    for h in range(2):
        pieces[far_side, h] = across(pieces[first[h], h], orbs, first[1 - h])

    def spread_over_rest(sources):
        for bit in reversed(bits[:-2]):
            for k in [k for k, h in list(pieces) if h == 0 and k in sources]:
                for h in range(2):
                    pieces[k | bit, h] = across(pieces[k, h], orbs, bit)
            sources = sources + [k | bit for k in sources]

    spread_over_rest([0, one, other])
    tables = (box_offset.reshape(-1), known)
    field, index, done, near, far = pairs(
        tables, (), [[pieces[k, 0], pieces[k, 1]] for k in range(orbs) if k not in late],
        direct, incoming, late, 8, FILL, grid_cells, "forward_pairs",
    )
    if len(late) > 1:
        ready = lax.optimization_barrier((pieces[far_side, 0], pieces[far_side, 1], done))
        pieces[far_side, 0], pieces[far_side, 1], done = ready
        spread_over_rest([far_side])
    near = lax.all_to_all(near, "orb", split_axis=0, concat_axis=0, tiled=True)
    far = along_space(far, 1)
    (field,) = pairs(
        tables, (index, done, field), [[pieces[k, 0], pieces[k, 1]] for k in range(orbs)],
        None, None, late, 16, 16, grid_cells, "group_pairs",
    )
    return finish(field, near, far, pair_left[0, 1])


def solution(mesh):
    split = P(("space", "orb"), None, None)
    return jax.shard_map(
        per_device, mesh=mesh, in_specs=(split, P(), split, split), out_specs=split,
        check_vma=False,
    )
```

```python
import functools

import jax
import jax.numpy as jnp
from jax import lax
from jax.experimental import pallas as pl
from jax.experimental.pallas import tpu as pltpu
from jax.sharding import PartitionSpec as P

B = 40
ITERS = 4
SCREEN = 0.25

GROUPS = 3
TILES = 14
LANES = 128
USED = GROUPS * B
SUB = 8
PLANES = B // SUB
CELLS = TILES * PLANES
CELL = 2 * SUB
HALF = B // 2
VMEM_BYTES = 52 * 2**20
FIELDS = 8


def lanes_of(shape):
    return lax.broadcasted_iota(jnp.int32, shape, len(shape) - 1)


def overlaps():
    pieces = []
    for b in range(B):
        group = b // TILES
        for flat in range(b * B // LANES, (b * B + B - 1) // LANES + 1):
            pieces.append((b, flat, b * B - flat * LANES - group * B))
    return pieces


def pack_body(box_ref, table_ref, whole_ref, first_ref, second_ref, stage):
    count = box_ref.shape[0]
    lane = lanes_of((B, LANES))
    for n in range(count):
        tiles = [jnp.zeros((B, LANES), jnp.float32) for _ in range(TILES)]
        loaded = {}
        for b, flat, shift in overlaps():
            if flat not in loaded:
                width = min(LANES, B * B - flat * LANES)
                part = box_ref[n, :, flat * LANES : flat * LANES + width].astype(jnp.float32)
                if width < LANES:
                    part = jnp.concatenate(
                        [part, jnp.zeros((B, LANES - width), jnp.float32)], axis=1
                    )
                stage[flat] = part
                loaded[flat] = jnp.concatenate(
                    [stage[flat, pl.ds(p, SUB, stride=PLANES), :] for p in range(PLANES)], axis=0
                )
            first = max(b * B, flat * LANES) - b * B + (b // TILES) * B
            last = min(b * B + B, flat * LANES + LANES) - b * B + (b // TILES) * B
            moved = pltpu.roll(loaded[flat], (-shift) % LANES, axis=1)
            keep = (lane >= first) & (lane < last)
            tiles[b % TILES] = jnp.where(keep, moved, tiles[b % TILES])
        if n == 0:
            tiles[0] = tiles[0] + table_ref[...]
        out_ref = first_ref if n < count // 2 else second_ref
        for t in range(TILES):
            value = tiles[t].astype(out_ref.dtype)
            whole_ref[n, t] = value
            out_ref[n % (count // 2), t] = value


def pack(orbitals, table):
    count = orbitals.shape[0]
    return pl.pallas_call(
        pack_body,
        out_shape=[
            jax.ShapeDtypeStruct((size, TILES, B, LANES), jnp.bfloat16)
            for size in (count, count // 2, count // 2)
        ],
        in_specs=[pl.BlockSpec(memory_space=pltpu.VMEM)] * 2,
        out_specs=[pl.BlockSpec(memory_space=pltpu.VMEM)] * 3,
        scratch_shapes=[pltpu.VMEM((-(-B * B // LANES), B, LANES), jnp.float32)],
        compiler_params=pltpu.CompilerParams(vmem_limit_bytes=VMEM_BYTES),
        name="pack",
    )(orbitals, table)


def finish_body(count, slots, field_ref, near_ref, far_ref, row_ref, out_ref, total, stage):
    lane = lanes_of((B, LANES))
    for n in range(count):
        for t in range(TILES):
            total[n, t] = field_ref[n, t] + far_ref[n, t].astype(jnp.float32)

    def add(j, carry):
        row = row_ref[j]
        for t in range(TILES):
            total[row, t] += near_ref[j, t].astype(jnp.float32)
        return carry

    lax.fori_loop(0, slots, add, 0)
    for n in range(count):
        flats = {}
        for b, flat, shift in overlaps():
            first = max(b * B, flat * LANES) - flat * LANES
            last = min(b * B + B, flat * LANES + LANES) - flat * LANES
            moved = pltpu.roll(total[n, b % TILES], shift % LANES, axis=1)
            keep = (lane >= first) & (lane < last)
            before = flats.get(flat)
            flats[flat] = moved if before is None else jnp.where(keep, moved, before)
        for flat, value in flats.items():
            for p in range(PLANES):
                stage[flat, pl.ds(p, SUB, stride=PLANES), :] = value[p * SUB : p * SUB + SUB]
            width = min(LANES, B * B - flat * LANES)
            out_ref[n, :, flat * LANES : flat * LANES + width] = stage[flat, :, :width]


def finish(field, near, far, rows):
    count, slots = field.shape[0], near.shape[0]
    vmem = pl.BlockSpec(memory_space=pltpu.VMEM)
    return pl.pallas_call(
        functools.partial(finish_body, count, slots),
        out_shape=jax.ShapeDtypeStruct((count, B, B * B), jnp.float32),
        in_specs=[vmem, vmem, vmem, pl.BlockSpec(memory_space=pltpu.SMEM)],
        out_specs=vmem,
        scratch_shapes=[
            pltpu.VMEM((count, TILES, B, LANES), jnp.float32),
            pltpu.VMEM((-(-B * B // LANES), B, LANES), jnp.float32),
        ],
        compiler_params=pltpu.CompilerParams(vmem_limit_bytes=VMEM_BYTES),
        name="finish",
    )(field, near, far, rows)


def geometry(offset_ref, left, right, grid_cells):
    shift, live = [], jnp.int32(1)
    for axis in range(3):
        gap = offset_ref[3 * right + axis] - offset_ref[3 * left + axis] + grid_cells // 2
        gap = jnp.where(gap < 0, gap + grid_cells, gap)
        gap = jnp.where(gap >= grid_cells, gap - grid_cells, gap) - grid_cells // 2
        live = jnp.where((gap > HALF) | (gap < -HALF), 0, live)
        shift.append(gap)
    return shift, live


def wrapped(shift, size):
    start = lax.rem(B * size - shift, size)
    turn = lax.div(B * size - shift, size) - B
    pairs = []
    for i in range(size):
        over = jnp.where(start + i >= size, 1, 0)
        pairs.append((start + i - size * over, turn + over))
    return pairs


def put_padded(pad, t, p, value):
    start = (t * PLANES + p) * CELL + SUB
    pad[start : start + SUB, :] = value


def displaced(pad, shift):
    lane = lanes_of((SUB, LANES))
    group = lane // B
    source_col = lane - group * B - shift[2]
    col_ok = (source_col >= 0) & (source_col < B) & (lane < USED)
    source_row = jnp.where(col_ok, TILES * group - shift[1], -2 * B)
    rows = [p * CELL + SUB + turn for p, turn in wrapped(shift[0], PLANES)]
    for t, (source, turn) in enumerate(wrapped(shift[1], TILES)):
        keep = (source_row + t >= 0) & (source_row + t < B)
        if t >= B - TILES * (GROUPS - 1):
            keep = keep & (lane < USED - B)
        amount = (shift[2] - B * turn + 2 * LANES) & (LANES - 1)
        tile = []
        for p in range(PLANES):
            block = pad[pl.ds(source * (PLANES * CELL) + rows[p], SUB), :]
            tile.append(jnp.where(keep, pltpu.roll(block, amount, axis=1), 0.0))
        yield t, tile


def tree_sum(values):
    while len(values) > 1:
        paired = [a + b for a, b in zip(values[::2], values[1::2])]
        values = paired + ([values[-1]] if len(values) % 2 else [])
    return values[0]


def blocks(value):
    return [value[p * SUB : p * SUB + SUB] for p in range(PLANES)]


def cell(t, p):
    start = (t * PLANES + p) * SUB
    return slice(start, start + SUB)


def make_operator():
    lane = lanes_of((SUB, LANES))
    sublane = lax.broadcasted_iota(jnp.int32, (SUB, LANES), 0)
    column = lane % B
    has_before = (column > 0) & (lane < USED)
    has_after = (column < B - 1) & (lane < USED)
    not_first = lane >= B
    not_last = lane < USED - B
    has_above = sublane > 0
    has_below = sublane < SUB - 1

    def operator(t, before, here, after):
        if t == 0:
            before = [jnp.where(not_first, pltpu.roll(v, B, axis=1), 0.0) for v in before]
        if t == TILES - 1:
            after = [jnp.where(not_last, pltpu.roll(v, LANES - B, axis=1), 0.0) for v in after]
        result = []
        for p in range(PLANES):
            if p == 0:
                above = jnp.where(has_above, pltpu.roll(here[PLANES - 1], 1, axis=0), 0.0)
            else:
                above = here[p - 1]
            if p == PLANES - 1:
                below = jnp.where(has_below, pltpu.roll(here[0], SUB - 1, axis=0), 0.0)
            else:
                below = here[p + 1]
            prior = jnp.where(has_before, pltpu.roll(here[p], 1, axis=1), 0.0)
            following = jnp.where(has_after, pltpu.roll(here[p], LANES - 1, axis=1), 0.0)
            around = (above + below) + (before[p] + after[p]) + (prior + following)
            value = (6.0 + SCREEN) * here[p] - around
            if t == B - TILES * (GROUPS - 1):
                value = jnp.where(not_last, value, 0.0)
            result.append(value)
        return result

    return operator


def side_by_side(first, last, body):
    def pair(i, carry):
        for _ in zip(body(first + 2 * i, 0), body(first + 2 * i + 1, 1)):
            pass
        return carry

    lax.fori_loop(0, lax.div(last - first, 2), pair, 0)

    @pl.when(lax.rem(last - first, 2) == 1)
    def _():
        for _ in body(last - 1, 0):
            pass


def solve(used, directions, residuals, image, partial, norms, steps, ratios):
    operator = make_operator()

    def totals():
        rows = jnp.sum(partial[...], axis=1)
        return jnp.broadcast_to(jnp.sum(rows, axis=1, keepdims=True), rows.shape)

    norms[...] = totals()
    for k in range(ITERS):
        last = k == ITERS - 1

        residual = residuals[(k - 1) % 2]

        def stencil(m, side, k=k, last=last, residual=residual):
            if k > 0:
                ratio = jnp.broadcast_to(ratios[pl.ds(m, 1), :], (SUB, LANES))

            def fetch(t, keep):
                values = []
                for p in range(PLANES):
                    if k == 0:
                        value = directions[0][m, cell(t, p), :]
                    else:
                        value = residual[m, cell(t, p), :]
                        value = value + ratio * directions[k - 1][m, cell(t, p), :]
                        if keep:
                            directions[k][m, cell(t, p), :] = value
                    values.append(value)
                return values

            before, here = fetch(TILES - 1, False), fetch(0, True)
            total = None
            for t in range(TILES):
                after = fetch((t + 1) % TILES, t < TILES - 1)
                applied = operator(t, before, here, after)
                if not last:
                    for p in range(PLANES):
                        image[m, cell(t, p), :] = applied[p]
                part = tree_sum([x * y for x, y in zip(here, applied)])
                total = part if total is None else total + part
                before, here = here, after
                yield
            partial[m] = total
            yield

        side_by_side(0, used, stencil)
        steps[k] = norms[...] / totals()
        if last:
            break
        source = directions[0] if k == 0 else residual
        target = residuals[k % 2]

        def reduce(m, side, k=k, source=source, target=target):
            step = jnp.broadcast_to(steps[k, pl.ds(m, 1), :], (SUB, LANES))
            total = None
            for t in range(TILES):
                squares = []
                for p in range(PLANES):
                    value = source[m, cell(t, p), :] - step * image[m, cell(t, p), :]
                    target[m, cell(t, p), :] = value
                    squares.append(value * value)
                part = tree_sum(squares)
                total = part if total is None else total + part
                yield
            partial[m] = total
            yield

        side_by_side(0, used, reduce)
        new = totals()
        ratios[...] = new / norms[...]
        norms[...] = new


def run_slots(used, nears, fars, shift_of, left_of, right_of, near_to, far_to, held, scratch):
    pads, shifted, partial, norms, steps, ratios, odd, even, image, *directions = scratch

    def box(row, t):
        return blocks(held[row, t].astype(jnp.float32))

    def load(m, side):
        pad = pads.at[side]
        left, right = left_of(m), right_of(m)
        for t in range(TILES):
            for p, block in enumerate(box(right, t)):
                put_padded(pad, t, p, block)
            yield
        total = None
        for t, moved in displaced(pad, shift_of(m)):
            squares = []
            for p, value in enumerate(box(left, t)):
                shifted[m, cell(t, p), :] = moved[p]
                density = moved[p] * value
                directions[0][m, cell(t, p), :] = density
                squares.append(density * density)
            part = tree_sum(squares)
            total = part if total is None else total + part
            yield
        partial[m] = total
        yield

    side_by_side(0, used, load)
    solve(used, directions, (odd, even), image, partial, norms, steps, ratios)

    def unload(near, far):
        def one(m, side):
            pad = pads.at[side]
            left = left_of(m)
            weights = [
                jnp.broadcast_to(steps[k, pl.ds(m, 1), :], (SUB, LANES)) for k in range(ITERS)
            ]
            put_near = near_to(m) if near else None
            put_far = far_to(m) if far else None
            for t in range(TILES):
                solved = [
                    tree_sum([w * d[m, cell(t, p), :] for w, d in zip(weights, directions)])
                    for p in range(PLANES)
                ]
                if near:
                    terms = [v * shifted[m, cell(t, p), :] for p, v in enumerate(solved)]
                    put_near(t, jnp.concatenate(terms, axis=0))
                if far:
                    for p, value in enumerate(box(left, t)):
                        put_padded(pad, t, p, solved[p] * value)
                yield
            if far:
                for t, moved in displaced(pad, [-s for s in shift_of(m)]):
                    put_far(t, jnp.concatenate(moved, axis=0))
                    yield

        return one

    if nears is fars:
        side_by_side(*nears, unload(True, True))
    else:
        side_by_side(*nears, unload(True, False))
        side_by_side(*fars, unload(False, True))


def slot_scratch(batch):
    row = pltpu.VMEM((batch, LANES), jnp.float32)
    box = pltpu.VMEM((batch, CELLS * SUB, LANES), jnp.float32)
    return [
        pltpu.SMEM((batch * FIELDS,), jnp.int32),
        pltpu.VMEM((2, CELLS * CELL + SUB, LANES), jnp.float32),
        box,
        pltpu.VMEM((batch, SUB, LANES), jnp.float32),
        row,
        pltpu.VMEM((ITERS, batch, LANES), jnp.float32),
        row,
    ] + [box] * (3 + ITERS)


def clear(ref):
    for n in range(ref.shape[0]):
        for t in range(TILES):
            ref[n, t] = jnp.zeros((B, LANES), ref.dtype)


def append(listed, used, values):
    for i, value in enumerate(values):
        listed[used * FIELDS + i] = value


def adding(ref, row):
    def put(t, value):
        ref[row, t] += value

    return put


def piece_copies(pieces, index, held, slot, sem):
    part = pieces[0].shape[0]
    if len(pieces) == 1:
        pltpu.make_async_copy(pieces[0].at[index], held.at[slot], sem).start()
        return
    for h, piece in enumerate(pieces):

        @pl.when(lax.div(index, part) == h)
        def _(h=h, piece=piece):
            pltpu.make_async_copy(piece.at[index - h * part], held.at[slot], sem).start()


def wait_box(pieces, held, slot, sem):
    pltpu.make_async_copy(pieces[0].at[0], held.at[slot], sem).wait()


def read_tables(meta, orbs, me, count, index_ref):
    free = LANES - USED
    lines = orbs // free
    row = lax.broadcasted_iota(jnp.int32, (B, LANES), 0)
    lane = lanes_of((B, LANES)) - USED

    def digits(value, length):
        value = value.astype(jnp.int32)
        for _ in range(length):
            rest = lax.div(value, count)
            yield value - rest * count
            value = rest

    weight = jnp.zeros((B, LANES), jnp.float32)
    for place, kind in enumerate((0, 2, 3)):
        chosen = (row == kind * lines + lax.div(me, free)) & (lane == lax.rem(me, free))
        weight = jnp.where(chosen, float(count**place), weight)
    for k in range(orbs):
        source = jnp.bitwise_xor(me, k)
        total = jnp.sum(meta[k].astype(jnp.float32) * weight)
        for kind, value in enumerate(digits(total, 3)):
            index_ref[kind * orbs + source] = value
    weight = jnp.zeros((B, LANES), jnp.float32)
    for place in range(free):
        weight = jnp.where(lane == place, float(count**place), weight)
    arrived = meta[orbs].astype(jnp.float32) * weight
    for line in range(lines):
        total = jnp.sum(jnp.where(row == lines + line, arrived, 0.0))
        for place, value in enumerate(digits(total, free)):
            index_ref[3 * orbs + line * free + place] = value


def split_pieces(refs, orbs):
    refs, pieces = list(refs), []
    for k in range(orbs):
        pieces.append([refs.pop(0) for _ in range(1 if k < 2 else 2)])
    return refs, pieces


def forward_body(orbs, count, grid_cells, where_ref, offset_ref, *refs):
    refs, pieces = split_pieces(refs, orbs)
    incoming, near_ref, far_ref, index_ref = refs[:4]
    meta, held, far_sum, meta_sem, box_sem, listed, *scratch = refs[4:]
    batch = listed.shape[0] // FIELDS
    me = where_ref[2]
    first_left, first_right = where_ref[0], where_ref[1]

    tables = [
        pltpu.make_async_copy(source[0].at[0, 0], meta.at[k], meta_sem.at[k])
        for k, source in enumerate(pieces + [[incoming]])
    ]
    for copy in tables:
        copy.start()
    rights = [
        pltpu.make_async_copy(
            incoming.at[n], held.at[orbs + n], box_sem.at[orbs + n]
        )
        for n in range(count)
    ]
    for copy in rights:
        copy.start()
    scratch[0][...] = jnp.zeros(scratch[0].shape, jnp.float32)
    clear(far_sum)
    for copy in tables:
        copy.wait()
    read_tables(meta, orbs, me, count, index_ref)
    for k in range(orbs):
        source = jnp.bitwise_xor(me, k)
        piece_copies(pieces[k], index_ref[2 * orbs + source], held, source, box_sem.at[k])
    for k in range(orbs):
        wait_box(pieces[k], held, jnp.bitwise_xor(me, k), box_sem.at[k])
    for copy in rights:
        copy.wait()

    def run(i, carry):
        def gather(j, used):
            slot = i * batch + j
            left, right = slot * count + index_ref[2 * orbs + slot], index_ref[3 * orbs + slot]
            shift, live = geometry(
                offset_ref, first_left + left, first_right + right, grid_cells
            )

            @pl.when(live == 1)
            def _():
                append(listed, used, [slot, orbs + right, *shift])

            @pl.when(live == 0)
            def _():
                for t in range(TILES):
                    near_ref[slot, t] = jnp.zeros((B, LANES), near_ref.dtype)

            return used + live

        used = lax.fori_loop(0, batch, gather, jnp.int32(0))

        def shift_of(m):
            return [listed[m * FIELDS + 2 + axis] for axis in range(3)]

        def near_to(m):
            row = listed[m * FIELDS]

            def put(t, value):
                near_ref[row, t] = value.astype(near_ref.dtype)

            return put

        def far_to(m):
            return adding(far_sum, listed[m * FIELDS + 1] - orbs)

        every = (0, used)
        run_slots(
            used, every, every, shift_of,
            lambda m: listed[m * FIELDS], lambda m: listed[m * FIELDS + 1],
            near_to, far_to, held, scratch,
        )
        return carry

    lax.fori_loop(0, orbs // batch, run, 0)
    for n in range(count):
        for t in range(TILES):
            far_ref[n, t] = far_sum[n, t].astype(far_ref.dtype)


def forward_pairs(where, offsets, pieces, incoming, count, grid_cells):
    orbs, parts = len(pieces), sum(len(piece) for piece in pieces)
    vmem, smem, left = (pl.BlockSpec(memory_space=m) for m in (pltpu.VMEM, pltpu.SMEM, pl.ANY))
    shape = (TILES, B, LANES)
    return pl.pallas_call(
        functools.partial(forward_body, orbs, count, grid_cells),
        out_shape=(
            jax.ShapeDtypeStruct((orbs,) + shape, jnp.bfloat16),
            jax.ShapeDtypeStruct((count,) + shape, jnp.bfloat16),
            jax.ShapeDtypeStruct((4 * orbs,), jnp.int32),
        ),
        in_specs=[smem] * 2 + [left] * (parts + 1),
        out_specs=(vmem, vmem, smem),
        scratch_shapes=[
            pltpu.VMEM((orbs + 1, B, LANES), jnp.bfloat16),
            pltpu.VMEM((orbs + count,) + shape, jnp.bfloat16),
            pltpu.VMEM((count,) + shape, jnp.float32),
            pltpu.SemaphoreType.DMA((orbs + 1,)),
            pltpu.SemaphoreType.DMA((orbs + count,)),
        ] + slot_scratch(8),
        compiler_params=pltpu.CompilerParams(vmem_limit_bytes=VMEM_BYTES),
        name="forward_pairs",
    )(where, offsets, *[half for piece in pieces for half in piece], incoming)


def group_body(orbs, count, grid_cells, where_ref, offset_ref, mine_ref, sent_ref, index_ref, *refs):
    refs, pieces = split_pieces(refs, orbs)
    field, held, sem, listed, *scratch = refs
    half = listed.shape[0] // FIELDS // 2
    first, me = where_ref[0], where_ref[2]
    mine = me * count
    own = 2 * orbs

    for k in range(orbs):
        source = jnp.bitwise_xor(me, k)
        piece_copies(pieces[k], index_ref[source], held, source, sem.at[k])
        piece_copies(pieces[k], index_ref[orbs + source], held, orbs + source, sem.at[orbs + k])
    owned = [
        pltpu.make_async_copy(pieces[0][0].at[n], held.at[own + n], sem.at[own + n])
        for n in range(count)
    ]
    for copy in owned:
        copy.start()
    scratch[0][...] = jnp.zeros(scratch[0].shape, jnp.float32)
    clear(field)
    for k in range(orbs):
        source = jnp.bitwise_xor(me, k)
        wait_box(pieces[k], held, source, sem.at[k])
        wait_box(pieces[k], held, orbs + source, sem.at[orbs + k])
    for copy in owned:
        copy.wait()

    def run(i, carry):
        def listing(near):
            def gather(j, used):
                slot = i * half + lax.rem(me + 1 + j, half)
                if near:
                    left, right = mine + mine_ref[slot], slot * count + index_ref[slot]
                    boxes = [own + mine_ref[slot], slot]
                else:
                    left, right = slot * count + index_ref[orbs + slot], mine + sent_ref[slot]
                    boxes = [orbs + slot, own + sent_ref[slot]]
                shift, live = geometry(offset_ref, first + left, first + right, grid_cells)
                if not near:
                    live = jnp.where(slot == me, 0, live)
                else:
                    boxes[1] = jnp.where(slot == me, own + index_ref[slot], boxes[1])

                @pl.when(live == 1)
                def _():
                    append(listed, used, boxes + [*shift])

                return used + live

            return gather

        near_count = lax.fori_loop(0, half, listing(True), jnp.int32(0))
        used = lax.fori_loop(0, half, listing(False), near_count)
        left, right = mine + mine_ref[me], mine + index_ref[me]
        inside = geometry(offset_ref, first + left, first + right, grid_cells)[1]
        inside = jnp.where(lax.div(me, half) == i, inside, 0)

        def shift_of(m):
            return [listed[m * FIELDS + 2 + axis] for axis in range(3)]

        def near_to(m):
            return adding(field, listed[m * FIELDS] - own)

        def far_to(m):
            return adding(field, listed[m * FIELDS + 1] - own)

        run_slots(
            used, (0, near_count), (near_count - inside, used), shift_of,
            lambda m: listed[m * FIELDS], lambda m: listed[m * FIELDS + 1],
            near_to, far_to, held, scratch,
        )
        return carry

    lax.fori_loop(0, orbs // half, run, 0)


def group_pairs(where, offsets, mine, sent, index, pieces, count, grid_cells):
    orbs, parts = len(pieces), sum(len(piece) for piece in pieces)
    vmem, smem, left = (pl.BlockSpec(memory_space=m) for m in (pltpu.VMEM, pltpu.SMEM, pl.ANY))
    shape = (TILES, B, LANES)
    return pl.pallas_call(
        functools.partial(group_body, orbs, count, grid_cells),
        out_shape=jax.ShapeDtypeStruct((count,) + shape, jnp.float32),
        in_specs=[smem] * 5 + [left] * parts,
        out_specs=vmem,
        scratch_shapes=[
            pltpu.VMEM((2 * orbs + count,) + shape, jnp.bfloat16),
            pltpu.SemaphoreType.DMA((2 * orbs + count,)),
        ] + slot_scratch(16),
        compiler_params=pltpu.CompilerParams(vmem_limit_bytes=VMEM_BYTES),
        name="group_pairs",
    )(where, offsets, mine, sent, index, *[half for piece in pieces for half in piece])


def along_space(block, distance):
    size = lax.axis_size("space")
    return lax.ppermute(block, "space", [((i - distance) % size, i) for i in range(size)])


def across(block, orbs, offset):
    return lax.ppermute(block, "orb", [(i, i ^ offset) for i in range(orbs)])


def group_exchange(whole, halves, orbs):
    bits = [1 << i for i in range(orbs.bit_length() - 1)]
    found = []
    for half, order in zip(halves, (bits[1:], bits[:0:-1])):
        known = {0: half}
        for bit in order:
            for k in list(known):
                known[k ^ bit] = across(known[k], orbs, bit)
        for k in list(known):
            if k > 0:
                known[k ^ bits[0]] = across(known[k], orbs, bits[0])
        found.append(known)
    near_by = [[whole], [across(whole, orbs, bits[0])]]
    return near_by + [[known[k] for known in found] for k in range(2, orbs)]


def per_device(orbitals, box_offset, send_index, pair_left):
    count = orbitals.shape[0]
    spaces, orbs = lax.axis_size("space"), lax.axis_size("orb")
    grid_cells = spaces * HALF
    space, orb = lax.axis_index("space"), lax.axis_index("orb")
    group_first = space * orbs * count
    offsets = box_offset.reshape(-1)

    free = LANES - USED
    entries = jnp.concatenate([send_index[0].reshape(-1), pair_left[0].reshape(-1)])
    lines = 4 * orbs // free
    table = jnp.pad(
        entries.astype(jnp.float32).reshape(lines, free), ((0, B - lines), (USED, 0))
    )
    whole, *halves = pack(orbitals, table)

    incoming = along_space(whole, -1)
    pieces = group_exchange(whole, halves, orbs)
    where = jnp.stack([group_first, ((space + 1) % spaces * orbs + orb) * count, orb])
    near, far, index = forward_pairs(where, offsets, pieces, incoming, count, grid_cells)
    near = lax.all_to_all(near, "orb", split_axis=0, concat_axis=0, tiled=True)
    far = along_space(far, 1)
    field = group_pairs(
        where, offsets, pair_left[0, 0], send_index[0, 0], index, pieces, count, grid_cells
    )
    return finish(field, near, far, pair_left[0, 1])


def solution(mesh):
    split = P(("space", "orb"), None, None)
    return jax.shard_map(
        per_device, mesh=mesh, in_specs=(split, P(), split, split), out_specs=split,
        check_vma=False,
    )
```

```python
import functools

import jax
import jax.numpy as jnp
from jax import lax
from jax.experimental import pallas as pl
from jax.experimental.pallas import tpu as pltpu
from jax.sharding import PartitionSpec as P

B = 40
ITERS = 4
SCREEN = 0.25

GROUPS = 3
TILES = 14
LANES = 128
USED = GROUPS * B
SUB = 8
PLANES = B // SUB
CELLS = TILES * PLANES
CELL = 2 * SUB
HALF = B // 2
VMEM_BYTES = 52 * 2**20
FIELDS = 8


def lanes_of(shape):
    return lax.broadcasted_iota(jnp.int32, shape, len(shape) - 1)


def overlaps():
    pieces = []
    for b in range(B):
        group = b // TILES
        for flat in range(b * B // LANES, (b * B + B - 1) // LANES + 1):
            pieces.append((b, flat, b * B - flat * LANES - group * B))
    return pieces


def pack_body(box_ref, table_ref, first_ref, second_ref, stage):
    count = box_ref.shape[0]
    lane = lanes_of((B, LANES))
    for n in range(count):
        tiles = [jnp.zeros((B, LANES), jnp.float32) for _ in range(TILES)]
        loaded = {}
        for b, flat, shift in overlaps():
            if flat not in loaded:
                width = min(LANES, B * B - flat * LANES)
                part = box_ref[n, :, flat * LANES : flat * LANES + width].astype(jnp.float32)
                if width < LANES:
                    part = jnp.concatenate(
                        [part, jnp.zeros((B, LANES - width), jnp.float32)], axis=1
                    )
                stage[flat] = part
                loaded[flat] = jnp.concatenate(
                    [stage[flat, pl.ds(p, SUB, stride=PLANES), :] for p in range(PLANES)], axis=0
                )
            first = max(b * B, flat * LANES) - b * B + (b // TILES) * B
            last = min(b * B + B, flat * LANES + LANES) - b * B + (b // TILES) * B
            moved = pltpu.roll(loaded[flat], (-shift) % LANES, axis=1)
            keep = (lane >= first) & (lane < last)
            tiles[b % TILES] = jnp.where(keep, moved, tiles[b % TILES])
        if n == 0:
            tiles[0] = tiles[0] + table_ref[...]
        out_ref = first_ref if n < count // 2 else second_ref
        for t in range(TILES):
            out_ref[n % (count // 2), t] = tiles[t].astype(out_ref.dtype)


def pack(orbitals, table):
    count = orbitals.shape[0]
    return pl.pallas_call(
        pack_body,
        out_shape=[jax.ShapeDtypeStruct((count // 2, TILES, B, LANES), jnp.bfloat16)] * 2,
        in_specs=[pl.BlockSpec(memory_space=pltpu.VMEM)] * 2,
        out_specs=[pl.BlockSpec(memory_space=pltpu.VMEM)] * 2,
        scratch_shapes=[pltpu.VMEM((-(-B * B // LANES), B, LANES), jnp.float32)],
        compiler_params=pltpu.CompilerParams(vmem_limit_bytes=VMEM_BYTES),
        name="pack",
    )(orbitals, table)


def finish_body(count, slots, field_ref, near_ref, far_ref, row_ref, out_ref, total, stage):
    lane = lanes_of((B, LANES))
    for n in range(count):
        for t in range(TILES):
            total[n, t] = field_ref[n, t] + far_ref[n, t].astype(jnp.float32)

    def add(j, carry):
        row = row_ref[j]
        for t in range(TILES):
            total[row, t] += near_ref[j, t].astype(jnp.float32)
        return carry

    lax.fori_loop(0, slots, add, 0)
    for n in range(count):
        flats = {}
        for b, flat, shift in overlaps():
            first = max(b * B, flat * LANES) - flat * LANES
            last = min(b * B + B, flat * LANES + LANES) - flat * LANES
            moved = pltpu.roll(total[n, b % TILES], shift % LANES, axis=1)
            keep = (lane >= first) & (lane < last)
            before = flats.get(flat)
            flats[flat] = moved if before is None else jnp.where(keep, moved, before)
        for flat, value in flats.items():
            for p in range(PLANES):
                stage[flat, pl.ds(p, SUB, stride=PLANES), :] = value[p * SUB : p * SUB + SUB]
            width = min(LANES, B * B - flat * LANES)
            out_ref[n, :, flat * LANES : flat * LANES + width] = stage[flat, :, :width]


def finish(field, near, far, rows):
    count, slots = field.shape[0], near.shape[0]
    vmem = pl.BlockSpec(memory_space=pltpu.VMEM)
    return pl.pallas_call(
        functools.partial(finish_body, count, slots),
        out_shape=jax.ShapeDtypeStruct((count, B, B * B), jnp.float32),
        in_specs=[vmem, vmem, vmem, pl.BlockSpec(memory_space=pltpu.SMEM)],
        out_specs=vmem,
        scratch_shapes=[
            pltpu.VMEM((count, TILES, B, LANES), jnp.float32),
            pltpu.VMEM((-(-B * B // LANES), B, LANES), jnp.float32),
        ],
        compiler_params=pltpu.CompilerParams(vmem_limit_bytes=VMEM_BYTES),
        name="finish",
    )(field, near, far, rows)


def geometry(offset_ref, left, right, grid_cells):
    shift, live = [], jnp.int32(1)
    for axis in range(3):
        gap = offset_ref[3 * right + axis] - offset_ref[3 * left + axis] + grid_cells // 2
        gap = jnp.where(gap < 0, gap + grid_cells, gap)
        gap = jnp.where(gap >= grid_cells, gap - grid_cells, gap) - grid_cells // 2
        live = jnp.where((gap > HALF) | (gap < -HALF), 0, live)
        shift.append(gap)
    return shift, live


def lane_group(lane):
    return sum(jnp.where(lane >= B * (i + 1), 1, 0) for i in range(GROUPS))


def wrapped(shift, size):
    from_zero = B * size - shift
    quotient = (from_zero * (2**16 // size + 1)) >> 16
    start, turn = from_zero - size * quotient, quotient - B
    pairs = []
    for i in range(size):
        over = jnp.where(start + i >= size, 1, 0)
        pairs.append((start + i - size * over, turn + over))
    return pairs


def put_padded(pad, t, p, value):
    start = (t * PLANES + p) * CELL + SUB
    pad[start : start + SUB, :] = value


def displaced(pad, shift):
    lane = lanes_of((SUB, LANES))
    group = lane_group(lane)
    source_col = lane - group * B - shift[2]
    col_ok = (source_col >= 0) & (source_col < B) & (lane < USED)
    source_row = jnp.where(col_ok, TILES * group - shift[1], -2 * B)
    rows = [p * CELL + SUB + turn for p, turn in wrapped(shift[0], PLANES)]
    for t, (source, turn) in enumerate(wrapped(shift[1], TILES)):
        keep = (source_row + t >= 0) & (source_row + t < B)
        if t >= B - TILES * (GROUPS - 1):
            keep = keep & (lane < USED - B)
        amount = (shift[2] - B * turn + 2 * LANES) & (LANES - 1)
        tile = []
        for p in range(PLANES):
            block = pad[pl.ds(source * (PLANES * CELL) + rows[p], SUB), :]
            tile.append(jnp.where(keep, pltpu.roll(block, amount, axis=1), 0.0))
        yield t, tile


def tree_sum(values):
    while len(values) > 1:
        paired = [a + b for a, b in zip(values[::2], values[1::2])]
        values = paired + ([values[-1]] if len(values) % 2 else [])
    return values[0]


def blocks(value):
    return [value[p * SUB : p * SUB + SUB] for p in range(PLANES)]


def cell(t, p):
    start = (t * PLANES + p) * SUB
    return slice(start, start + SUB)


def make_operator():
    lane = lanes_of((SUB, LANES))
    sublane = lax.broadcasted_iota(jnp.int32, (SUB, LANES), 0)
    column = lane - B * lane_group(lane)
    has_before = (column > 0) & (lane < USED)
    has_after = (column < B - 1) & (lane < USED)
    not_first = lane >= B
    not_last = lane < USED - B
    has_above = sublane > 0
    has_below = sublane < SUB - 1

    def operator(t, before, here, after):
        if t == 0:
            before = [jnp.where(not_first, pltpu.roll(v, B, axis=1), 0.0) for v in before]
        if t == TILES - 1:
            after = [jnp.where(not_last, pltpu.roll(v, LANES - B, axis=1), 0.0) for v in after]
        result = []
        for p in range(PLANES):
            if p == 0:
                above = jnp.where(has_above, pltpu.roll(here[PLANES - 1], 1, axis=0), 0.0)
            else:
                above = here[p - 1]
            if p == PLANES - 1:
                below = jnp.where(has_below, pltpu.roll(here[0], SUB - 1, axis=0), 0.0)
            else:
                below = here[p + 1]
            prior = jnp.where(has_before, pltpu.roll(here[p], 1, axis=1), 0.0)
            following = jnp.where(has_after, pltpu.roll(here[p], LANES - 1, axis=1), 0.0)
            around = (above + below) + (before[p] + after[p]) + (prior + following)
            value = (6.0 + SCREEN) * here[p] - around
            if t == B - TILES * (GROUPS - 1):
                value = jnp.where(not_last, value, 0.0)
            result.append(value)
        return result

    return operator


def side_by_side(used, body):
    def pair(i, carry):
        for _ in zip(body(2 * i, 0), body(2 * i + 1, 1)):
            pass
        return carry

    lax.fori_loop(0, used >> 1, pair, 0)

    @pl.when((used & 1) == 1)
    def _():
        for _ in body(used - 1, 0):
            pass


def solve(used, directions, residual, image, partial, norms, steps, ratios):
    operator = make_operator()

    def totals():
        rows = jnp.sum(partial[...], axis=1)
        return jnp.broadcast_to(jnp.sum(rows, axis=1, keepdims=True), rows.shape)

    norms[...] = totals()
    for k in range(ITERS):
        last = k == ITERS - 1

        def stencil(m, side, k=k, last=last):
            ratio = None if k == 0 else ratios[pl.ds(m, 1), :]

            def fetch(t, keep):
                values = []
                for p in range(PLANES):
                    if k == 0:
                        value = directions[0][m, cell(t, p), :]
                    else:
                        value = residual[m, cell(t, p), :]
                        value = value + ratio * directions[k - 1][m, cell(t, p), :]
                        if keep:
                            directions[k][m, cell(t, p), :] = value
                    values.append(value)
                return values

            before, here = fetch(TILES - 1, False), fetch(0, True)
            total = None
            for t in range(TILES):
                after = fetch((t + 1) % TILES, t < TILES - 1)
                applied = operator(t, before, here, after)
                if not last:
                    for p in range(PLANES):
                        image[m, cell(t, p), :] = applied[p]
                part = tree_sum([x * y for x, y in zip(here, applied)])
                total = part if total is None else total + part
                before, here = here, after
                yield
            partial[m] = total
            yield

        side_by_side(used, stencil)
        steps[k] = norms[...] / totals()
        if last:
            break
        source = directions[0] if k == 0 else residual

        def reduce(m, side, k=k, source=source):
            step = steps[k, pl.ds(m, 1), :]
            total = None
            for t in range(TILES):
                squares = []
                for p in range(PLANES):
                    value = source[m, cell(t, p), :] - step * image[m, cell(t, p), :]
                    residual[m, cell(t, p), :] = value
                    squares.append(value * value)
                part = tree_sum(squares)
                total = part if total is None else total + part
                yield
            partial[m] = total
            yield

        side_by_side(used, reduce)
        new = totals()
        ratios[...] = new / norms[...]
        norms[...] = new


def run_slots(used, nears, fars, shift_of, left_at, right_at, near_to, far_to, scratch):
    pads, shifted, partial, norms, steps, ratios, residual, image, *directions = scratch

    def load(m, side):
        pad = pads.at[side]
        for t in range(TILES):
            for p, block in enumerate(blocks(right_at(m, t))):
                put_padded(pad, t, p, block)
            yield
        total = None
        for t, moved in displaced(pad, shift_of(m)):
            squares = []
            for p, left in enumerate(blocks(left_at(m, t))):
                shifted[m, cell(t, p), :] = moved[p]
                density = moved[p] * left
                directions[0][m, cell(t, p), :] = density
                squares.append(density * density)
            part = tree_sum(squares)
            total = part if total is None else total + part
            yield
        partial[m] = total
        yield

    side_by_side(used, load)
    solve(used, directions, residual, image, partial, norms, steps, ratios)

    def potential(m, t):
        weights = [steps[k, pl.ds(m, 1), :] for k in range(ITERS)]
        return [
            tree_sum([w * d[m, cell(t, p), :] for w, d in zip(weights, directions)])
            for p in range(PLANES)
        ]

    def unload(near, far):
        def one(m, carry):
            pad = pads.at[0]
            for t in range(TILES):
                solved = potential(m, t)
                if near:
                    near_to(
                        m, t,
                        jnp.concatenate(
                            [v * shifted[m, cell(t, p), :] for p, v in enumerate(solved)], axis=0
                        ),
                    )
                if far:
                    for p, left in enumerate(blocks(left_at(m, t))):
                        put_padded(pad, t, p, solved[p] * left)
            if far:
                for t, moved in displaced(pad, [-s for s in shift_of(m)]):
                    far_to(m, t, jnp.concatenate(moved, axis=0))
            return carry

        return one

    if nears is fars:
        lax.fori_loop(*nears, unload(True, True), 0)
    else:
        lax.fori_loop(*nears, unload(True, False), 0)
        lax.fori_loop(*fars, unload(False, True), 0)


def slot_scratch(batch):
    row = pltpu.VMEM((batch, LANES), jnp.float32)
    box = pltpu.VMEM((batch, CELLS * SUB, LANES), jnp.float32)
    return [
        pltpu.SMEM((batch * FIELDS,), jnp.int32),
        pltpu.VMEM((2, CELLS * CELL + SUB, LANES), jnp.float32),
        box,
        pltpu.VMEM((batch, SUB, LANES), jnp.float32),
        row,
        pltpu.VMEM((ITERS, batch, LANES), jnp.float32),
        row,
    ] + [box] * (2 + ITERS)


def clear(ref):
    for n in range(ref.shape[0]):
        for t in range(TILES):
            ref[n, t] = jnp.zeros((B, LANES), ref.dtype)


def append(listed, used, values):
    for i, value in enumerate(values):
        listed[used * FIELDS + i] = value


def piece_copies(pieces, index, held, slot, sem):
    part = pieces[0].shape[0]
    for h, piece in enumerate(pieces):

        @pl.when((index >= h * part) & (index < (h + 1) * part))
        def _(h=h, piece=piece):
            pltpu.make_async_copy(piece.at[index - h * part], held.at[slot], sem).start()


def wait_box(pieces, held, slot, sem):
    pltpu.make_async_copy(pieces[0].at[0], held.at[slot], sem).wait()


def read_tables(meta, orbs, me, count, index_ref):
    free = LANES - USED
    lines = orbs // free
    bits = count.bit_length() - 1
    row = lax.broadcasted_iota(jnp.int32, (B, LANES), 0)
    lane = lanes_of((B, LANES)) - USED

    def digits(value, length):
        value = value.astype(jnp.int32)
        for _ in range(length):
            rest = value >> bits if count == 1 << bits else lax.div(value, count)
            yield value - rest * count
            value = rest

    weight = jnp.zeros((B, LANES), jnp.float32)
    for place, kind in enumerate((0, 2, 3)):
        chosen = (row - kind * lines) * free + lane == me
        chosen = chosen & (lane >= 0)
        weight = jnp.where(chosen, float(count**place), weight)
    for k in range(orbs):
        source = jnp.bitwise_xor(me, k)
        total = jnp.sum(meta[k].astype(jnp.float32) * weight)
        for kind, value in enumerate(digits(total, 3)):
            index_ref[kind * orbs + source] = value
    weight = jnp.zeros((B, LANES), jnp.float32)
    for place in range(free):
        weight = jnp.where(lane == place, float(count**place), weight)
    arrived = meta[orbs].astype(jnp.float32) * weight
    for line in range(lines):
        total = jnp.sum(jnp.where(row == lines + line, arrived, 0.0))
        for place, value in enumerate(digits(total, free)):
            index_ref[3 * orbs + line * free + place] = value


def forward_body(orbs, count, grid_cells, where_ref, offset_ref, *refs):
    pieces = [refs[2 * k : 2 * k + 2] for k in range(orbs)]
    incoming = refs[2 * orbs : 2 * orbs + 2]
    near_ref, far_ref, index_ref, meta, held, far_sum, meta_sem, box_sem, listed = refs[
        2 * orbs + 2 : 2 * orbs + 11
    ]
    scratch = refs[2 * orbs + 11 :]
    batch = listed.shape[0] // FIELDS
    part = count // 2
    me = where_ref[2]
    first_left, first_right = where_ref[0], where_ref[1]

    tables = [
        pltpu.make_async_copy(source[0].at[0, 0], meta.at[k], meta_sem.at[k])
        for k, source in enumerate(pieces + [incoming])
    ]
    for copy in tables:
        copy.start()
    rights = [
        pltpu.make_async_copy(
            incoming[n // part].at[n % part], held.at[orbs + n], box_sem.at[orbs + n]
        )
        for n in range(count)
    ]
    for copy in rights:
        copy.start()
    scratch[0][...] = jnp.zeros(scratch[0].shape, jnp.float32)
    clear(far_sum)
    for copy in tables:
        copy.wait()
    read_tables(meta, orbs, me, count, index_ref)
    for k in range(orbs):
        source = jnp.bitwise_xor(me, k)
        piece_copies(pieces[k], index_ref[2 * orbs + source], held, source, box_sem.at[k])
    for k in range(orbs):
        wait_box(pieces[k], held, jnp.bitwise_xor(me, k), box_sem.at[k])
    for copy in rights:
        copy.wait()

    def run(i, carry):
        def gather(j, used):
            slot = i * batch + j
            left, right = slot * count + index_ref[2 * orbs + slot], index_ref[3 * orbs + slot]
            shift, live = geometry(
                offset_ref, first_left + left, first_right + right, grid_cells
            )

            @pl.when(live == 1)
            def _():
                append(listed, used, [slot, orbs + right, *shift])

            @pl.when(live == 0)
            def _():
                for t in range(TILES):
                    near_ref[slot, t] = jnp.zeros((B, LANES), near_ref.dtype)

            return used + live

        used = lax.fori_loop(0, batch, gather, jnp.int32(0))

        def shift_of(m):
            return [listed[m * FIELDS + 2 + axis] for axis in range(3)]

        def near_to(m, t, value):
            near_ref[listed[m * FIELDS], t] = value.astype(near_ref.dtype)

        def far_to(m, t, value):
            far_sum[listed[m * FIELDS + 1] - orbs, t] += value

        every = (0, used)
        run_slots(
            used, every, every, shift_of,
            lambda m, t: held[listed[m * FIELDS], t].astype(jnp.float32),
            lambda m, t: held[listed[m * FIELDS + 1], t].astype(jnp.float32),
            near_to, far_to, scratch,
        )
        return carry

    lax.fori_loop(0, orbs // batch, run, 0)
    for n in range(count):
        for t in range(TILES):
            far_ref[n, t] = far_sum[n, t].astype(far_ref.dtype)


def forward_pairs(where, offsets, pieces, incoming, count, grid_cells):
    orbs = len(pieces)
    vmem, smem, left = (pl.BlockSpec(memory_space=m) for m in (pltpu.VMEM, pltpu.SMEM, pl.ANY))
    shape = (TILES, B, LANES)
    return pl.pallas_call(
        functools.partial(forward_body, orbs, count, grid_cells),
        out_shape=(
            jax.ShapeDtypeStruct((orbs,) + shape, jnp.bfloat16),
            jax.ShapeDtypeStruct((count,) + shape, jnp.bfloat16),
            jax.ShapeDtypeStruct((4 * orbs,), jnp.int32),
        ),
        in_specs=[smem] * 2 + [left] * (2 * orbs + 2),
        out_specs=(vmem, vmem, smem),
        scratch_shapes=[
            pltpu.VMEM((orbs + 1, B, LANES), jnp.bfloat16),
            pltpu.VMEM((orbs + count,) + shape, jnp.bfloat16),
            pltpu.VMEM((count,) + shape, jnp.float32),
            pltpu.SemaphoreType.DMA((orbs + 1,)),
            pltpu.SemaphoreType.DMA((orbs + count,)),
        ] + slot_scratch(8),
        compiler_params=pltpu.CompilerParams(vmem_limit_bytes=VMEM_BYTES),
        name="forward_pairs",
    )(where, offsets, *[half for piece in pieces for half in piece], *incoming)


def group_body(orbs, count, grid_cells, where_ref, offset_ref, mine_ref, sent_ref, index_ref, *refs):
    pieces = [refs[2 * k : 2 * k + 2] for k in range(orbs)]
    field, held, sem, listed = refs[2 * orbs : 2 * orbs + 4]
    scratch = refs[2 * orbs + 4 :]
    half = listed.shape[0] // FIELDS // 2
    part = count // 2
    first, me = where_ref[0], where_ref[2]
    mine = me * count
    own = 2 * orbs

    for k in range(orbs):
        source = jnp.bitwise_xor(me, k)
        piece_copies(pieces[k], index_ref[source], held, source, sem.at[k])
        piece_copies(pieces[k], index_ref[orbs + source], held, orbs + source, sem.at[orbs + k])
    owned = [
        pltpu.make_async_copy(pieces[0][n // part].at[n % part], held.at[own + n], sem.at[own + n])
        for n in range(count)
    ]
    for copy in owned:
        copy.start()
    scratch[0][...] = jnp.zeros(scratch[0].shape, jnp.float32)
    clear(field)
    for k in range(orbs):
        source = jnp.bitwise_xor(me, k)
        wait_box(pieces[k], held, source, sem.at[k])
        wait_box(pieces[k], held, orbs + source, sem.at[orbs + k])
    for copy in owned:
        copy.wait()

    def run(i, carry):
        def listing(near):
            def gather(j, used):
                slot = i * half + ((me + 1 + j) & (half - 1))
                if near:
                    left, right = mine + mine_ref[slot], slot * count + index_ref[slot]
                    boxes = [own + mine_ref[slot], slot]
                else:
                    left, right = slot * count + index_ref[orbs + slot], mine + sent_ref[slot]
                    boxes = [orbs + slot, own + sent_ref[slot]]
                shift, live = geometry(offset_ref, first + left, first + right, grid_cells)
                if not near:
                    live = jnp.where(slot == me, 0, live)
                else:
                    boxes[1] = jnp.where(slot == me, own + index_ref[slot], boxes[1])

                @pl.when(live == 1)
                def _():
                    append(listed, used, boxes + [*shift])

                return used + live

            return gather

        near_count = lax.fori_loop(0, half, listing(True), jnp.int32(0))
        used = lax.fori_loop(0, half, listing(False), near_count)
        left, right = mine + mine_ref[me], mine + index_ref[me]
        inside = geometry(offset_ref, first + left, first + right, grid_cells)[1]
        inside = jnp.where((me >= i * half) & (me < (i + 1) * half), inside, 0)

        def shift_of(m):
            return [listed[m * FIELDS + 2 + axis] for axis in range(3)]

        def near_to(m, t, value):
            field[listed[m * FIELDS] - own, t] += value

        def far_to(m, t, value):
            field[listed[m * FIELDS + 1] - own, t] += value

        run_slots(
            used, (0, near_count), (near_count - inside, used), shift_of,
            lambda m, t: held[listed[m * FIELDS], t].astype(jnp.float32),
            lambda m, t: held[listed[m * FIELDS + 1], t].astype(jnp.float32),
            near_to, far_to, scratch,
        )
        return carry

    lax.fori_loop(0, orbs // half, run, 0)


def group_pairs(where, offsets, mine, sent, index, pieces, count, grid_cells):
    orbs = len(pieces)
    vmem, smem, left = (pl.BlockSpec(memory_space=m) for m in (pltpu.VMEM, pltpu.SMEM, pl.ANY))
    shape = (TILES, B, LANES)
    return pl.pallas_call(
        functools.partial(group_body, orbs, count, grid_cells),
        out_shape=jax.ShapeDtypeStruct((count,) + shape, jnp.float32),
        in_specs=[smem] * 5 + [left] * (2 * orbs),
        out_specs=vmem,
        scratch_shapes=[
            pltpu.VMEM((2 * orbs + count,) + shape, jnp.bfloat16),
            pltpu.SemaphoreType.DMA((2 * orbs + count,)),
        ] + slot_scratch(16),
        compiler_params=pltpu.CompilerParams(vmem_limit_bytes=VMEM_BYTES),
        name="group_pairs",
    )(where, offsets, mine, sent, index, *[half for piece in pieces for half in piece])


def along_space(block, distance):
    size = lax.axis_size("space")
    return lax.ppermute(block, "space", [((i - distance) % size, i) for i in range(size)])


def group_exchange(packed, orbs):
    bits = [1 << i for i in range(orbs.bit_length() - 1)]
    orders = (bits[1:] + bits[:1], bits[:0:-1] + bits[:1])
    halves = []
    for block, order in zip(packed, orders):
        known = {0: block}
        for bit in order:
            route = [(i, i ^ bit) for i in range(orbs)]
            for k in list(known):
                known[k ^ bit] = lax.ppermute(known[k], "orb", route)
        halves.append(known)
    return [[known[k] for known in halves] for k in range(orbs)]


def per_device(orbitals, box_offset, send_index, pair_left):
    count = orbitals.shape[0]
    spaces, orbs = lax.axis_size("space"), lax.axis_size("orb")
    grid_cells = spaces * HALF
    space, orb = lax.axis_index("space"), lax.axis_index("orb")
    group_first = space * orbs * count
    offsets = box_offset.reshape(-1)

    free = LANES - USED
    entries = jnp.concatenate([send_index[0].reshape(-1), pair_left[0].reshape(-1)])
    lines = 4 * orbs // free
    table = jnp.pad(
        entries.astype(jnp.float32).reshape(lines, free), ((0, B - lines), (USED, 0))
    )
    packed = pack(orbitals, table)

    incoming = [along_space(half, -1) for half in packed]
    pieces = group_exchange(packed, orbs)
    where = jnp.stack([group_first, ((space + 1) % spaces * orbs + orb) * count, orb])
    near, far, index = forward_pairs(where, offsets, pieces, incoming, count, grid_cells)
    near = lax.all_to_all(near, "orb", split_axis=0, concat_axis=0, tiled=True)
    far = along_space(far, 1)
    field = group_pairs(
        where, offsets, pair_left[0, 0], send_index[0, 0], index, pieces, count, grid_cells
    )
    return finish(field, near, far, pair_left[0, 1])


def solution(mesh):
    split = P(("space", "orb"), None, None)
    return jax.shard_map(
        per_device, mesh=mesh, in_specs=(split, P(), split, split), out_specs=split,
        check_vma=False,
    )
```

```python
import functools

import jax
import jax.numpy as jnp
from jax import lax
from jax.experimental import pallas as pl
from jax.experimental.pallas import tpu as pltpu
from jax.sharding import PartitionSpec as P

B = 40
ITERS = 4
SCREEN = 0.25

GROUPS = 3
TILES = 14
LANES = 128
USED = GROUPS * B
SUB = 8
PLANES = B // SUB
CELLS = TILES * PLANES
CELL = 2 * SUB
HALF = B // 2
VMEM_BYTES = 56 * 2**20
FIELDS = 8


def lanes_of(shape):
    return lax.broadcasted_iota(jnp.int32, shape, len(shape) - 1)


def overlaps():
    pieces = []
    for b in range(B):
        group = b // TILES
        for flat in range(b * B // LANES, (b * B + B - 1) // LANES + 1):
            pieces.append((b, flat, b * B - flat * LANES - group * B))
    return pieces


def pack_body(box_ref, table_ref, first_ref, second_ref, stage):
    count = box_ref.shape[0]
    lane = lanes_of((B, LANES))
    for n in range(count):
        tiles = [jnp.zeros((B, LANES), jnp.float32) for _ in range(TILES)]
        loaded = {}
        for b, flat, shift in overlaps():
            if flat not in loaded:
                width = min(LANES, B * B - flat * LANES)
                part = box_ref[n, :, flat * LANES : flat * LANES + width].astype(jnp.float32)
                if width < LANES:
                    part = jnp.concatenate(
                        [part, jnp.zeros((B, LANES - width), jnp.float32)], axis=1
                    )
                stage[flat] = part
                loaded[flat] = jnp.concatenate(
                    [stage[flat, pl.ds(p, SUB, stride=PLANES), :] for p in range(PLANES)], axis=0
                )
            first = max(b * B, flat * LANES) - b * B + (b // TILES) * B
            last = min(b * B + B, flat * LANES + LANES) - b * B + (b // TILES) * B
            moved = pltpu.roll(loaded[flat], (-shift) % LANES, axis=1)
            keep = (lane >= first) & (lane < last)
            tiles[b % TILES] = jnp.where(keep, moved, tiles[b % TILES])
        if n == 0:
            tiles[0] = tiles[0] + table_ref[...]
        out_ref = first_ref if n < count // 2 else second_ref
        for t in range(TILES):
            out_ref[n % (count // 2), t] = tiles[t].astype(out_ref.dtype)


def pack(orbitals, table):
    count = orbitals.shape[0]
    return pl.pallas_call(
        pack_body,
        out_shape=[jax.ShapeDtypeStruct((count // 2, TILES, B, LANES), jnp.bfloat16)] * 2,
        in_specs=[pl.BlockSpec(memory_space=pltpu.VMEM)] * 2,
        out_specs=[pl.BlockSpec(memory_space=pltpu.VMEM)] * 2,
        scratch_shapes=[pltpu.VMEM((-(-B * B // LANES), B, LANES), jnp.float32)],
        compiler_params=pltpu.CompilerParams(vmem_limit_bytes=VMEM_BYTES),
        name="pack",
    )(orbitals, table)


def finish_body(count, slots, field_ref, near_ref, far_ref, row_ref, out_ref, total, stage):
    lane = lanes_of((B, LANES))
    for n in range(count):
        for t in range(TILES):
            total[n, t] = field_ref[n, t] + far_ref[n, t].astype(jnp.float32)

    def add(j, carry):
        row = row_ref[j]
        for t in range(TILES):
            total[row, t] += near_ref[j, t].astype(jnp.float32)
        return carry

    lax.fori_loop(0, slots, add, 0)
    for n in range(count):
        flats = {}
        for b, flat, shift in overlaps():
            first = max(b * B, flat * LANES) - flat * LANES
            last = min(b * B + B, flat * LANES + LANES) - flat * LANES
            moved = pltpu.roll(total[n, b % TILES], shift % LANES, axis=1)
            keep = (lane >= first) & (lane < last)
            before = flats.get(flat)
            flats[flat] = moved if before is None else jnp.where(keep, moved, before)
        for flat, value in flats.items():
            for p in range(PLANES):
                stage[flat, pl.ds(p, SUB, stride=PLANES), :] = value[p * SUB : p * SUB + SUB]
            width = min(LANES, B * B - flat * LANES)
            out_ref[n, :, flat * LANES : flat * LANES + width] = stage[flat, :, :width]


def finish(field, near, far, rows):
    count, slots = field.shape[0], near.shape[0]
    vmem = pl.BlockSpec(memory_space=pltpu.VMEM)
    return pl.pallas_call(
        functools.partial(finish_body, count, slots),
        out_shape=jax.ShapeDtypeStruct((count, B, B * B), jnp.float32),
        in_specs=[vmem, vmem, vmem, pl.BlockSpec(memory_space=pltpu.SMEM)],
        out_specs=vmem,
        scratch_shapes=[
            pltpu.VMEM((count, TILES, B, LANES), jnp.float32),
            pltpu.VMEM((-(-B * B // LANES), B, LANES), jnp.float32),
        ],
        compiler_params=pltpu.CompilerParams(vmem_limit_bytes=VMEM_BYTES),
        name="finish",
    )(field, near, far, rows)


def geometry(offset_ref, left, right, grid_cells):
    shift, live = [], jnp.int32(1)
    for axis in range(3):
        gap = offset_ref[3 * right + axis] - offset_ref[3 * left + axis] + grid_cells // 2
        gap = jnp.where(gap < 0, gap + grid_cells, gap)
        gap = jnp.where(gap >= grid_cells, gap - grid_cells, gap) - grid_cells // 2
        live = jnp.where((gap > HALF) | (gap < -HALF), 0, live)
        shift.append(gap)
    return shift, live


def lane_group(lane):
    return sum(jnp.where(lane >= B * (i + 1), 1, 0) for i in range(GROUPS))


def wrapped(shift, size):
    from_zero = B * size - shift
    quotient = (from_zero * (2**16 // size + 1)) >> 16
    start, turn = from_zero - size * quotient, quotient - B
    pairs = []
    for i in range(size):
        over = jnp.where(start + i >= size, 1, 0)
        pairs.append((start + i - size * over, turn + over))
    return pairs


def put_padded(pad, t, p, value):
    start = (t * PLANES + p) * CELL + SUB
    pad[start : start + SUB, :] = value


def displaced(pad, shift):
    lane = lanes_of((SUB, LANES))
    group = lane_group(lane)
    source_col = lane - group * B - shift[2]
    col_ok = (source_col >= 0) & (source_col < B) & (lane < USED)
    source_row = jnp.where(col_ok, TILES * group - shift[1], -2 * B)
    rows = [p * CELL + SUB + turn for p, turn in wrapped(shift[0], PLANES)]
    for t, (source, turn) in enumerate(wrapped(shift[1], TILES)):
        keep = (source_row + t >= 0) & (source_row + t < B)
        if t >= B - TILES * (GROUPS - 1):
            keep = keep & (lane < USED - B)
        amount = (shift[2] - B * turn + 2 * LANES) & (LANES - 1)
        tile = []
        for p in range(PLANES):
            block = pad[pl.ds(source * (PLANES * CELL) + rows[p], SUB), :]
            tile.append(jnp.where(keep, pltpu.roll(block, amount, axis=1), 0.0))
        yield t, tile


def tree_sum(values):
    while len(values) > 1:
        paired = [a + b for a, b in zip(values[::2], values[1::2])]
        values = paired + ([values[-1]] if len(values) % 2 else [])
    return values[0]


def blocks(value):
    return [value[p * SUB : p * SUB + SUB] for p in range(PLANES)]


def cell(t, p):
    start = (t * PLANES + p) * SUB
    return slice(start, start + SUB)


def make_operator():
    lane = lanes_of((SUB, LANES))
    sublane = lax.broadcasted_iota(jnp.int32, (SUB, LANES), 0)
    column = lane - B * lane_group(lane)
    has_before = (column > 0) & (lane < USED)
    has_after = (column < B - 1) & (lane < USED)
    not_first = lane >= B
    not_last = lane < USED - B
    has_above = sublane > 0
    has_below = sublane < SUB - 1

    def operator(t, before, here, after):
        if t == 0:
            before = [jnp.where(not_first, pltpu.roll(v, B, axis=1), 0.0) for v in before]
        if t == TILES - 1:
            after = [jnp.where(not_last, pltpu.roll(v, LANES - B, axis=1), 0.0) for v in after]
        result = []
        for p in range(PLANES):
            if p == 0:
                above = jnp.where(has_above, pltpu.roll(here[PLANES - 1], 1, axis=0), 0.0)
            else:
                above = here[p - 1]
            if p == PLANES - 1:
                below = jnp.where(has_below, pltpu.roll(here[0], SUB - 1, axis=0), 0.0)
            else:
                below = here[p + 1]
            prior = jnp.where(has_before, pltpu.roll(here[p], 1, axis=1), 0.0)
            following = jnp.where(has_after, pltpu.roll(here[p], LANES - 1, axis=1), 0.0)
            around = (above + below) + (before[p] + after[p]) + (prior + following)
            value = (6.0 + SCREEN) * here[p] - around
            if t == B - TILES * (GROUPS - 1):
                value = jnp.where(not_last, value, 0.0)
            result.append(value)
        return result

    return operator


def side_by_side(used, body):
    def pair(i, carry):
        for _ in zip(body(2 * i, 0), body(2 * i + 1, 1)):
            pass
        return carry

    lax.fori_loop(0, used >> 1, pair, 0)

    @pl.when((used & 1) == 1)
    def _():
        for _ in body(used - 1, 0):
            pass


def put_sum(sums, kind, m, value):
    sums[kind, pl.ds(m, 1), :] = jnp.sum(value, axis=0, keepdims=True)


def solve(used, directions, residuals, images, sums, steps, ratios):
    operator = make_operator()

    for k in range(ITERS):
        last = k == ITERS - 1
        source = directions[0] if k == 1 else residuals[k % 2]
        target = residuals[(k + 1) % 2]

        def stencil(m, side, k=k, last=last, source=source, target=target):
            squares = []
            if k > 0:
                step = jnp.broadcast_to(steps[k - 1, pl.ds(m, 1), :], (SUB, LANES))
                ratio = jnp.broadcast_to(ratios[pl.ds(m, 1), :], (SUB, LANES))

            def stored(t):
                return [directions[k][m, cell(t, p), :] for p in range(PLANES)]

            def fetch(t):
                if k == 0:
                    return stored(t)
                values, parts = [], []
                for p in range(PLANES):
                    left = source[m, cell(t, p), :] - step * images[(k - 1) % 2][m, cell(t, p), :]
                    if not last:
                        target[m, cell(t, p), :] = left
                    parts.append(left * left)
                    value = left + ratio * directions[k - 1][m, cell(t, p), :]
                    directions[k][m, cell(t, p), :] = value
                    values.append(value)
                squares.append(tree_sum(parts))
                if len(squares) == 2:
                    squares[:] = [squares[0] + squares[1]]
                return values

            before, here = fetch(TILES - 1), fetch(0)
            total = spread = None
            for t in range(TILES):
                after = fetch(t + 1) if t < TILES - 2 else stored((t + 1) % TILES)
                applied = operator(t, before, here, after)
                if not last:
                    for p in range(PLANES):
                        images[k % 2][m, cell(t, p), :] = applied[p]
                    part = tree_sum([x * x for x in applied])
                    spread = part if spread is None else spread + part
                part = tree_sum([x * y for x, y in zip(here, applied)])
                total = part if total is None else total + part
                before, here = here, after
                yield
            put_sum(sums, 1, m, total)
            if not last:
                put_sum(sums, 2, m, spread)
            if k > 0:
                put_sum(sums, 0, m, squares[0])
            yield

        side_by_side(used, stencil)
        norm, product, square = (
            jnp.broadcast_to(jnp.sum(sums[kind], axis=1, keepdims=True), sums.shape[1:])
            for kind in range(3)
        )
        step = norm / product
        steps[k] = step
        if not last:
            ratios[...] = jnp.maximum(step * step * square - norm, 0.0) / norm


def run_slots(used, nears, fars, shift_of, left_at, right_at, near_to, far_to, scratch):
    pads, shifted, sums, steps, ratios, *boxes = scratch
    residuals, images, directions = boxes[:2], boxes[2:4], boxes[4:]

    def load(m, side):
        pad = pads.at[side]
        for t in range(TILES):
            for p, block in enumerate(blocks(right_at(m, t))):
                put_padded(pad, t, p, block)
            yield
        total = None
        for t, moved in displaced(pad, shift_of(m)):
            squares = []
            for p, left in enumerate(blocks(left_at(m, t))):
                shifted[m, cell(t, p), :] = moved[p]
                density = moved[p] * left
                directions[0][m, cell(t, p), :] = density
                squares.append(density * density)
            part = tree_sum(squares)
            total = part if total is None else total + part
            yield
        put_sum(sums, 0, m, total)
        yield

    side_by_side(used, load)
    solve(used, directions, residuals, images, sums, steps, ratios)

    def potential(m, t):
        weights = [steps[k, pl.ds(m, 1), :] for k in range(ITERS)]
        return [
            tree_sum([w * d[m, cell(t, p), :] for w, d in zip(weights, directions)])
            for p in range(PLANES)
        ]

    def unload(near, far):
        def one(m, carry):
            pad = pads.at[0]
            for t in range(TILES):
                solved = potential(m, t)
                if near:
                    near_to(
                        m, t,
                        jnp.concatenate(
                            [v * shifted[m, cell(t, p), :] for p, v in enumerate(solved)], axis=0
                        ),
                    )
                if far:
                    for p, left in enumerate(blocks(left_at(m, t))):
                        put_padded(pad, t, p, solved[p] * left)
            if far:
                for t, moved in displaced(pad, [-s for s in shift_of(m)]):
                    far_to(m, t, jnp.concatenate(moved, axis=0))
            return carry

        return one

    if nears is fars:
        lax.fori_loop(*nears, unload(True, True), 0)
    else:
        lax.fori_loop(*nears, unload(True, False), 0)
        lax.fori_loop(*fars, unload(False, True), 0)


def slot_scratch(batch):
    row = pltpu.VMEM((batch, LANES), jnp.float32)
    box = pltpu.VMEM((batch, CELLS * SUB, LANES), jnp.float32)
    return [
        pltpu.SMEM((batch * FIELDS,), jnp.int32),
        pltpu.VMEM((2, CELLS * CELL + SUB, LANES), jnp.float32),
        box,
        pltpu.VMEM((3, batch, LANES), jnp.float32),
        pltpu.VMEM((ITERS, batch, LANES), jnp.float32),
        row,
    ] + [box] * (4 + ITERS)


def clear(ref):
    for n in range(ref.shape[0]):
        for t in range(TILES):
            ref[n, t] = jnp.zeros((B, LANES), ref.dtype)


def append(listed, used, values):
    for i, value in enumerate(values):
        listed[used * FIELDS + i] = value


def piece_copies(pieces, index, held, slot, sem):
    part = pieces[0].shape[0]
    for h, piece in enumerate(pieces):

        @pl.when((index >= h * part) & (index < (h + 1) * part))
        def _(h=h, piece=piece):
            pltpu.make_async_copy(piece.at[index - h * part], held.at[slot], sem).start()


def wait_box(pieces, held, slot, sem):
    pltpu.make_async_copy(pieces[0].at[0], held.at[slot], sem).wait()


def read_tables(meta, orbs, me, count, index_ref):
    free = LANES - USED
    lines = orbs // free
    bits = count.bit_length() - 1
    row = lax.broadcasted_iota(jnp.int32, (B, LANES), 0)
    lane = lanes_of((B, LANES)) - USED

    def digits(value, length):
        value = value.astype(jnp.int32)
        for _ in range(length):
            rest = value >> bits if count == 1 << bits else lax.div(value, count)
            yield value - rest * count
            value = rest

    weight = jnp.zeros((B, LANES), jnp.float32)
    for place, kind in enumerate((0, 2, 3)):
        chosen = (row - kind * lines) * free + lane == me
        chosen = chosen & (lane >= 0)
        weight = jnp.where(chosen, float(count**place), weight)
    for k in range(orbs):
        source = jnp.bitwise_xor(me, k)
        total = jnp.sum(meta[k].astype(jnp.float32) * weight)
        for kind, value in enumerate(digits(total, 3)):
            index_ref[kind * orbs + source] = value
    weight = jnp.zeros((B, LANES), jnp.float32)
    for place in range(free):
        weight = jnp.where(lane == place, float(count**place), weight)
    arrived = meta[orbs].astype(jnp.float32) * weight
    for line in range(lines):
        total = jnp.sum(jnp.where(row == lines + line, arrived, 0.0))
        for place, value in enumerate(digits(total, free)):
            index_ref[3 * orbs + line * free + place] = value


def forward_body(orbs, count, grid_cells, where_ref, offset_ref, *refs):
    pieces = [refs[2 * k : 2 * k + 2] for k in range(orbs)]
    incoming = refs[2 * orbs : 2 * orbs + 2]
    near_ref, far_ref, index_ref, meta, held, far_sum, meta_sem, box_sem, listed = refs[
        2 * orbs + 2 : 2 * orbs + 11
    ]
    scratch = refs[2 * orbs + 11 :]
    batch = listed.shape[0] // FIELDS
    part = count // 2
    me = where_ref[2]
    first_left, first_right = where_ref[0], where_ref[1]

    tables = [
        pltpu.make_async_copy(source[0].at[0, 0], meta.at[k], meta_sem.at[k])
        for k, source in enumerate(pieces + [incoming])
    ]
    for copy in tables:
        copy.start()
    rights = [
        pltpu.make_async_copy(
            incoming[n // part].at[n % part], held.at[orbs + n], box_sem.at[orbs + n]
        )
        for n in range(count)
    ]
    for copy in rights:
        copy.start()
    scratch[0][...] = jnp.zeros(scratch[0].shape, jnp.float32)
    clear(far_sum)
    for copy in tables:
        copy.wait()
    read_tables(meta, orbs, me, count, index_ref)
    for k in range(orbs):
        source = jnp.bitwise_xor(me, k)
        piece_copies(pieces[k], index_ref[2 * orbs + source], held, source, box_sem.at[k])
    for k in range(orbs):
        wait_box(pieces[k], held, jnp.bitwise_xor(me, k), box_sem.at[k])
    for copy in rights:
        copy.wait()

    def run(i, carry):
        def gather(j, used):
            slot = i * batch + j
            left, right = slot * count + index_ref[2 * orbs + slot], index_ref[3 * orbs + slot]
            shift, live = geometry(
                offset_ref, first_left + left, first_right + right, grid_cells
            )

            @pl.when(live == 1)
            def _():
                append(listed, used, [slot, orbs + right, *shift])

            @pl.when(live == 0)
            def _():
                for t in range(TILES):
                    near_ref[slot, t] = jnp.zeros((B, LANES), near_ref.dtype)

            return used + live

        used = lax.fori_loop(0, batch, gather, jnp.int32(0))

        def shift_of(m):
            return [listed[m * FIELDS + 2 + axis] for axis in range(3)]

        def near_to(m, t, value):
            near_ref[listed[m * FIELDS], t] = value.astype(near_ref.dtype)

        def far_to(m, t, value):
            far_sum[listed[m * FIELDS + 1] - orbs, t] += value

        every = (0, used)
        run_slots(
            used, every, every, shift_of,
            lambda m, t: held[listed[m * FIELDS], t].astype(jnp.float32),
            lambda m, t: held[listed[m * FIELDS + 1], t].astype(jnp.float32),
            near_to, far_to, scratch,
        )
        return carry

    lax.fori_loop(0, orbs // batch, run, 0)
    for n in range(count):
        for t in range(TILES):
            far_ref[n, t] = far_sum[n, t].astype(far_ref.dtype)


def forward_pairs(where, offsets, pieces, incoming, count, grid_cells):
    orbs = len(pieces)
    vmem, smem, left = (pl.BlockSpec(memory_space=m) for m in (pltpu.VMEM, pltpu.SMEM, pl.ANY))
    shape = (TILES, B, LANES)
    return pl.pallas_call(
        functools.partial(forward_body, orbs, count, grid_cells),
        out_shape=(
            jax.ShapeDtypeStruct((orbs,) + shape, jnp.bfloat16),
            jax.ShapeDtypeStruct((count,) + shape, jnp.bfloat16),
            jax.ShapeDtypeStruct((4 * orbs,), jnp.int32),
        ),
        in_specs=[smem] * 2 + [left] * (2 * orbs + 2),
        out_specs=(vmem, vmem, smem),
        scratch_shapes=[
            pltpu.VMEM((orbs + 1, B, LANES), jnp.bfloat16),
            pltpu.VMEM((orbs + count,) + shape, jnp.bfloat16),
            pltpu.VMEM((count,) + shape, jnp.float32),
            pltpu.SemaphoreType.DMA((orbs + 1,)),
            pltpu.SemaphoreType.DMA((orbs + count,)),
        ] + slot_scratch(8),
        compiler_params=pltpu.CompilerParams(vmem_limit_bytes=VMEM_BYTES),
        name="forward_pairs",
    )(where, offsets, *[half for piece in pieces for half in piece], *incoming)


def group_body(orbs, count, grid_cells, where_ref, offset_ref, mine_ref, sent_ref, index_ref, *refs):
    pieces = [refs[2 * k : 2 * k + 2] for k in range(orbs)]
    field, held, sem, listed = refs[2 * orbs : 2 * orbs + 4]
    scratch = refs[2 * orbs + 4 :]
    half = listed.shape[0] // FIELDS // 2
    part = count // 2
    first, me = where_ref[0], where_ref[2]
    mine = me * count
    own = 2 * orbs

    for k in range(orbs):
        source = jnp.bitwise_xor(me, k)
        piece_copies(pieces[k], index_ref[source], held, source, sem.at[k])
        piece_copies(pieces[k], index_ref[orbs + source], held, orbs + source, sem.at[orbs + k])
    owned = [
        pltpu.make_async_copy(pieces[0][n // part].at[n % part], held.at[own + n], sem.at[own + n])
        for n in range(count)
    ]
    for copy in owned:
        copy.start()
    scratch[0][...] = jnp.zeros(scratch[0].shape, jnp.float32)
    clear(field)
    for k in range(orbs):
        source = jnp.bitwise_xor(me, k)
        wait_box(pieces[k], held, source, sem.at[k])
        wait_box(pieces[k], held, orbs + source, sem.at[orbs + k])
    for copy in owned:
        copy.wait()

    def run(i, carry):
        def listing(near):
            def gather(j, used):
                slot = i * half + ((me + 1 + j) & (half - 1))
                if near:
                    left, right = mine + mine_ref[slot], slot * count + index_ref[slot]
                    boxes = [own + mine_ref[slot], slot]
                else:
                    left, right = slot * count + index_ref[orbs + slot], mine + sent_ref[slot]
                    boxes = [orbs + slot, own + sent_ref[slot]]
                shift, live = geometry(offset_ref, first + left, first + right, grid_cells)
                if not near:
                    live = jnp.where(slot == me, 0, live)
                else:
                    boxes[1] = jnp.where(slot == me, own + index_ref[slot], boxes[1])

                @pl.when(live == 1)
                def _():
                    append(listed, used, boxes + [*shift])

                return used + live

            return gather

        near_count = lax.fori_loop(0, half, listing(True), jnp.int32(0))
        used = lax.fori_loop(0, half, listing(False), near_count)
        left, right = mine + mine_ref[me], mine + index_ref[me]
        inside = geometry(offset_ref, first + left, first + right, grid_cells)[1]
        inside = jnp.where((me >= i * half) & (me < (i + 1) * half), inside, 0)

        def shift_of(m):
            return [listed[m * FIELDS + 2 + axis] for axis in range(3)]

        def near_to(m, t, value):
            field[listed[m * FIELDS] - own, t] += value

        def far_to(m, t, value):
            field[listed[m * FIELDS + 1] - own, t] += value

        run_slots(
            used, (0, near_count), (near_count - inside, used), shift_of,
            lambda m, t: held[listed[m * FIELDS], t].astype(jnp.float32),
            lambda m, t: held[listed[m * FIELDS + 1], t].astype(jnp.float32),
            near_to, far_to, scratch,
        )
        return carry

    lax.fori_loop(0, orbs // half, run, 0)


def group_pairs(where, offsets, mine, sent, index, pieces, count, grid_cells):
    orbs = len(pieces)
    vmem, smem, left = (pl.BlockSpec(memory_space=m) for m in (pltpu.VMEM, pltpu.SMEM, pl.ANY))
    shape = (TILES, B, LANES)
    return pl.pallas_call(
        functools.partial(group_body, orbs, count, grid_cells),
        out_shape=jax.ShapeDtypeStruct((count,) + shape, jnp.float32),
        in_specs=[smem] * 5 + [left] * (2 * orbs),
        out_specs=vmem,
        scratch_shapes=[
            pltpu.VMEM((2 * orbs + count,) + shape, jnp.bfloat16),
            pltpu.SemaphoreType.DMA((2 * orbs + count,)),
        ] + slot_scratch(16),
        compiler_params=pltpu.CompilerParams(vmem_limit_bytes=VMEM_BYTES),
        name="group_pairs",
    )(where, offsets, mine, sent, index, *[half for piece in pieces for half in piece])


def along_space(block, distance):
    size = lax.axis_size("space")
    return lax.ppermute(block, "space", [((i - distance) % size, i) for i in range(size)])


def group_exchange(packed, orbs):
    bits = [1 << i for i in range(orbs.bit_length() - 1)]
    orders = (bits[1:] + bits[:1], bits[:0:-1] + bits[:1])
    halves = []
    for block, order in zip(packed, orders):
        known = {0: block}
        for bit in order:
            route = [(i, i ^ bit) for i in range(orbs)]
            for k in list(known):
                known[k ^ bit] = lax.ppermute(known[k], "orb", route)
        halves.append(known)
    return [[known[k] for known in halves] for k in range(orbs)]


def per_device(orbitals, box_offset, send_index, pair_left):
    count = orbitals.shape[0]
    spaces, orbs = lax.axis_size("space"), lax.axis_size("orb")
    grid_cells = spaces * HALF
    space, orb = lax.axis_index("space"), lax.axis_index("orb")
    group_first = space * orbs * count
    offsets = box_offset.reshape(-1)

    free = LANES - USED
    entries = jnp.concatenate([send_index[0].reshape(-1), pair_left[0].reshape(-1)])
    lines = 4 * orbs // free
    table = jnp.pad(
        entries.astype(jnp.float32).reshape(lines, free), ((0, B - lines), (USED, 0))
    )
    packed = pack(orbitals, table)

    incoming = [along_space(half, -1) for half in packed]
    pieces = group_exchange(packed, orbs)
    where = jnp.stack([group_first, ((space + 1) % spaces * orbs + orb) * count, orb])
    near, far, index = forward_pairs(where, offsets, pieces, incoming, count, grid_cells)
    near = lax.all_to_all(near, "orb", split_axis=0, concat_axis=0, tiled=True)
    far = along_space(far, 1)
    field = group_pairs(
        where, offsets, pair_left[0, 0], send_index[0, 0], index, pieces, count, grid_cells
    )
    return finish(field, near, far, pair_left[0, 1])


def solution(mesh):
    split = P(("space", "orb"), None, None)
    return jax.shard_map(
        per_device, mesh=mesh, in_specs=(split, P(), split, split), out_specs=split,
        check_vma=False,
    )
```

```python
import functools

import jax
import jax.numpy as jnp
from jax import lax
from jax.experimental import pallas as pl
from jax.experimental.pallas import tpu as pltpu
from jax.sharding import PartitionSpec as P

B = 40
ITERS = 4
SCREEN = 0.25

GROUPS = 3
TILES = 14
LANES = 128
USED = GROUPS * B
SUB = 8
PLANES = B // SUB
CELLS = TILES * PLANES
CELL = 2 * SUB
HALF = B // 2
MIB = 2**20
FIELDS = 8


def lanes_of(shape):
    return lax.broadcasted_iota(jnp.int32, shape, len(shape) - 1)


def overlaps():
    pieces = []
    for b in range(B):
        group = b // TILES
        for flat in range(b * B // LANES, (b * B + B - 1) // LANES + 1):
            pieces.append((b, flat, b * B - flat * LANES - group * B))
    return pieces


def pack_body(box_ref, table_ref, first_ref, second_ref, stage):
    count = box_ref.shape[0]
    lane = lanes_of((B, LANES))
    for n in range(count):
        tiles = [jnp.zeros((B, LANES), jnp.float32) for _ in range(TILES)]
        loaded = {}
        for b, flat, shift in overlaps():
            if flat not in loaded:
                width = min(LANES, B * B - flat * LANES)
                part = box_ref[n, :, flat * LANES : flat * LANES + width].astype(jnp.float32)
                if width < LANES:
                    part = jnp.concatenate(
                        [part, jnp.zeros((B, LANES - width), jnp.float32)], axis=1
                    )
                stage[flat] = part
                loaded[flat] = jnp.concatenate(
                    [stage[flat, pl.ds(p, SUB, stride=PLANES), :] for p in range(PLANES)], axis=0
                )
            first = max(b * B, flat * LANES) - b * B + (b // TILES) * B
            last = min(b * B + B, flat * LANES + LANES) - b * B + (b // TILES) * B
            moved = pltpu.roll(loaded[flat], (-shift) % LANES, axis=1)
            keep = (lane >= first) & (lane < last)
            tiles[b % TILES] = jnp.where(keep, moved, tiles[b % TILES])
        if n == 0:
            tiles[0] = tiles[0] + table_ref[...]
        out_ref = first_ref if n < count // 2 else second_ref
        for t in range(TILES):
            out_ref[n % (count // 2), t] = tiles[t].astype(out_ref.dtype)


def pack(orbitals, table):
    count = orbitals.shape[0]
    return pl.pallas_call(
        pack_body,
        out_shape=[jax.ShapeDtypeStruct((count // 2, TILES, B, LANES), jnp.bfloat16)] * 2,
        in_specs=[pl.BlockSpec(memory_space=pltpu.VMEM)] * 2,
        out_specs=[pl.BlockSpec(memory_space=pltpu.VMEM)] * 2,
        scratch_shapes=[pltpu.VMEM((-(-B * B // LANES), B, LANES), jnp.float32)],
        compiler_params=pltpu.CompilerParams(vmem_limit_bytes=16 * MIB),
        name="pack",
    )(orbitals, table)


def finish_body(count, slots, field_ref, near_ref, far_ref, row_ref, out_ref, total, stage):
    lane = lanes_of((B, LANES))
    for n in range(count):
        for t in range(TILES):
            total[n, t] = field_ref[n, t] + far_ref[n, t].astype(jnp.float32)

    def add(j, carry):
        row = row_ref[j]
        for t in range(TILES):
            total[row, t] += near_ref[j, t].astype(jnp.float32)
        return carry

    lax.fori_loop(0, slots, add, 0)
    for n in range(count):
        flats = {}
        for b, flat, shift in overlaps():
            first = max(b * B, flat * LANES) - flat * LANES
            last = min(b * B + B, flat * LANES + LANES) - flat * LANES
            moved = pltpu.roll(total[n, b % TILES], shift % LANES, axis=1)
            keep = (lane >= first) & (lane < last)
            before = flats.get(flat)
            flats[flat] = moved if before is None else jnp.where(keep, moved, before)
        for flat, value in flats.items():
            for p in range(PLANES):
                stage[flat, pl.ds(p, SUB, stride=PLANES), :] = value[p * SUB : p * SUB + SUB]
            width = min(LANES, B * B - flat * LANES)
            out_ref[n, :, flat * LANES : flat * LANES + width] = stage[flat, :, :width]


def finish(field, near, far, rows):
    count, slots = field.shape[0], near.shape[0]
    vmem = pl.BlockSpec(memory_space=pltpu.VMEM)
    return pl.pallas_call(
        functools.partial(finish_body, count, slots),
        out_shape=jax.ShapeDtypeStruct((count, B, B * B), jnp.float32),
        in_specs=[vmem, vmem, vmem, pl.BlockSpec(memory_space=pltpu.SMEM)],
        out_specs=vmem,
        scratch_shapes=[
            pltpu.VMEM((count, TILES, B, LANES), jnp.float32),
            pltpu.VMEM((-(-B * B // LANES), B, LANES), jnp.float32),
        ],
        compiler_params=pltpu.CompilerParams(vmem_limit_bytes=16 * MIB),
        name="finish",
    )(field, near, far, rows)


def geometry(offset_ref, left, right, grid_cells):
    shift, live = [], jnp.int32(1)
    for axis in range(3):
        gap = offset_ref[3 * right + axis] - offset_ref[3 * left + axis] + grid_cells // 2
        gap = jnp.where(gap < 0, gap + grid_cells, gap)
        gap = jnp.where(gap >= grid_cells, gap - grid_cells, gap) - grid_cells // 2
        live = jnp.where((gap > HALF) | (gap < -HALF), 0, live)
        shift.append(gap)
    return shift, live


def lane_group(lane):
    return sum(jnp.where(lane >= B * (i + 1), 1, 0) for i in range(GROUPS))


def wrapped(shift, size):
    from_zero = B * size - shift
    quotient = (from_zero * (2**16 // size + 1)) >> 16
    start, turn = from_zero - size * quotient, quotient - B
    pairs = []
    for i in range(size):
        over = jnp.where(start + i >= size, 1, 0)
        pairs.append((start + i - size * over, turn + over))
    return pairs


def put_padded(pad, t, p, value):
    start = (t * PLANES + p) * CELL + SUB
    pad[start : start + SUB, :] = value


def displaced(pad, shift):
    lane = lanes_of((SUB, LANES))
    group = lane_group(lane)
    source_col = lane - group * B - shift[2]
    col_ok = (source_col >= 0) & (source_col < B) & (lane < USED)
    source_row = jnp.where(col_ok, TILES * group - shift[1], -2 * B)
    rows = [p * CELL + SUB + turn for p, turn in wrapped(shift[0], PLANES)]
    for t, (source, turn) in enumerate(wrapped(shift[1], TILES)):
        keep = (source_row + t >= 0) & (source_row + t < B)
        if t >= B - TILES * (GROUPS - 1):
            keep = keep & (lane < USED - B)
        amount = (shift[2] - B * turn + 2 * LANES) & (LANES - 1)
        tile = []
        for p in range(PLANES):
            block = pad[pl.ds(source * (PLANES * CELL) + rows[p], SUB), :]
            tile.append(jnp.where(keep, pltpu.roll(block, amount, axis=1), 0.0))
        yield t, tile


def tree_sum(values):
    while len(values) > 1:
        paired = [a + b for a, b in zip(values[::2], values[1::2])]
        values = paired + ([values[-1]] if len(values) % 2 else [])
    return values[0]


def blocks(value):
    return [value[p * SUB : p * SUB + SUB] for p in range(PLANES)]


def cell(t, p):
    start = (t * PLANES + p) * SUB
    return slice(start, start + SUB)


def make_operator():
    lane = lanes_of((SUB, LANES))
    sublane = lax.broadcasted_iota(jnp.int32, (SUB, LANES), 0)
    column = lane - B * lane_group(lane)
    has_before = (column > 0) & (lane < USED)
    has_after = (column < B - 1) & (lane < USED)
    not_first = lane >= B
    not_last = lane < USED - B
    has_above = sublane > 0
    has_below = sublane < SUB - 1

    def operator(t, before, here, after):
        if t == 0:
            before = [jnp.where(not_first, pltpu.roll(v, B, axis=1), 0.0) for v in before]
        if t == TILES - 1:
            after = [jnp.where(not_last, pltpu.roll(v, LANES - B, axis=1), 0.0) for v in after]
        result = []
        for p in range(PLANES):
            if p == 0:
                above = jnp.where(has_above, pltpu.roll(here[PLANES - 1], 1, axis=0), 0.0)
            else:
                above = here[p - 1]
            if p == PLANES - 1:
                below = jnp.where(has_below, pltpu.roll(here[0], SUB - 1, axis=0), 0.0)
            else:
                below = here[p + 1]
            prior = jnp.where(has_before, pltpu.roll(here[p], 1, axis=1), 0.0)
            following = jnp.where(has_after, pltpu.roll(here[p], LANES - 1, axis=1), 0.0)
            around = (above + below) + (before[p] + after[p]) + (prior + following)
            value = (6.0 + SCREEN) * here[p] - around
            if t == B - TILES * (GROUPS - 1):
                value = jnp.where(not_last, value, 0.0)
            result.append(value)
        return result

    return operator


def side_by_side(used, body):
    def pair(i, carry):
        for _ in zip(body(2 * i, 0), body(2 * i + 1, 1)):
            pass
        return carry

    lax.fori_loop(0, used >> 1, pair, 0)

    @pl.when((used & 1) == 1)
    def _():
        for _ in body(used - 1, 0):
            pass


def put_sum(sums, kind, m, value):
    sums[kind, pl.ds(m, 1), :] = jnp.sum(value, axis=0, keepdims=True)


def solve(used, directions, residuals, images, sums, steps, ratios):
    operator = make_operator()

    for k in range(ITERS):
        last = k == ITERS - 1
        source = directions[0] if k == 1 else residuals[k % 2]
        target = residuals[(k + 1) % 2]

        def stencil(m, side, k=k, last=last, source=source, target=target):
            squares = []
            if k > 0:
                step = jnp.broadcast_to(steps[k - 1, pl.ds(m, 1), :], (SUB, LANES))
                ratio = jnp.broadcast_to(ratios[pl.ds(m, 1), :], (SUB, LANES))

            def stored(t):
                return [directions[k][m, cell(t, p), :] for p in range(PLANES)]

            def fetch(t):
                if k == 0:
                    return stored(t)
                values, parts = [], []
                for p in range(PLANES):
                    left = source[m, cell(t, p), :] - step * images[(k - 1) % 2][m, cell(t, p), :]
                    if not last:
                        target[m, cell(t, p), :] = left
                    parts.append(left * left)
                    value = left + ratio * directions[k - 1][m, cell(t, p), :]
                    directions[k][m, cell(t, p), :] = value
                    values.append(value)
                squares.append(tree_sum(parts))
                if len(squares) == 2:
                    squares[:] = [squares[0] + squares[1]]
                return values

            before, here = fetch(TILES - 1), fetch(0)
            total = spread = None
            for t in range(TILES):
                after = fetch(t + 1) if t < TILES - 2 else stored((t + 1) % TILES)
                applied = operator(t, before, here, after)
                if not last:
                    for p in range(PLANES):
                        images[k % 2][m, cell(t, p), :] = applied[p]
                    part = tree_sum([x * x for x in applied])
                    spread = part if spread is None else spread + part
                part = tree_sum([x * y for x, y in zip(here, applied)])
                total = part if total is None else total + part
                before, here = here, after
                yield
            put_sum(sums, 1, m, total)
            if not last:
                put_sum(sums, 2, m, spread)
            if k > 0:
                put_sum(sums, 0, m, squares[0])
            yield

        side_by_side(used, stencil)
        norm, product, square = (
            jnp.broadcast_to(jnp.sum(sums[kind], axis=1, keepdims=True), sums.shape[1:])
            for kind in range(3)
        )
        step = norm / product
        steps[k] = step
        if not last:
            ratios[...] = jnp.maximum(step * step * square - norm, 0.0) / norm


def run_slots(used, nears, fars, shift_of, left_at, right_at, near_to, far_to, scratch):
    pads, shifted, sums, steps, ratios, *boxes = scratch
    residuals, images, directions = boxes[:2], boxes[2:4], boxes[4:]

    def load(m, side):
        pad = pads.at[side]
        for t in range(TILES):
            for p, block in enumerate(blocks(right_at(m, t))):
                put_padded(pad, t, p, block)
            yield
        total = None
        for t, moved in displaced(pad, shift_of(m)):
            squares = []
            for p, left in enumerate(blocks(left_at(m, t))):
                shifted[m, cell(t, p), :] = moved[p]
                density = moved[p] * left
                directions[0][m, cell(t, p), :] = density
                squares.append(density * density)
            part = tree_sum(squares)
            total = part if total is None else total + part
            yield
        put_sum(sums, 0, m, total)
        yield

    side_by_side(used, load)
    solve(used, directions, residuals, images, sums, steps, ratios)

    def potential(m, t):
        weights = [steps[k, pl.ds(m, 1), :] for k in range(ITERS)]
        return [
            tree_sum([w * d[m, cell(t, p), :] for w, d in zip(weights, directions)])
            for p in range(PLANES)
        ]

    def unload(near, far):
        def one(m, carry):
            pad = pads.at[0]
            for t in range(TILES):
                solved = potential(m, t)
                if near:
                    near_to(
                        m, t,
                        jnp.concatenate(
                            [v * shifted[m, cell(t, p), :] for p, v in enumerate(solved)], axis=0
                        ),
                    )
                if far:
                    for p, left in enumerate(blocks(left_at(m, t))):
                        put_padded(pad, t, p, solved[p] * left)
            if far:
                for t, moved in displaced(pad, [-s for s in shift_of(m)]):
                    far_to(m, t, jnp.concatenate(moved, axis=0))
            return carry

        return one

    if nears is fars:
        lax.fori_loop(*nears, unload(True, True), 0)
    else:
        lax.fori_loop(*nears, unload(True, False), 0)
        lax.fori_loop(*fars, unload(False, True), 0)


def slot_scratch(batch):
    row = pltpu.VMEM((batch, LANES), jnp.float32)
    box = pltpu.VMEM((batch, CELLS * SUB, LANES), jnp.float32)
    return [
        pltpu.SMEM((batch * FIELDS,), jnp.int32),
        pltpu.VMEM((2, CELLS * CELL + SUB, LANES), jnp.float32),
        box,
        pltpu.VMEM((3, batch, LANES), jnp.float32),
        pltpu.VMEM((ITERS, batch, LANES), jnp.float32),
        row,
    ] + [box] * (4 + ITERS)


def clear(ref):
    for n in range(ref.shape[0]):
        for t in range(TILES):
            ref[n, t] = jnp.zeros((B, LANES), ref.dtype)


def append(listed, used, values):
    for i, value in enumerate(values):
        listed[used * FIELDS + i] = value


def piece_copies(pieces, index, held, slot, sem):
    part = pieces[0].shape[0]
    for h, piece in enumerate(pieces):

        @pl.when((index >= h * part) & (index < (h + 1) * part))
        def _(h=h, piece=piece):
            pltpu.make_async_copy(piece.at[index - h * part], held.at[slot], sem).start()


def wait_box(pieces, held, slot, sem):
    pltpu.make_async_copy(pieces[0].at[0], held.at[slot], sem).wait()


def read_tables(meta, orbs, me, count, index_ref):
    free = LANES - USED
    lines = orbs // free
    bits = count.bit_length() - 1
    row = lax.broadcasted_iota(jnp.int32, (B, LANES), 0)
    lane = lanes_of((B, LANES)) - USED

    def digits(value, length):
        value = value.astype(jnp.int32)
        for _ in range(length):
            rest = value >> bits if count == 1 << bits else lax.div(value, count)
            yield value - rest * count
            value = rest

    weight = jnp.zeros((B, LANES), jnp.float32)
    for place, kind in enumerate((0, 2, 3)):
        chosen = (row - kind * lines) * free + lane == me
        chosen = chosen & (lane >= 0)
        weight = jnp.where(chosen, float(count**place), weight)
    for k in range(orbs):
        source = jnp.bitwise_xor(me, k)
        total = jnp.sum(meta[k].astype(jnp.float32) * weight)
        for kind, value in enumerate(digits(total, 3)):
            index_ref[kind * orbs + source] = value
    weight = jnp.zeros((B, LANES), jnp.float32)
    for place in range(free):
        weight = jnp.where(lane == place, float(count**place), weight)
    arrived = meta[orbs].astype(jnp.float32) * weight
    for line in range(lines):
        total = jnp.sum(jnp.where(row == lines + line, arrived, 0.0))
        for place, value in enumerate(digits(total, free)):
            index_ref[3 * orbs + line * free + place] = value


def forward_body(orbs, count, grid_cells, where_ref, offset_ref, *refs):
    pieces = [refs[2 * k : 2 * k + 2] for k in range(orbs)]
    incoming = refs[2 * orbs : 2 * orbs + 2]
    near_ref, far_ref, index_ref, meta, held, far_sum, meta_sem, box_sem, listed = refs[
        2 * orbs + 2 : 2 * orbs + 11
    ]
    scratch = refs[2 * orbs + 11 :]
    batch = listed.shape[0] // FIELDS
    part = count // 2
    me = where_ref[2]
    first_left, first_right = where_ref[0], where_ref[1]

    tables = [
        pltpu.make_async_copy(source[0].at[0, 0], meta.at[k], meta_sem.at[k])
        for k, source in enumerate(pieces + [incoming])
    ]
    for copy in tables:
        copy.start()
    rights = [
        pltpu.make_async_copy(
            incoming[n // part].at[n % part], held.at[orbs + n], box_sem.at[orbs + n]
        )
        for n in range(count)
    ]
    for copy in rights:
        copy.start()
    scratch[0][...] = jnp.zeros(scratch[0].shape, jnp.float32)
    clear(far_sum)
    for copy in tables:
        copy.wait()
    read_tables(meta, orbs, me, count, index_ref)
    for k in range(orbs):
        source = jnp.bitwise_xor(me, k)
        piece_copies(pieces[k], index_ref[2 * orbs + source], held, source, box_sem.at[k])
    for k in range(orbs):
        wait_box(pieces[k], held, jnp.bitwise_xor(me, k), box_sem.at[k])
    for copy in rights:
        copy.wait()

    def run(i, carry):
        def gather(j, used):
            slot = i * batch + j
            left, right = slot * count + index_ref[2 * orbs + slot], index_ref[3 * orbs + slot]
            shift, live = geometry(
                offset_ref, first_left + left, first_right + right, grid_cells
            )

            @pl.when(live == 1)
            def _():
                append(listed, used, [slot, orbs + right, *shift])

            @pl.when(live == 0)
            def _():
                for t in range(TILES):
                    near_ref[slot, t] = jnp.zeros((B, LANES), near_ref.dtype)

            return used + live

        used = lax.fori_loop(0, batch, gather, jnp.int32(0))

        def shift_of(m):
            return [listed[m * FIELDS + 2 + axis] for axis in range(3)]

        def near_to(m, t, value):
            near_ref[listed[m * FIELDS], t] = value.astype(near_ref.dtype)

        def far_to(m, t, value):
            far_sum[listed[m * FIELDS + 1] - orbs, t] += value

        every = (0, used)
        run_slots(
            used, every, every, shift_of,
            lambda m, t: held[listed[m * FIELDS], t].astype(jnp.float32),
            lambda m, t: held[listed[m * FIELDS + 1], t].astype(jnp.float32),
            near_to, far_to, scratch,
        )
        return carry

    lax.fori_loop(0, orbs // batch, run, 0)
    for n in range(count):
        for t in range(TILES):
            far_ref[n, t] = far_sum[n, t].astype(far_ref.dtype)


def forward_pairs(where, offsets, pieces, incoming, count, grid_cells):
    orbs = len(pieces)
    vmem, smem, left = (pl.BlockSpec(memory_space=m) for m in (pltpu.VMEM, pltpu.SMEM, pl.ANY))
    shape = (TILES, B, LANES)
    return pl.pallas_call(
        functools.partial(forward_body, orbs, count, grid_cells),
        out_shape=(
            jax.ShapeDtypeStruct((orbs,) + shape, jnp.bfloat16),
            jax.ShapeDtypeStruct((count,) + shape, jnp.bfloat16),
            jax.ShapeDtypeStruct((4 * orbs,), jnp.int32),
        ),
        in_specs=[smem] * 2 + [left] * (2 * orbs + 2),
        out_specs=(vmem, vmem, smem),
        scratch_shapes=[
            pltpu.VMEM((orbs + 1, B, LANES), jnp.bfloat16),
            pltpu.VMEM((orbs + count,) + shape, jnp.bfloat16),
            pltpu.VMEM((count,) + shape, jnp.float32),
            pltpu.SemaphoreType.DMA((orbs + 1,)),
            pltpu.SemaphoreType.DMA((orbs + count,)),
        ] + slot_scratch(8),
        compiler_params=pltpu.CompilerParams(vmem_limit_bytes=32 * MIB),
        name="forward_pairs",
    )(where, offsets, *[half for piece in pieces for half in piece], *incoming)


def group_body(orbs, count, grid_cells, where_ref, offset_ref, mine_ref, sent_ref, index_ref, *refs):
    pieces = [refs[2 * k : 2 * k + 2] for k in range(orbs)]
    field, held, sem, listed = refs[2 * orbs : 2 * orbs + 4]
    scratch = refs[2 * orbs + 4 :]
    half = listed.shape[0] // FIELDS // 2
    part = count // 2
    first, me = where_ref[0], where_ref[2]
    mine = me * count
    own = 2 * orbs

    for k in range(orbs):
        source = jnp.bitwise_xor(me, k)
        piece_copies(pieces[k], index_ref[source], held, source, sem.at[k])
        piece_copies(pieces[k], index_ref[orbs + source], held, orbs + source, sem.at[orbs + k])
    owned = [
        pltpu.make_async_copy(pieces[0][n // part].at[n % part], held.at[own + n], sem.at[own + n])
        for n in range(count)
    ]
    for copy in owned:
        copy.start()
    scratch[0][...] = jnp.zeros(scratch[0].shape, jnp.float32)
    clear(field)
    for k in range(orbs):
        source = jnp.bitwise_xor(me, k)
        wait_box(pieces[k], held, source, sem.at[k])
        wait_box(pieces[k], held, orbs + source, sem.at[orbs + k])
    for copy in owned:
        copy.wait()

    def run(i, carry):
        def listing(near):
            def gather(j, used):
                slot = i * half + ((me + 1 + j) & (half - 1))
                if near:
                    left, right = mine + mine_ref[slot], slot * count + index_ref[slot]
                    boxes = [own + mine_ref[slot], slot]
                else:
                    left, right = slot * count + index_ref[orbs + slot], mine + sent_ref[slot]
                    boxes = [orbs + slot, own + sent_ref[slot]]
                shift, live = geometry(offset_ref, first + left, first + right, grid_cells)
                if not near:
                    live = jnp.where(slot == me, 0, live)
                else:
                    boxes[1] = jnp.where(slot == me, own + index_ref[slot], boxes[1])

                @pl.when(live == 1)
                def _():
                    append(listed, used, boxes + [*shift])

                return used + live

            return gather

        near_count = lax.fori_loop(0, half, listing(True), jnp.int32(0))
        used = lax.fori_loop(0, half, listing(False), near_count)
        left, right = mine + mine_ref[me], mine + index_ref[me]
        inside = geometry(offset_ref, first + left, first + right, grid_cells)[1]
        inside = jnp.where((me >= i * half) & (me < (i + 1) * half), inside, 0)

        def shift_of(m):
            return [listed[m * FIELDS + 2 + axis] for axis in range(3)]

        def near_to(m, t, value):
            field[listed[m * FIELDS] - own, t] += value

        def far_to(m, t, value):
            field[listed[m * FIELDS + 1] - own, t] += value

        run_slots(
            used, (0, near_count), (near_count - inside, used), shift_of,
            lambda m, t: held[listed[m * FIELDS], t].astype(jnp.float32),
            lambda m, t: held[listed[m * FIELDS + 1], t].astype(jnp.float32),
            near_to, far_to, scratch,
        )
        return carry

    lax.fori_loop(0, orbs // half, run, 0)


def group_pairs(where, offsets, mine, sent, index, pieces, count, grid_cells):
    orbs = len(pieces)
    vmem, smem, left = (pl.BlockSpec(memory_space=m) for m in (pltpu.VMEM, pltpu.SMEM, pl.ANY))
    shape = (TILES, B, LANES)
    return pl.pallas_call(
        functools.partial(group_body, orbs, count, grid_cells),
        out_shape=jax.ShapeDtypeStruct((count,) + shape, jnp.float32),
        in_specs=[smem] * 5 + [left] * (2 * orbs),
        out_specs=vmem,
        scratch_shapes=[
            pltpu.VMEM((2 * orbs + count,) + shape, jnp.bfloat16),
            pltpu.SemaphoreType.DMA((2 * orbs + count,)),
        ] + slot_scratch(16),
        compiler_params=pltpu.CompilerParams(vmem_limit_bytes=52 * MIB),
        name="group_pairs",
    )(where, offsets, mine, sent, index, *[half for piece in pieces for half in piece])


def along_space(block, distance):
    size = lax.axis_size("space")
    return lax.ppermute(block, "space", [((i - distance) % size, i) for i in range(size)])


def group_exchange(packed, orbs):
    bits = [1 << i for i in range(orbs.bit_length() - 1)]
    orders = (bits[1:] + bits[:1], bits[:0:-1] + bits[:1])
    halves = []
    for block, order in zip(packed, orders):
        known = {0: block}
        for bit in order:
            route = [(i, i ^ bit) for i in range(orbs)]
            for k in list(known):
                known[k ^ bit] = lax.ppermute(known[k], "orb", route)
        halves.append(known)
    return [[known[k] for known in halves] for k in range(orbs)]


def per_device(orbitals, box_offset, send_index, pair_left):
    count = orbitals.shape[0]
    spaces, orbs = lax.axis_size("space"), lax.axis_size("orb")
    grid_cells = spaces * HALF
    space, orb = lax.axis_index("space"), lax.axis_index("orb")
    group_first = space * orbs * count
    offsets = box_offset.reshape(-1)

    free = LANES - USED
    entries = jnp.concatenate([send_index[0].reshape(-1), pair_left[0].reshape(-1)])
    lines = 4 * orbs // free
    table = jnp.pad(
        entries.astype(jnp.float32).reshape(lines, free), ((0, B - lines), (USED, 0))
    )
    packed = pack(orbitals, table)

    pieces = group_exchange(packed, orbs)
    *held_back, pieces[2][0] = lax.optimization_barrier((*packed, pieces[2][0]))
    incoming = [along_space(half, -1) for half in held_back]
    where = jnp.stack([group_first, ((space + 1) % spaces * orbs + orb) * count, orb])
    near, far, index = forward_pairs(where, offsets, pieces, incoming, count, grid_cells)
    near = lax.all_to_all(near, "orb", split_axis=0, concat_axis=0, tiled=True)
    far = along_space(far, 1)
    field = group_pairs(
        where, offsets, pair_left[0, 0], send_index[0, 0], index, pieces, count, grid_cells
    )
    return finish(field, near, far, pair_left[0, 1])


def solution(mesh):
    split = P(("space", "orb"), None, None)
    return jax.shard_map(
        per_device, mesh=mesh, in_specs=(split, P(), split, split), out_specs=split,
        check_vma=False,
    )
```

```python
import functools

import jax
import jax.numpy as jnp
from jax import lax
from jax.experimental import pallas as pl
from jax.experimental.pallas import tpu as pltpu
from jax.sharding import PartitionSpec as P

B = 40
ITERS = 4
SCREEN = 0.25

GROUPS = 3
TILES = 14
LANES = 128
USED = GROUPS * B
SUB = 8
PLANES = B // SUB
CELLS = TILES * PLANES
CELL = 2 * SUB
HALF = B // 2
VMEM_BYTES = 52 * 2**20
FIELDS = 8


def lanes_of(shape):
    return lax.broadcasted_iota(jnp.int32, shape, len(shape) - 1)


def overlaps():
    pieces = []
    for b in range(B):
        group = b // TILES
        for flat in range(b * B // LANES, (b * B + B - 1) // LANES + 1):
            pieces.append((b, flat, b * B - flat * LANES - group * B))
    return pieces


def pack_body(box_ref, table_ref, first_ref, second_ref, stage):
    count = box_ref.shape[0]
    lane = lanes_of((B, LANES))
    for n in range(count):
        tiles = [jnp.zeros((B, LANES), jnp.float32) for _ in range(TILES)]
        loaded = {}
        for b, flat, shift in overlaps():
            if flat not in loaded:
                width = min(LANES, B * B - flat * LANES)
                part = box_ref[n, :, flat * LANES : flat * LANES + width].astype(jnp.float32)
                if width < LANES:
                    part = jnp.concatenate(
                        [part, jnp.zeros((B, LANES - width), jnp.float32)], axis=1
                    )
                stage[flat] = part
                loaded[flat] = jnp.concatenate(
                    [stage[flat, pl.ds(p, SUB, stride=PLANES), :] for p in range(PLANES)], axis=0
                )
            first = max(b * B, flat * LANES) - b * B + (b // TILES) * B
            last = min(b * B + B, flat * LANES + LANES) - b * B + (b // TILES) * B
            moved = pltpu.roll(loaded[flat], (-shift) % LANES, axis=1)
            keep = (lane >= first) & (lane < last)
            tiles[b % TILES] = jnp.where(keep, moved, tiles[b % TILES])
        if n == 0:
            tiles[0] = tiles[0] + table_ref[...]
        out_ref = first_ref if n < count // 2 else second_ref
        for t in range(TILES):
            out_ref[n % (count // 2), t] = tiles[t].astype(out_ref.dtype)


def pack(orbitals, table):
    count = orbitals.shape[0]
    return pl.pallas_call(
        pack_body,
        out_shape=[jax.ShapeDtypeStruct((count // 2, TILES, B, LANES), jnp.bfloat16)] * 2,
        in_specs=[pl.BlockSpec(memory_space=pltpu.VMEM)] * 2,
        out_specs=[pl.BlockSpec(memory_space=pltpu.VMEM)] * 2,
        scratch_shapes=[pltpu.VMEM((-(-B * B // LANES), B, LANES), jnp.float32)],
        compiler_params=pltpu.CompilerParams(vmem_limit_bytes=VMEM_BYTES),
        name="pack",
    )(orbitals, table)


def finish_body(count, slots, field_ref, near_ref, far_ref, row_ref, out_ref, total, stage):
    lane = lanes_of((B, LANES))
    for n in range(count):
        for t in range(TILES):
            total[n, t] = field_ref[n, t] + far_ref[n, t].astype(jnp.float32)

    def add(j, carry):
        row = row_ref[j]
        for t in range(TILES):
            total[row, t] += near_ref[j, t].astype(jnp.float32)
        return carry

    lax.fori_loop(0, slots, add, 0)
    for n in range(count):
        flats = {}
        for b, flat, shift in overlaps():
            first = max(b * B, flat * LANES) - flat * LANES
            last = min(b * B + B, flat * LANES + LANES) - flat * LANES
            moved = pltpu.roll(total[n, b % TILES], shift % LANES, axis=1)
            keep = (lane >= first) & (lane < last)
            before = flats.get(flat)
            flats[flat] = moved if before is None else jnp.where(keep, moved, before)
        for flat, value in flats.items():
            for p in range(PLANES):
                stage[flat, pl.ds(p, SUB, stride=PLANES), :] = value[p * SUB : p * SUB + SUB]
            width = min(LANES, B * B - flat * LANES)
            out_ref[n, :, flat * LANES : flat * LANES + width] = stage[flat, :, :width]


def finish(field, near, far, rows):
    count, slots = field.shape[0], near.shape[0]
    vmem = pl.BlockSpec(memory_space=pltpu.VMEM)
    return pl.pallas_call(
        functools.partial(finish_body, count, slots),
        out_shape=jax.ShapeDtypeStruct((count, B, B * B), jnp.float32),
        in_specs=[vmem, vmem, vmem, pl.BlockSpec(memory_space=pltpu.SMEM)],
        out_specs=vmem,
        scratch_shapes=[
            pltpu.VMEM((count, TILES, B, LANES), jnp.float32),
            pltpu.VMEM((-(-B * B // LANES), B, LANES), jnp.float32),
        ],
        compiler_params=pltpu.CompilerParams(vmem_limit_bytes=VMEM_BYTES),
        name="finish",
    )(field, near, far, rows)


def geometry(offset_ref, left, right, grid_cells):
    shift, live = [], jnp.int32(1)
    for axis in range(3):
        gap = offset_ref[3 * right + axis] - offset_ref[3 * left + axis] + grid_cells // 2
        gap = jnp.where(gap < 0, gap + grid_cells, gap)
        gap = jnp.where(gap >= grid_cells, gap - grid_cells, gap) - grid_cells // 2
        live = jnp.where((gap > HALF) | (gap < -HALF), 0, live)
        shift.append(gap)
    return shift, live


def lane_group(lane):
    return sum(jnp.where(lane >= B * (i + 1), 1, 0) for i in range(GROUPS))


def wrapped(shift, size):
    from_zero = B * size - shift
    quotient = (from_zero * (2**16 // size + 1)) >> 16
    start, turn = from_zero - size * quotient, quotient - B
    pairs = []
    for i in range(size):
        over = jnp.where(start + i >= size, 1, 0)
        pairs.append((start + i - size * over, turn + over))
    return pairs


def put_padded(pad, t, p, value):
    start = (t * PLANES + p) * CELL + SUB
    pad[start : start + SUB, :] = value


def displaced(pad, shift):
    lane = lanes_of((SUB, LANES))
    group = lane_group(lane)
    source_col = lane - group * B - shift[2]
    col_ok = (source_col >= 0) & (source_col < B) & (lane < USED)
    source_row = jnp.where(col_ok, TILES * group - shift[1], -2 * B)
    rows = [p * CELL + SUB + turn for p, turn in wrapped(shift[0], PLANES)]
    for t, (source, turn) in enumerate(wrapped(shift[1], TILES)):
        keep = (source_row + t >= 0) & (source_row + t < B)
        if t >= B - TILES * (GROUPS - 1):
            keep = keep & (lane < USED - B)
        amount = (shift[2] - B * turn + 2 * LANES) & (LANES - 1)
        tile = []
        for p in range(PLANES):
            block = pad[pl.ds(source * (PLANES * CELL) + rows[p], SUB), :]
            tile.append(jnp.where(keep, pltpu.roll(block, amount, axis=1), 0.0))
        yield t, tile


def tree_sum(values):
    while len(values) > 1:
        paired = [a + b for a, b in zip(values[::2], values[1::2])]
        values = paired + ([values[-1]] if len(values) % 2 else [])
    return values[0]


def blocks(value):
    return [value[p * SUB : p * SUB + SUB] for p in range(PLANES)]


def cell(t, p):
    start = (t * PLANES + p) * SUB
    return slice(start, start + SUB)


def make_operator():
    lane = lanes_of((SUB, LANES))
    sublane = lax.broadcasted_iota(jnp.int32, (SUB, LANES), 0)
    column = lane - B * lane_group(lane)
    has_before = (column > 0) & (lane < USED)
    has_after = (column < B - 1) & (lane < USED)
    not_first = lane >= B
    not_last = lane < USED - B
    has_above = sublane > 0
    has_below = sublane < SUB - 1

    def operator(t, before, here, after):
        if t == 0:
            before = [jnp.where(not_first, pltpu.roll(v, B, axis=1), 0.0) for v in before]
        if t == TILES - 1:
            after = [jnp.where(not_last, pltpu.roll(v, LANES - B, axis=1), 0.0) for v in after]
        result = []
        for p in range(PLANES):
            if p == 0:
                above = jnp.where(has_above, pltpu.roll(here[PLANES - 1], 1, axis=0), 0.0)
            else:
                above = here[p - 1]
            if p == PLANES - 1:
                below = jnp.where(has_below, pltpu.roll(here[0], SUB - 1, axis=0), 0.0)
            else:
                below = here[p + 1]
            prior = jnp.where(has_before, pltpu.roll(here[p], 1, axis=1), 0.0)
            following = jnp.where(has_after, pltpu.roll(here[p], LANES - 1, axis=1), 0.0)
            around = (above + below) + (before[p] + after[p]) + (prior + following)
            value = (6.0 + SCREEN) * here[p] - around
            if t == B - TILES * (GROUPS - 1):
                value = jnp.where(not_last, value, 0.0)
            result.append(value)
        return result

    return operator


def side_by_side(first, last, body):
    def pair(i, carry):
        for _ in zip(body(first + 2 * i, 0), body(first + 2 * i + 1, 1)):
            pass
        return carry

    lax.fori_loop(0, (last - first) >> 1, pair, 0)

    @pl.when(((last - first) & 1) == 1)
    def _():
        for _ in body(last - 1, 0):
            pass


def put_sum(sums, kind, m, value):
    sums[kind, pl.ds(m, 1), :] = jnp.sum(value, axis=0, keepdims=True)


def solve(used, directions, residuals, images, sums, steps, ratios):
    operator = make_operator()

    for k in range(ITERS):
        last = k == ITERS - 1
        source = directions[0] if k == 1 else residuals[k % 2]
        target = residuals[(k + 1) % 2]

        def stencil(m, side, k=k, last=last, source=source, target=target):
            squares = []
            if k > 0:
                step = jnp.broadcast_to(steps[k - 1, pl.ds(m, 1), :], (SUB, LANES))
                ratio = jnp.broadcast_to(ratios[pl.ds(m, 1), :], (SUB, LANES))

            def stored(t):
                return [directions[k][m, cell(t, p), :] for p in range(PLANES)]

            def fetch(t):
                if k == 0:
                    return stored(t)
                values, parts = [], []
                for p in range(PLANES):
                    left = source[m, cell(t, p), :] - step * images[(k - 1) % 2][m, cell(t, p), :]
                    if not last:
                        target[m, cell(t, p), :] = left
                    parts.append(left * left)
                    value = left + ratio * directions[k - 1][m, cell(t, p), :]
                    directions[k][m, cell(t, p), :] = value
                    values.append(value)
                squares.append(tree_sum(parts))
                if len(squares) == 2:
                    squares[:] = [squares[0] + squares[1]]
                return values

            before, here = fetch(TILES - 1), fetch(0)
            total = spread = None
            for t in range(TILES):
                after = fetch(t + 1) if t < TILES - 2 else stored((t + 1) % TILES)
                applied = operator(t, before, here, after)
                if not last:
                    for p in range(PLANES):
                        images[k % 2][m, cell(t, p), :] = applied[p]
                    part = tree_sum([x * x for x in applied])
                    spread = part if spread is None else spread + part
                part = tree_sum([x * y for x, y in zip(here, applied)])
                total = part if total is None else total + part
                before, here = here, after
                yield
            put_sum(sums, 1, m, total)
            if not last:
                put_sum(sums, 2, m, spread)
            if k > 0:
                put_sum(sums, 0, m, squares[0])
            yield

        side_by_side(0, used, stencil)
        norm, product, square = (
            jnp.broadcast_to(jnp.sum(sums[kind], axis=1, keepdims=True), sums.shape[1:])
            for kind in range(3)
        )
        step = norm / product
        steps[k] = step
        if not last:
            ratios[...] = jnp.maximum(step * step * square - norm, 0.0) / norm


def run_slots(used, nears, fars, shift_of, left_of, right_of, near_to, far_to, held, scratch):
    pads, shifted, sums, steps, ratios, *boxes = scratch
    residuals, images, directions = boxes[:2], boxes[2:4], boxes[4:]

    def box(row, t):
        return blocks(held[row, t].astype(jnp.float32))

    def load(m, side):
        pad = pads.at[side]
        left, right = left_of(m), right_of(m)
        for t in range(TILES):
            for p, block in enumerate(box(right, t)):
                put_padded(pad, t, p, block)
            yield
        total = None
        for t, moved in displaced(pad, shift_of(m)):
            squares = []
            for p, value in enumerate(box(left, t)):
                shifted[m, cell(t, p), :] = moved[p]
                density = moved[p] * value
                directions[0][m, cell(t, p), :] = density
                squares.append(density * density)
            part = tree_sum(squares)
            total = part if total is None else total + part
            yield
        put_sum(sums, 0, m, total)
        yield

    side_by_side(0, used, load)
    solve(used, directions, residuals, images, sums, steps, ratios)

    def unload(near, far):
        def one(m, side):
            pad = pads.at[side]
            left = left_of(m)
            weights = [
                jnp.broadcast_to(steps[k, pl.ds(m, 1), :], (SUB, LANES)) for k in range(ITERS)
            ]
            put_near = near_to(m) if near else None
            put_far = far_to(m) if far else None
            for t in range(TILES):
                solved = [
                    tree_sum([w * d[m, cell(t, p), :] for w, d in zip(weights, directions)])
                    for p in range(PLANES)
                ]
                if near:
                    terms = [v * shifted[m, cell(t, p), :] for p, v in enumerate(solved)]
                    put_near(t, jnp.concatenate(terms, axis=0))
                if far:
                    for p, value in enumerate(box(left, t)):
                        put_padded(pad, t, p, solved[p] * value)
                yield
            if far:
                for t, moved in displaced(pad, [-s for s in shift_of(m)]):
                    put_far(t, jnp.concatenate(moved, axis=0))
                    yield

        return one

    if nears is fars:
        side_by_side(*nears, unload(True, True))
    else:
        side_by_side(*nears, unload(True, False))
        side_by_side(*fars, unload(False, True))


def slot_scratch(batch):
    row = pltpu.VMEM((batch, LANES), jnp.float32)
    box = pltpu.VMEM((batch, CELLS * SUB, LANES), jnp.float32)
    return [
        pltpu.SMEM((batch * FIELDS,), jnp.int32),
        pltpu.VMEM((2, CELLS * CELL + SUB, LANES), jnp.float32),
        box,
        pltpu.VMEM((3, batch, LANES), jnp.float32),
        pltpu.VMEM((ITERS, batch, LANES), jnp.float32),
        row,
    ] + [box] * (4 + ITERS)


def clear(ref):
    for n in range(ref.shape[0]):
        for t in range(TILES):
            ref[n, t] = jnp.zeros((B, LANES), ref.dtype)


def append(listed, used, values):
    for i, value in enumerate(values):
        listed[used * FIELDS + i] = value


def adding(ref, row):
    def put(t, value):
        ref[row, t] += value

    return put


def piece_copies(pieces, index, held, slot, sem):
    part = pieces[0].shape[0]
    for h, piece in enumerate(pieces):

        @pl.when((index >= h * part) & (index < (h + 1) * part))
        def _(h=h, piece=piece):
            pltpu.make_async_copy(piece.at[index - h * part], held.at[slot], sem).start()


def wait_box(pieces, held, slot, sem):
    pltpu.make_async_copy(pieces[0].at[0], held.at[slot], sem).wait()


def read_tables(meta, orbs, me, count, index_ref):
    free = LANES - USED
    lines = orbs // free
    bits = count.bit_length() - 1
    row = lax.broadcasted_iota(jnp.int32, (B, LANES), 0)
    lane = lanes_of((B, LANES)) - USED

    def digits(value, length):
        value = value.astype(jnp.int32)
        for _ in range(length):
            rest = value >> bits if count == 1 << bits else lax.div(value, count)
            yield value - rest * count
            value = rest

    weight = jnp.zeros((B, LANES), jnp.float32)
    for place, kind in enumerate((0, 2, 3)):
        chosen = (row - kind * lines) * free + lane == me
        chosen = chosen & (lane >= 0)
        weight = jnp.where(chosen, float(count**place), weight)
    for k in range(orbs):
        source = jnp.bitwise_xor(me, k)
        total = jnp.sum(meta[k].astype(jnp.float32) * weight)
        for kind, value in enumerate(digits(total, 3)):
            index_ref[kind * orbs + source] = value
    weight = jnp.zeros((B, LANES), jnp.float32)
    for place in range(free):
        weight = jnp.where(lane == place, float(count**place), weight)
    arrived = meta[orbs].astype(jnp.float32) * weight
    for line in range(lines):
        total = jnp.sum(jnp.where(row == lines + line, arrived, 0.0))
        for place, value in enumerate(digits(total, free)):
            index_ref[3 * orbs + line * free + place] = value


def forward_body(orbs, count, grid_cells, where_ref, offset_ref, *refs):
    pieces = [refs[2 * k : 2 * k + 2] for k in range(orbs)]
    incoming = refs[2 * orbs : 2 * orbs + 2]
    near_ref, far_ref, index_ref, meta, held, far_sum, meta_sem, box_sem, listed = refs[
        2 * orbs + 2 : 2 * orbs + 11
    ]
    scratch = refs[2 * orbs + 11 :]
    batch = listed.shape[0] // FIELDS
    part = count // 2
    me = where_ref[2]
    first_left, first_right = where_ref[0], where_ref[1]

    tables = [
        pltpu.make_async_copy(source[0].at[0, 0], meta.at[k], meta_sem.at[k])
        for k, source in enumerate(pieces + [incoming])
    ]
    for copy in tables:
        copy.start()
    rights = [
        pltpu.make_async_copy(
            incoming[n // part].at[n % part], held.at[orbs + n], box_sem.at[orbs + n]
        )
        for n in range(count)
    ]
    for copy in rights:
        copy.start()
    scratch[0][...] = jnp.zeros(scratch[0].shape, jnp.float32)
    clear(far_sum)
    for copy in tables:
        copy.wait()
    read_tables(meta, orbs, me, count, index_ref)
    for k in range(orbs):
        source = jnp.bitwise_xor(me, k)
        piece_copies(pieces[k], index_ref[2 * orbs + source], held, source, box_sem.at[k])

    def run(i, carry):
        def gather(j, used):
            slot = i * batch + j
            left, right = slot * count + index_ref[2 * orbs + slot], index_ref[3 * orbs + slot]
            shift, live = geometry(
                offset_ref, first_left + left, first_right + right, grid_cells
            )

            @pl.when(live == 1)
            def _():
                append(listed, used, [slot, orbs + right, *shift])

            @pl.when(live == 0)
            def _():
                for t in range(TILES):
                    near_ref[slot, t] = jnp.zeros((B, LANES), near_ref.dtype)

            return used + live

        used = lax.fori_loop(0, batch, gather, jnp.int32(0))

        @pl.when(i == 0)
        def _():
            for k in range(orbs):
                wait_box(pieces[k], held, jnp.bitwise_xor(me, k), box_sem.at[k])
            for copy in rights:
                copy.wait()

        def shift_of(m):
            return [listed[m * FIELDS + 2 + axis] for axis in range(3)]

        def near_to(m):
            row = listed[m * FIELDS]

            def put(t, value):
                near_ref[row, t] = value.astype(near_ref.dtype)

            return put

        def far_to(m):
            return adding(far_sum, listed[m * FIELDS + 1] - orbs)

        every = (0, used)
        run_slots(
            used, every, every, shift_of,
            lambda m: listed[m * FIELDS], lambda m: listed[m * FIELDS + 1],
            near_to, far_to, held, scratch,
        )
        return carry

    lax.fori_loop(0, orbs // batch, run, 0)
    for n in range(count):
        for t in range(TILES):
            far_ref[n, t] = far_sum[n, t].astype(far_ref.dtype)


def forward_pairs(where, offsets, pieces, incoming, count, grid_cells):
    orbs = len(pieces)
    vmem, smem, left = (pl.BlockSpec(memory_space=m) for m in (pltpu.VMEM, pltpu.SMEM, pl.ANY))
    shape = (TILES, B, LANES)
    return pl.pallas_call(
        functools.partial(forward_body, orbs, count, grid_cells),
        out_shape=(
            jax.ShapeDtypeStruct((orbs,) + shape, jnp.bfloat16),
            jax.ShapeDtypeStruct((count,) + shape, jnp.bfloat16),
            jax.ShapeDtypeStruct((4 * orbs,), jnp.int32),
        ),
        in_specs=[smem] * 2 + [left] * (2 * orbs + 2),
        out_specs=(vmem, vmem, smem),
        scratch_shapes=[
            pltpu.VMEM((orbs + 1, B, LANES), jnp.bfloat16),
            pltpu.VMEM((orbs + count,) + shape, jnp.bfloat16),
            pltpu.VMEM((count,) + shape, jnp.float32),
            pltpu.SemaphoreType.DMA((orbs + 1,)),
            pltpu.SemaphoreType.DMA((orbs + count,)),
        ] + slot_scratch(8),
        compiler_params=pltpu.CompilerParams(vmem_limit_bytes=VMEM_BYTES),
        name="forward_pairs",
    )(where, offsets, *[half for piece in pieces for half in piece], *incoming)


def group_body(orbs, count, grid_cells, where_ref, offset_ref, mine_ref, sent_ref, index_ref, *refs):
    pieces = [refs[2 * k : 2 * k + 2] for k in range(orbs)]
    field, held, sem, listed = refs[2 * orbs : 2 * orbs + 4]
    scratch = refs[2 * orbs + 4 :]
    half = listed.shape[0] // FIELDS // 2
    part = count // 2
    first, me = where_ref[0], where_ref[2]
    mine = me * count
    own = 2 * orbs

    for k in range(orbs):
        source = jnp.bitwise_xor(me, k)
        piece_copies(pieces[k], index_ref[source], held, source, sem.at[k])
        piece_copies(pieces[k], index_ref[orbs + source], held, orbs + source, sem.at[orbs + k])
    owned = [
        pltpu.make_async_copy(pieces[0][n // part].at[n % part], held.at[own + n], sem.at[own + n])
        for n in range(count)
    ]
    for copy in owned:
        copy.start()
    scratch[0][...] = jnp.zeros(scratch[0].shape, jnp.float32)
    clear(field)

    def run(i, carry):
        def listing(near):
            def gather(j, used):
                slot = i * half + ((me + 1 + j) & (half - 1))
                if near:
                    left, right = mine + mine_ref[slot], slot * count + index_ref[slot]
                    boxes = [own + mine_ref[slot], slot]
                else:
                    left, right = slot * count + index_ref[orbs + slot], mine + sent_ref[slot]
                    boxes = [orbs + slot, own + sent_ref[slot]]
                shift, live = geometry(offset_ref, first + left, first + right, grid_cells)
                if not near:
                    live = jnp.where(slot == me, 0, live)
                else:
                    boxes[1] = jnp.where(slot == me, own + index_ref[slot], boxes[1])

                @pl.when(live == 1)
                def _():
                    append(listed, used, boxes + [*shift])

                return used + live

            return gather

        near_count = lax.fori_loop(0, half, listing(True), jnp.int32(0))
        used = lax.fori_loop(0, half, listing(False), near_count)
        left, right = mine + mine_ref[me], mine + index_ref[me]
        inside = geometry(offset_ref, first + left, first + right, grid_cells)[1]
        inside = jnp.where((me >= i * half) & (me < (i + 1) * half), inside, 0)

        @pl.when(i == 0)
        def _():
            for k in range(orbs):
                source = jnp.bitwise_xor(me, k)
                wait_box(pieces[k], held, source, sem.at[k])
                wait_box(pieces[k], held, orbs + source, sem.at[orbs + k])
            for copy in owned:
                copy.wait()

        def shift_of(m):
            return [listed[m * FIELDS + 2 + axis] for axis in range(3)]

        def near_to(m):
            return adding(field, listed[m * FIELDS] - own)

        def far_to(m):
            return adding(field, listed[m * FIELDS + 1] - own)

        run_slots(
            used, (0, near_count), (near_count - inside, used), shift_of,
            lambda m: listed[m * FIELDS], lambda m: listed[m * FIELDS + 1],
            near_to, far_to, held, scratch,
        )
        return carry

    lax.fori_loop(0, orbs // half, run, 0)


def group_pairs(where, offsets, mine, sent, index, pieces, count, grid_cells):
    orbs = len(pieces)
    vmem, smem, left = (pl.BlockSpec(memory_space=m) for m in (pltpu.VMEM, pltpu.SMEM, pl.ANY))
    shape = (TILES, B, LANES)
    return pl.pallas_call(
        functools.partial(group_body, orbs, count, grid_cells),
        out_shape=jax.ShapeDtypeStruct((count,) + shape, jnp.float32),
        in_specs=[smem] * 5 + [left] * (2 * orbs),
        out_specs=vmem,
        scratch_shapes=[
            pltpu.VMEM((2 * orbs + count,) + shape, jnp.bfloat16),
            pltpu.SemaphoreType.DMA((2 * orbs + count,)),
        ] + slot_scratch(16),
        compiler_params=pltpu.CompilerParams(vmem_limit_bytes=VMEM_BYTES),
        name="group_pairs",
    )(where, offsets, mine, sent, index, *[half for piece in pieces for half in piece])


def along_space(block, distance):
    size = lax.axis_size("space")
    return lax.ppermute(block, "space", [((i - distance) % size, i) for i in range(size)])


def group_exchange(packed, orbs):
    bits = [1 << i for i in range(orbs.bit_length() - 1)]
    orders = (bits[1:] + bits[:1], bits[:0:-1] + bits[:1])
    halves = []
    for block, order in zip(packed, orders):
        known = {0: block}
        for bit in order:
            route = [(i, i ^ bit) for i in range(orbs)]
            for k in list(known):
                known[k ^ bit] = lax.ppermute(known[k], "orb", route)
        halves.append(known)
    return [[known[k] for known in halves] for k in range(orbs)]


def per_device(orbitals, box_offset, send_index, pair_left):
    count = orbitals.shape[0]
    spaces, orbs = lax.axis_size("space"), lax.axis_size("orb")
    grid_cells = spaces * HALF
    space, orb = lax.axis_index("space"), lax.axis_index("orb")
    group_first = space * orbs * count
    offsets = box_offset.reshape(-1)

    free = LANES - USED
    entries = jnp.concatenate([send_index[0].reshape(-1), pair_left[0].reshape(-1)])
    lines = 4 * orbs // free
    table = jnp.pad(
        entries.astype(jnp.float32).reshape(lines, free), ((0, B - lines), (USED, 0))
    )
    packed = pack(orbitals, table)

    incoming = [along_space(half, -1) for half in packed]
    pieces = group_exchange(packed, orbs)
    where = jnp.stack([group_first, ((space + 1) % spaces * orbs + orb) * count, orb])
    near, far, index = forward_pairs(where, offsets, pieces, incoming, count, grid_cells)
    near = lax.all_to_all(near, "orb", split_axis=0, concat_axis=0, tiled=True)
    far = along_space(far, 1)
    field = group_pairs(
        where, offsets, pair_left[0, 0], send_index[0, 0], index, pieces, count, grid_cells
    )
    return finish(field, near, far, pair_left[0, 1])


def solution(mesh):
    split = P(("space", "orb"), None, None)
    return jax.shard_map(
        per_device, mesh=mesh, in_specs=(split, P(), split, split), out_specs=split,
        check_vma=False,
    )
```

```python
import functools

import jax
import jax.numpy as jnp
from jax import lax
from jax.experimental import pallas as pl
from jax.experimental.pallas import tpu as pltpu
from jax.sharding import PartitionSpec as P

B = 40
ITERS = 4
SCREEN = 0.25

GROUPS = 3
TILES = 14
LANES = 128
USED = GROUPS * B
SUB = 8
PLANES = B // SUB
CELLS = TILES * PLANES
CELL = 2 * SUB
HALF = B // 2
VMEM_BYTES = 52 * 2**20
FIELDS = 8


def lanes_of(shape):
    return lax.broadcasted_iota(jnp.int32, shape, len(shape) - 1)


def overlaps():
    pieces = []
    for b in range(B):
        group = b // TILES
        for flat in range(b * B // LANES, (b * B + B - 1) // LANES + 1):
            pieces.append((b, flat, b * B - flat * LANES - group * B))
    return pieces


def index_table(refs):
    free = LANES - USED
    rows = []
    for ref in refs:
        entries = ref[0].astype(jnp.float32)
        for g in range(2):
            for start in range(0, entries.shape[1], free):
                part = entries[g : g + 1, start : start + free]
                rows.append(jnp.concatenate([jnp.zeros((1, USED), jnp.float32), part], axis=1))
    return jnp.concatenate(rows + [jnp.zeros((B - len(rows), LANES), jnp.float32)], axis=0)


def pack_body(box_ref, send_ref, left_ref, first_ref, second_ref, stage):
    count = box_ref.shape[0]
    lane = lanes_of((B, LANES))
    for n in range(count):
        tiles = [jnp.zeros((B, LANES), jnp.float32) for _ in range(TILES)]
        loaded = {}
        for b, flat, shift in overlaps():
            if flat not in loaded:
                width = min(LANES, B * B - flat * LANES)
                part = box_ref[n, :, flat * LANES : flat * LANES + width].astype(jnp.float32)
                if width < LANES:
                    part = jnp.concatenate(
                        [part, jnp.zeros((B, LANES - width), jnp.float32)], axis=1
                    )
                stage[flat] = part
                loaded[flat] = jnp.concatenate(
                    [stage[flat, pl.ds(p, SUB, stride=PLANES), :] for p in range(PLANES)], axis=0
                )
            first = max(b * B, flat * LANES) - b * B + (b // TILES) * B
            last = min(b * B + B, flat * LANES + LANES) - b * B + (b // TILES) * B
            moved = pltpu.roll(loaded[flat], (-shift) % LANES, axis=1)
            keep = (lane >= first) & (lane < last)
            tiles[b % TILES] = jnp.where(keep, moved, tiles[b % TILES])
        if n == 0:
            tiles[0] = tiles[0] + index_table((send_ref, left_ref))
        out_ref = first_ref if n < count // 2 else second_ref
        for t in range(TILES):
            out_ref[n % (count // 2), t] = tiles[t].astype(out_ref.dtype)


def pack(orbitals, send_index, pair_left):
    count = orbitals.shape[0]
    return pl.pallas_call(
        pack_body,
        out_shape=[jax.ShapeDtypeStruct((count // 2, TILES, B, LANES), jnp.bfloat16)] * 2,
        in_specs=[pl.BlockSpec(memory_space=pltpu.VMEM)] * 3,
        out_specs=[pl.BlockSpec(memory_space=pltpu.VMEM)] * 2,
        scratch_shapes=[pltpu.VMEM((-(-B * B // LANES), B, LANES), jnp.float32)],
        compiler_params=pltpu.CompilerParams(vmem_limit_bytes=VMEM_BYTES),
        name="pack",
    )(orbitals, send_index, pair_left)


def finish_body(field_ref, near_ref, far_ref, row_ref, out_ref, total, near, far, made, stage, *sems):
    count, slots = field_ref.shape[0], near_ref.shape[0]
    field_sem, near_sem, far_sem, out_sem = sems

    def copy(source, target, sem):
        made = pltpu.make_async_copy(source, target, sem)
        made.start()
        return made

    fields = [copy(field_ref.at[n], total.at[n], field_sem.at[n]) for n in range(count)]
    fars = [copy(far_ref.at[n], far.at[n], far_sem.at[n]) for n in range(count)]
    nears = [copy(near_ref.at[j], near.at[j], near_sem.at[j]) for j in range(slots)]
    for n in range(count):
        fields[n].wait()
        fars[n].wait()
        for t in range(TILES):
            total[n, t] += far[n, t].astype(jnp.float32)
    for j in range(slots):
        nears[j].wait()
        row = row_ref[j]
        for t in range(TILES):
            total[row, t] += near[j, t].astype(jnp.float32)
    lane = lanes_of((B, LANES))
    sent = []
    for n in range(count):
        flats = {}
        for b, flat, shift in overlaps():
            first = max(b * B, flat * LANES) - flat * LANES
            last = min(b * B + B, flat * LANES + LANES) - flat * LANES
            moved = pltpu.roll(total[n, b % TILES], shift % LANES, axis=1)
            keep = (lane >= first) & (lane < last)
            before = flats.get(flat)
            flats[flat] = moved if before is None else jnp.where(keep, moved, before)
        for flat, value in flats.items():
            for p in range(PLANES):
                stage[flat, pl.ds(p, SUB, stride=PLANES), :] = value[p * SUB : p * SUB + SUB]
            width = min(LANES, B * B - flat * LANES)
            made[n, :, flat * LANES : flat * LANES + width] = stage[flat, :, :width]
        sent.append(copy(made.at[n], out_ref.at[n], out_sem.at[n]))
    for one in sent:
        one.wait()


def finish(field, near, far, rows):
    count, slots = field.shape[0], near.shape[0]
    left = pl.BlockSpec(memory_space=pltpu.HBM)
    shape = (TILES, B, LANES)
    return pl.pallas_call(
        finish_body,
        out_shape=jax.ShapeDtypeStruct((count, B, B * B), jnp.float32),
        in_specs=[left] * 3 + [pl.BlockSpec(memory_space=pltpu.SMEM)],
        out_specs=left,
        scratch_shapes=[
            pltpu.VMEM((count,) + shape, jnp.float32),
            pltpu.VMEM((slots,) + shape, near.dtype),
            pltpu.VMEM((count,) + shape, far.dtype),
            pltpu.VMEM((count, B, B * B), jnp.float32),
            pltpu.VMEM((-(-B * B // LANES), B, LANES), jnp.float32),
        ] + [pltpu.SemaphoreType.DMA((size,)) for size in (count, slots, count, count)],
        compiler_params=pltpu.CompilerParams(vmem_limit_bytes=VMEM_BYTES),
        name="finish",
    )(field, near, far, rows)


def geometry(offset_ref, left, right, grid_cells):
    shift, live = [], jnp.int32(1)
    for axis in range(3):
        gap = offset_ref[3 * right + axis] - offset_ref[3 * left + axis] + grid_cells // 2
        gap = jnp.where(gap < 0, gap + grid_cells, gap)
        gap = jnp.where(gap >= grid_cells, gap - grid_cells, gap) - grid_cells // 2
        live = jnp.where((gap > HALF) | (gap < -HALF), 0, live)
        shift.append(gap)
    return shift, live


def lane_group(lane):
    return sum(jnp.where(lane >= B * (i + 1), 1, 0) for i in range(GROUPS))


def wrapped(shift, size):
    from_zero = B * size - shift
    quotient = (from_zero * (2**16 // size + 1)) >> 16
    start, turn = from_zero - size * quotient, quotient - B
    pairs = []
    for i in range(size):
        over = jnp.where(start + i >= size, 1, 0)
        pairs.append((start + i - size * over, turn + over))
    return pairs


def put_padded(pad, t, p, value):
    start = (t * PLANES + p) * CELL + SUB
    pad[start : start + SUB, :] = value


def displaced(pad, shift):
    lane = lanes_of((SUB, LANES))
    group = lane_group(lane)
    source_col = lane - group * B - shift[2]
    col_ok = (source_col >= 0) & (source_col < B) & (lane < USED)
    source_row = jnp.where(col_ok, TILES * group - shift[1], -2 * B)
    rows = [p * CELL + SUB + turn for p, turn in wrapped(shift[0], PLANES)]
    for t, (source, turn) in enumerate(wrapped(shift[1], TILES)):
        keep = (source_row + t >= 0) & (source_row + t < B)
        if t >= B - TILES * (GROUPS - 1):
            keep = keep & (lane < USED - B)
        amount = (shift[2] - B * turn + 2 * LANES) & (LANES - 1)
        tile = []
        for p in range(PLANES):
            block = pad[pl.ds(source * (PLANES * CELL) + rows[p], SUB), :]
            tile.append(jnp.where(keep, pltpu.roll(block, amount, axis=1), 0.0))
        yield t, tile


def tree_sum(values):
    while len(values) > 1:
        paired = [a + b for a, b in zip(values[::2], values[1::2])]
        values = paired + ([values[-1]] if len(values) % 2 else [])
    return values[0]


def blocks(value):
    return [value[p * SUB : p * SUB + SUB] for p in range(PLANES)]


def cell(t, p):
    start = (t * PLANES + p) * SUB
    return slice(start, start + SUB)


def make_operator():
    lane = lanes_of((SUB, LANES))
    sublane = lax.broadcasted_iota(jnp.int32, (SUB, LANES), 0)
    column = lane - B * lane_group(lane)
    has_before = (column > 0) & (lane < USED)
    has_after = (column < B - 1) & (lane < USED)
    not_first = lane >= B
    not_last = lane < USED - B
    has_above = sublane > 0
    has_below = sublane < SUB - 1

    def operator(t, before, here, after):
        if t == 0:
            before = [jnp.where(not_first, pltpu.roll(v, B, axis=1), 0.0) for v in before]
        if t == TILES - 1:
            after = [jnp.where(not_last, pltpu.roll(v, LANES - B, axis=1), 0.0) for v in after]
        result = []
        for p in range(PLANES):
            if p == 0:
                above = jnp.where(has_above, pltpu.roll(here[PLANES - 1], 1, axis=0), 0.0)
            else:
                above = here[p - 1]
            if p == PLANES - 1:
                below = jnp.where(has_below, pltpu.roll(here[0], SUB - 1, axis=0), 0.0)
            else:
                below = here[p + 1]
            prior = jnp.where(has_before, pltpu.roll(here[p], 1, axis=1), 0.0)
            following = jnp.where(has_after, pltpu.roll(here[p], LANES - 1, axis=1), 0.0)
            around = (above + below) + (before[p] + after[p]) + (prior + following)
            value = (6.0 + SCREEN) * here[p] - around
            if t == B - TILES * (GROUPS - 1):
                value = jnp.where(not_last, value, 0.0)
            result.append(value)
        return result

    return operator


def side_by_side(first, last, body):
    def pair(i, carry):
        for _ in zip(body(first + 2 * i, 0), body(first + 2 * i + 1, 1)):
            pass
        return carry

    lax.fori_loop(0, (last - first) >> 1, pair, 0)

    @pl.when(((last - first) & 1) == 1)
    def _():
        for _ in body(last - 1, 0):
            pass


def put_sum(sums, kind, m, value):
    sums[kind, pl.ds(m, 1), :] = jnp.sum(value, axis=0, keepdims=True)


def solve(used, directions, residuals, images, sums, steps, ratios):
    operator = make_operator()

    for k in range(ITERS):
        last = k == ITERS - 1
        source = directions[0] if k == 1 else residuals[k % 2]
        target = residuals[(k + 1) % 2]

        def stencil(m, side, k=k, last=last, source=source, target=target):
            squares = []
            if k > 0:
                step = jnp.broadcast_to(steps[k - 1, pl.ds(m, 1), :], (SUB, LANES))
                ratio = jnp.broadcast_to(ratios[pl.ds(m, 1), :], (SUB, LANES))

            def stored(t):
                return [directions[k][m, cell(t, p), :] for p in range(PLANES)]

            def fetch(t):
                if k == 0:
                    return stored(t)
                values, parts = [], []
                for p in range(PLANES):
                    left = source[m, cell(t, p), :] - step * images[(k - 1) % 2][m, cell(t, p), :]
                    if not last:
                        target[m, cell(t, p), :] = left
                    parts.append(left * left)
                    value = left + ratio * directions[k - 1][m, cell(t, p), :]
                    directions[k][m, cell(t, p), :] = value
                    values.append(value)
                squares.append(tree_sum(parts))
                if len(squares) == 2:
                    squares[:] = [squares[0] + squares[1]]
                return values

            before, here = fetch(TILES - 1), fetch(0)
            total = spread = None
            for t in range(TILES):
                after = fetch(t + 1) if t < TILES - 2 else stored((t + 1) % TILES)
                applied = operator(t, before, here, after)
                if not last:
                    for p in range(PLANES):
                        images[k % 2][m, cell(t, p), :] = applied[p]
                    part = tree_sum([x * x for x in applied])
                    spread = part if spread is None else spread + part
                part = tree_sum([x * y for x, y in zip(here, applied)])
                total = part if total is None else total + part
                before, here = here, after
                yield
            put_sum(sums, 1, m, total)
            if not last:
                put_sum(sums, 2, m, spread)
            if k > 0:
                put_sum(sums, 0, m, squares[0])
            yield

        side_by_side(0, used, stencil)
        norm, product, square = (
            jnp.broadcast_to(jnp.sum(sums[kind], axis=1, keepdims=True), sums.shape[1:])
            for kind in range(3)
        )
        step = norm / product
        steps[k] = step
        if not last:
            ratios[...] = jnp.maximum(step * step * square - norm, 0.0) / norm


def run_slots(used, nears, fars, shift_of, left_of, right_of, near_to, far_to, held, scratch):
    pads, shifted, sums, steps, ratios, *boxes = scratch
    residuals, images, directions = boxes[:2], boxes[2:4], boxes[4:]

    def box(row, t):
        return blocks(held[row, t].astype(jnp.float32))

    def load(m, side):
        pad = pads.at[side]
        left, right = left_of(m), right_of(m)
        for t in range(TILES):
            for p, block in enumerate(box(right, t)):
                put_padded(pad, t, p, block)
            yield
        total = None
        for t, moved in displaced(pad, shift_of(m)):
            squares = []
            for p, value in enumerate(box(left, t)):
                shifted[m, cell(t, p), :] = moved[p]
                density = moved[p] * value
                directions[0][m, cell(t, p), :] = density
                squares.append(density * density)
            part = tree_sum(squares)
            total = part if total is None else total + part
            yield
        put_sum(sums, 0, m, total)
        yield

    side_by_side(0, used, load)
    solve(used, directions, residuals, images, sums, steps, ratios)

    def unload(near, far):
        def one(m, side):
            pad = pads.at[side]
            left = left_of(m)
            weights = [
                jnp.broadcast_to(steps[k, pl.ds(m, 1), :], (SUB, LANES)) for k in range(ITERS)
            ]
            put_near = near_to(m) if near else None
            put_far = far_to(m) if far else None
            for t in range(TILES):
                solved = [
                    tree_sum([w * d[m, cell(t, p), :] for w, d in zip(weights, directions)])
                    for p in range(PLANES)
                ]
                if near:
                    terms = [v * shifted[m, cell(t, p), :] for p, v in enumerate(solved)]
                    put_near(t, jnp.concatenate(terms, axis=0))
                if far:
                    for p, value in enumerate(box(left, t)):
                        put_padded(pad, t, p, solved[p] * value)
                yield
            if far:
                for t, moved in displaced(pad, [-s for s in shift_of(m)]):
                    put_far(t, jnp.concatenate(moved, axis=0))
                    yield

        return one

    if nears is fars:
        side_by_side(*nears, unload(True, True))
    else:
        side_by_side(*nears, unload(True, False))
        side_by_side(*fars, unload(False, True))


def slot_scratch(batch):
    row = pltpu.VMEM((batch, LANES), jnp.float32)
    box = pltpu.VMEM((batch, CELLS * SUB, LANES), jnp.float32)
    return [
        pltpu.SMEM((batch * FIELDS,), jnp.int32),
        pltpu.VMEM((2, CELLS * CELL + SUB, LANES), jnp.float32),
        box,
        pltpu.VMEM((3, batch, LANES), jnp.float32),
        pltpu.VMEM((ITERS, batch, LANES), jnp.float32),
        row,
    ] + [box] * (4 + ITERS)


def clear(ref):
    for n in range(ref.shape[0]):
        for t in range(TILES):
            ref[n, t] = jnp.zeros((B, LANES), ref.dtype)


def append(listed, used, values):
    for i, value in enumerate(values):
        listed[used * FIELDS + i] = value


def adding(ref, row):
    def put(t, value):
        ref[row, t] += value

    return put


def piece_copies(pieces, index, held, slot, sem):
    part = pieces[0].shape[0]
    for h, piece in enumerate(pieces):

        @pl.when((index >= h * part) & (index < (h + 1) * part))
        def _(h=h, piece=piece):
            pltpu.make_async_copy(piece.at[index - h * part], held.at[slot], sem).start()


def wait_box(pieces, held, slot, sem):
    pltpu.make_async_copy(pieces[0].at[0], held.at[slot], sem).wait()


def read_tables(meta, orbs, me, count, index_ref):
    free = LANES - USED
    lines = orbs // free
    bits = count.bit_length() - 1
    row = lax.broadcasted_iota(jnp.int32, (B, LANES), 0)
    lane = lanes_of((B, LANES)) - USED

    def digits(value, length):
        value = value.astype(jnp.int32)
        for _ in range(length):
            rest = value >> bits if count == 1 << bits else lax.div(value, count)
            yield value - rest * count
            value = rest

    weight = jnp.zeros((B, LANES), jnp.float32)
    for place, kind in enumerate((0, 2, 3)):
        chosen = (row - kind * lines) * free + lane == me
        chosen = chosen & (lane >= 0)
        weight = jnp.where(chosen, float(count**place), weight)
    for k in range(orbs):
        source = jnp.bitwise_xor(me, k)
        total = jnp.sum(meta[k].astype(jnp.float32) * weight)
        for kind, value in enumerate(digits(total, 3)):
            index_ref[kind * orbs + source] = value
    weight = jnp.zeros((B, LANES), jnp.float32)
    for place in range(free):
        weight = jnp.where(lane == place, float(count**place), weight)
    arrived = meta[orbs].astype(jnp.float32) * weight
    for line in range(lines):
        total = jnp.sum(jnp.where(row == lines + line, arrived, 0.0))
        for place, value in enumerate(digits(total, free)):
            index_ref[3 * orbs + line * free + place] = value


def forward_body(orbs, count, grid_cells, where_ref, offset_ref, *refs):
    pieces = [refs[2 * k : 2 * k + 2] for k in range(orbs)]
    incoming = refs[2 * orbs : 2 * orbs + 2]
    near_ref, far_ref, index_ref, meta, held, far_sum, meta_sem, box_sem, listed = refs[
        2 * orbs + 2 : 2 * orbs + 11
    ]
    scratch = refs[2 * orbs + 11 :]
    batch = listed.shape[0] // FIELDS
    part = count // 2
    me = where_ref[2]
    first_left, first_right = where_ref[0], where_ref[1]

    tables = [
        pltpu.make_async_copy(source[0].at[0, 0], meta.at[k], meta_sem.at[k])
        for k, source in enumerate(pieces + [incoming])
    ]
    for copy in tables:
        copy.start()
    rights = [
        pltpu.make_async_copy(
            incoming[n // part].at[n % part], held.at[orbs + n], box_sem.at[orbs + n]
        )
        for n in range(count)
    ]
    for copy in rights:
        copy.start()
    scratch[0][...] = jnp.zeros(scratch[0].shape, jnp.float32)
    clear(far_sum)
    for copy in tables:
        copy.wait()
    read_tables(meta, orbs, me, count, index_ref)
    for k in range(orbs):
        source = jnp.bitwise_xor(me, k)
        piece_copies(pieces[k], index_ref[2 * orbs + source], held, source, box_sem.at[k])

    def run(i, carry):
        def gather(j, used):
            slot = i * batch + j
            left, right = slot * count + index_ref[2 * orbs + slot], index_ref[3 * orbs + slot]
            shift, live = geometry(
                offset_ref, first_left + left, first_right + right, grid_cells
            )

            @pl.when(live == 1)
            def _():
                append(listed, used, [slot, orbs + right, *shift])

            @pl.when(live == 0)
            def _():
                for t in range(TILES):
                    near_ref[slot, t] = jnp.zeros((B, LANES), near_ref.dtype)

            return used + live

        used = lax.fori_loop(0, batch, gather, jnp.int32(0))

        @pl.when(i == 0)
        def _():
            for k in range(orbs):
                wait_box(pieces[k], held, jnp.bitwise_xor(me, k), box_sem.at[k])
            for copy in rights:
                copy.wait()

        def shift_of(m):
            return [listed[m * FIELDS + 2 + axis] for axis in range(3)]

        def near_to(m):
            row = listed[m * FIELDS]

            def put(t, value):
                near_ref[row, t] = value.astype(near_ref.dtype)

            return put

        def far_to(m):
            return adding(far_sum, listed[m * FIELDS + 1] - orbs)

        every = (0, used)
        run_slots(
            used, every, every, shift_of,
            lambda m: listed[m * FIELDS], lambda m: listed[m * FIELDS + 1],
            near_to, far_to, held, scratch,
        )
        return carry

    lax.fori_loop(0, orbs // batch, run, 0)
    for n in range(count):
        for t in range(TILES):
            far_ref[n, t] = far_sum[n, t].astype(far_ref.dtype)


def forward_pairs(where, offsets, pieces, incoming, count, grid_cells):
    orbs = len(pieces)
    vmem, smem, left = (pl.BlockSpec(memory_space=m) for m in (pltpu.VMEM, pltpu.SMEM, pl.ANY))
    shape = (TILES, B, LANES)
    return pl.pallas_call(
        functools.partial(forward_body, orbs, count, grid_cells),
        out_shape=(
            jax.ShapeDtypeStruct((orbs,) + shape, jnp.bfloat16),
            jax.ShapeDtypeStruct((count,) + shape, jnp.bfloat16),
            jax.ShapeDtypeStruct((4 * orbs,), jnp.int32),
        ),
        in_specs=[smem] * 2 + [left] * (2 * orbs + 2),
        out_specs=(vmem, vmem, smem),
        scratch_shapes=[
            pltpu.VMEM((orbs + 1, B, LANES), jnp.bfloat16),
            pltpu.VMEM((orbs + count,) + shape, jnp.bfloat16),
            pltpu.VMEM((count,) + shape, jnp.float32),
            pltpu.SemaphoreType.DMA((orbs + 1,)),
            pltpu.SemaphoreType.DMA((orbs + count,)),
        ] + slot_scratch(8),
        compiler_params=pltpu.CompilerParams(vmem_limit_bytes=VMEM_BYTES),
        name="forward_pairs",
    )(where, offsets, *[half for piece in pieces for half in piece], *incoming)


def group_body(orbs, count, grid_cells, where_ref, offset_ref, mine_ref, sent_ref, index_ref, *refs):
    pieces = [refs[2 * k : 2 * k + 2] for k in range(orbs)]
    field, held, sem, listed = refs[2 * orbs : 2 * orbs + 4]
    scratch = refs[2 * orbs + 4 :]
    half = listed.shape[0] // FIELDS // 2
    part = count // 2
    first, me = where_ref[0], where_ref[2]
    mine = me * count
    own = 2 * orbs

    for k in range(orbs):
        source = jnp.bitwise_xor(me, k)
        piece_copies(pieces[k], index_ref[source], held, source, sem.at[k])
        piece_copies(pieces[k], index_ref[orbs + source], held, orbs + source, sem.at[orbs + k])
    owned = [
        pltpu.make_async_copy(pieces[0][n // part].at[n % part], held.at[own + n], sem.at[own + n])
        for n in range(count)
    ]
    for copy in owned:
        copy.start()
    scratch[0][...] = jnp.zeros(scratch[0].shape, jnp.float32)
    clear(field)

    def run(i, carry):
        def listing(near):
            def gather(j, used):
                slot = i * half + ((me + 1 + j) & (half - 1))
                if near:
                    left, right = mine + mine_ref[slot], slot * count + index_ref[slot]
                    boxes = [own + mine_ref[slot], slot]
                else:
                    left, right = slot * count + index_ref[orbs + slot], mine + sent_ref[slot]
                    boxes = [orbs + slot, own + sent_ref[slot]]
                shift, live = geometry(offset_ref, first + left, first + right, grid_cells)
                if not near:
                    live = jnp.where(slot == me, 0, live)
                else:
                    boxes[1] = jnp.where(slot == me, own + index_ref[slot], boxes[1])

                @pl.when(live == 1)
                def _():
                    append(listed, used, boxes + [*shift])

                return used + live

            return gather

        near_count = lax.fori_loop(0, half, listing(True), jnp.int32(0))
        used = lax.fori_loop(0, half, listing(False), near_count)
        left, right = mine + mine_ref[me], mine + index_ref[me]
        inside = geometry(offset_ref, first + left, first + right, grid_cells)[1]
        inside = jnp.where((me >= i * half) & (me < (i + 1) * half), inside, 0)

        @pl.when(i == 0)
        def _():
            for k in range(orbs):
                source = jnp.bitwise_xor(me, k)
                wait_box(pieces[k], held, source, sem.at[k])
                wait_box(pieces[k], held, orbs + source, sem.at[orbs + k])
            for copy in owned:
                copy.wait()

        def shift_of(m):
            return [listed[m * FIELDS + 2 + axis] for axis in range(3)]

        def near_to(m):
            return adding(field, listed[m * FIELDS] - own)

        def far_to(m):
            return adding(field, listed[m * FIELDS + 1] - own)

        run_slots(
            used, (0, near_count), (near_count - inside, used), shift_of,
            lambda m: listed[m * FIELDS], lambda m: listed[m * FIELDS + 1],
            near_to, far_to, held, scratch,
        )
        return carry

    lax.fori_loop(0, orbs // half, run, 0)


def group_pairs(where, offsets, mine, sent, index, pieces, count, grid_cells):
    orbs = len(pieces)
    vmem, smem, left = (pl.BlockSpec(memory_space=m) for m in (pltpu.VMEM, pltpu.SMEM, pl.ANY))
    shape = (TILES, B, LANES)
    return pl.pallas_call(
        functools.partial(group_body, orbs, count, grid_cells),
        out_shape=jax.ShapeDtypeStruct((count,) + shape, jnp.float32),
        in_specs=[smem] * 5 + [left] * (2 * orbs),
        out_specs=vmem,
        scratch_shapes=[
            pltpu.VMEM((2 * orbs + count,) + shape, jnp.bfloat16),
            pltpu.SemaphoreType.DMA((2 * orbs + count,)),
        ] + slot_scratch(16),
        compiler_params=pltpu.CompilerParams(vmem_limit_bytes=VMEM_BYTES),
        name="group_pairs",
    )(where, offsets, mine, sent, index, *[half for piece in pieces for half in piece])


def along_space(block, distance):
    size = lax.axis_size("space")
    return lax.ppermute(block, "space", [((i - distance) % size, i) for i in range(size)])


def group_exchange(packed, orbs):
    bits = [1 << i for i in range(orbs.bit_length() - 1)]
    orders = (bits[1:] + bits[:1], bits[:0:-1] + bits[:1])
    halves = []
    for block, order in zip(packed, orders):
        known = {0: block}
        for bit in order:
            route = [(i, i ^ bit) for i in range(orbs)]
            for k in list(known):
                known[k ^ bit] = lax.ppermute(known[k], "orb", route)
        halves.append(known)
    return [[known[k] for known in halves] for k in range(orbs)]


def per_device(orbitals, box_offset, send_index, pair_left):
    count = orbitals.shape[0]
    spaces, orbs = lax.axis_size("space"), lax.axis_size("orb")
    grid_cells = spaces * HALF
    space, orb = lax.axis_index("space"), lax.axis_index("orb")
    group_first = space * orbs * count
    offsets = box_offset.reshape(-1)

    packed = pack(orbitals, send_index, pair_left)

    incoming = [along_space(half, -1) for half in packed]
    pieces = group_exchange(packed, orbs)
    where = jnp.stack([group_first, ((space + 1) % spaces * orbs + orb) * count, orb])
    near, far, index = forward_pairs(where, offsets, pieces, incoming, count, grid_cells)
    near = lax.all_to_all(near, "orb", split_axis=0, concat_axis=0, tiled=True)
    far = along_space(far, 1)
    field = group_pairs(
        where, offsets, pair_left[0, 0], send_index[0, 0], index, pieces, count, grid_cells
    )
    return finish(field, near, far, pair_left[0, 1])


def solution(mesh):
    split = P(("space", "orb"), None, None)
    return jax.shard_map(
        per_device, mesh=mesh, in_specs=(split, P(), split, split), out_specs=split,
        check_vma=False,
    )
```

```python
import functools

import jax
import jax.numpy as jnp
from jax import lax
from jax.experimental import pallas as pl
from jax.experimental.pallas import tpu as pltpu
from jax.sharding import PartitionSpec as P

B = 40
ITERS = 4
SCREEN = 0.25

GROUPS = 3
TILES = 14
LANES = 128
USED = GROUPS * B
SUB = 8
PLANES = B // SUB
CELLS = TILES * PLANES
CELL = 2 * SUB
HALF = B // 2
VMEM_BYTES = 52 * 2**20
FIELDS = 8


def lanes_of(shape):
    return lax.broadcasted_iota(jnp.int32, shape, len(shape) - 1)


def overlaps():
    pieces = []
    for b in range(B):
        group = b // TILES
        for flat in range(b * B // LANES, (b * B + B - 1) // LANES + 1):
            pieces.append((b, flat, b * B - flat * LANES - group * B))
    return pieces


def pack_body(box_ref, table_ref, whole_ref, first_ref, second_ref, stage):
    count = box_ref.shape[0]
    lane = lanes_of((B, LANES))
    for n in range(count):
        tiles = [jnp.zeros((B, LANES), jnp.float32) for _ in range(TILES)]
        loaded = {}
        for b, flat, shift in overlaps():
            if flat not in loaded:
                width = min(LANES, B * B - flat * LANES)
                part = box_ref[n, :, flat * LANES : flat * LANES + width].astype(jnp.float32)
                if width < LANES:
                    part = jnp.concatenate(
                        [part, jnp.zeros((B, LANES - width), jnp.float32)], axis=1
                    )
                stage[flat] = part
                loaded[flat] = jnp.concatenate(
                    [stage[flat, pl.ds(p, SUB, stride=PLANES), :] for p in range(PLANES)], axis=0
                )
            first = max(b * B, flat * LANES) - b * B + (b // TILES) * B
            last = min(b * B + B, flat * LANES + LANES) - b * B + (b // TILES) * B
            moved = pltpu.roll(loaded[flat], (-shift) % LANES, axis=1)
            keep = (lane >= first) & (lane < last)
            tiles[b % TILES] = jnp.where(keep, moved, tiles[b % TILES])
        if n == 0:
            tiles[0] = tiles[0] + table_ref[...]
        out_ref = first_ref if n < count // 2 else second_ref
        for t in range(TILES):
            value = tiles[t].astype(out_ref.dtype)
            whole_ref[n, t] = value
            out_ref[n % (count // 2), t] = value


def pack(orbitals, table):
    count = orbitals.shape[0]
    return pl.pallas_call(
        pack_body,
        out_shape=[
            jax.ShapeDtypeStruct((size, TILES, B, LANES), jnp.bfloat16)
            for size in (count, count // 2, count // 2)
        ],
        in_specs=[pl.BlockSpec(memory_space=pltpu.VMEM)] * 2,
        out_specs=[pl.BlockSpec(memory_space=pltpu.VMEM)] * 3,
        scratch_shapes=[pltpu.VMEM((-(-B * B // LANES), B, LANES), jnp.float32)],
        compiler_params=pltpu.CompilerParams(vmem_limit_bytes=VMEM_BYTES),
        name="pack",
    )(orbitals, table)


def finish_body(count, slots, field_ref, near_ref, far_ref, row_ref, out_ref, total, stage):
    lane = lanes_of((B, LANES))
    for n in range(count):
        for t in range(TILES):
            total[n, t] = field_ref[n, t] + far_ref[n, t].astype(jnp.float32)

    def add(j, carry):
        row = row_ref[j]
        for t in range(TILES):
            total[row, t] += near_ref[j, t].astype(jnp.float32)
        return carry

    lax.fori_loop(0, slots, add, 0)
    for n in range(count):
        flats = {}
        for b, flat, shift in overlaps():
            first = max(b * B, flat * LANES) - flat * LANES
            last = min(b * B + B, flat * LANES + LANES) - flat * LANES
            moved = pltpu.roll(total[n, b % TILES], shift % LANES, axis=1)
            keep = (lane >= first) & (lane < last)
            before = flats.get(flat)
            flats[flat] = moved if before is None else jnp.where(keep, moved, before)
        for flat, value in flats.items():
            for p in range(PLANES):
                stage[flat, pl.ds(p, SUB, stride=PLANES), :] = value[p * SUB : p * SUB + SUB]
            width = min(LANES, B * B - flat * LANES)
            out_ref[n, :, flat * LANES : flat * LANES + width] = stage[flat, :, :width]


def finish(field, near, far, rows):
    count, slots = field.shape[0], near.shape[0]
    vmem = pl.BlockSpec(memory_space=pltpu.VMEM)
    return pl.pallas_call(
        functools.partial(finish_body, count, slots),
        out_shape=jax.ShapeDtypeStruct((count, B, B * B), jnp.float32),
        in_specs=[vmem, vmem, vmem, pl.BlockSpec(memory_space=pltpu.SMEM)],
        out_specs=vmem,
        scratch_shapes=[
            pltpu.VMEM((count, TILES, B, LANES), jnp.float32),
            pltpu.VMEM((-(-B * B // LANES), B, LANES), jnp.float32),
        ],
        compiler_params=pltpu.CompilerParams(vmem_limit_bytes=VMEM_BYTES),
        name="finish",
    )(field, near, far, rows)


def geometry(offset_ref, left, right, grid_cells):
    shift, live = [], jnp.int32(1)
    for axis in range(3):
        gap = offset_ref[3 * right + axis] - offset_ref[3 * left + axis] + grid_cells // 2
        gap = jnp.where(gap < 0, gap + grid_cells, gap)
        gap = jnp.where(gap >= grid_cells, gap - grid_cells, gap) - grid_cells // 2
        live = jnp.where((gap > HALF) | (gap < -HALF), 0, live)
        shift.append(gap)
    return shift, live


def lane_group(lane):
    return sum(jnp.where(lane >= B * (i + 1), 1, 0) for i in range(GROUPS))


def wrapped(shift, size):
    from_zero = B * size - shift
    quotient = (from_zero * (2**16 // size + 1)) >> 16
    start, turn = from_zero - size * quotient, quotient - B
    pairs = []
    for i in range(size):
        over = jnp.where(start + i >= size, 1, 0)
        pairs.append((start + i - size * over, turn + over))
    return pairs


def put_padded(pad, t, p, value):
    start = (t * PLANES + p) * CELL + SUB
    pad[start : start + SUB, :] = value


def displaced(pad, shift):
    lane = lanes_of((SUB, LANES))
    group = lane_group(lane)
    source_col = lane - group * B - shift[2]
    col_ok = (source_col >= 0) & (source_col < B) & (lane < USED)
    source_row = jnp.where(col_ok, TILES * group - shift[1], -2 * B)
    rows = [p * CELL + SUB + turn for p, turn in wrapped(shift[0], PLANES)]
    for t, (source, turn) in enumerate(wrapped(shift[1], TILES)):
        keep = (source_row + t >= 0) & (source_row + t < B)
        if t >= B - TILES * (GROUPS - 1):
            keep = keep & (lane < USED - B)
        amount = (shift[2] - B * turn + 2 * LANES) & (LANES - 1)
        tile = []
        for p in range(PLANES):
            block = pad[pl.ds(source * (PLANES * CELL) + rows[p], SUB), :]
            tile.append(jnp.where(keep, pltpu.roll(block, amount, axis=1), 0.0))
        yield t, tile


def tree_sum(values):
    while len(values) > 1:
        paired = [a + b for a, b in zip(values[::2], values[1::2])]
        values = paired + ([values[-1]] if len(values) % 2 else [])
    return values[0]


def blocks(value):
    return [value[p * SUB : p * SUB + SUB] for p in range(PLANES)]


def cell(t, p):
    start = (t * PLANES + p) * SUB
    return slice(start, start + SUB)


def make_operator():
    lane = lanes_of((SUB, LANES))
    sublane = lax.broadcasted_iota(jnp.int32, (SUB, LANES), 0)
    column = lane - B * lane_group(lane)
    has_before = (column > 0) & (lane < USED)
    has_after = (column < B - 1) & (lane < USED)
    not_first = lane >= B
    not_last = lane < USED - B
    has_above = sublane > 0
    has_below = sublane < SUB - 1

    def operator(t, before, here, after):
        if t == 0:
            before = [jnp.where(not_first, pltpu.roll(v, B, axis=1), 0.0) for v in before]
        if t == TILES - 1:
            after = [jnp.where(not_last, pltpu.roll(v, LANES - B, axis=1), 0.0) for v in after]
        result = []
        for p in range(PLANES):
            if p == 0:
                above = jnp.where(has_above, pltpu.roll(here[PLANES - 1], 1, axis=0), 0.0)
            else:
                above = here[p - 1]
            if p == PLANES - 1:
                below = jnp.where(has_below, pltpu.roll(here[0], SUB - 1, axis=0), 0.0)
            else:
                below = here[p + 1]
            prior = jnp.where(has_before, pltpu.roll(here[p], 1, axis=1), 0.0)
            following = jnp.where(has_after, pltpu.roll(here[p], LANES - 1, axis=1), 0.0)
            around = (above + below) + (before[p] + after[p]) + (prior + following)
            value = (6.0 + SCREEN) * here[p] - around
            if t == B - TILES * (GROUPS - 1):
                value = jnp.where(not_last, value, 0.0)
            result.append(value)
        return result

    return operator


def side_by_side(first, last, body):
    def pair(i, carry):
        for _ in zip(body(first + 2 * i, 0), body(first + 2 * i + 1, 1)):
            pass
        return carry

    lax.fori_loop(0, (last - first) >> 1, pair, 0)

    @pl.when(((last - first) & 1) == 1)
    def _():
        for _ in body(last - 1, 0):
            pass


def put_sum(sums, kind, m, value):
    sums[kind, pl.ds(m, 1), :] = jnp.sum(value, axis=0, keepdims=True)


def solve(used, directions, residuals, images, sums, steps, ratios):
    operator = make_operator()

    for k in range(ITERS):
        last = k == ITERS - 1
        source = directions[0] if k == 1 else residuals[k % 2]
        target = residuals[(k + 1) % 2]

        def stencil(m, side, k=k, last=last, source=source, target=target):
            squares = []
            if k > 0:
                step = jnp.broadcast_to(steps[k - 1, pl.ds(m, 1), :], (SUB, LANES))
                ratio = jnp.broadcast_to(ratios[pl.ds(m, 1), :], (SUB, LANES))

            def stored(t):
                return [directions[k][m, cell(t, p), :] for p in range(PLANES)]

            def fetch(t):
                if k == 0:
                    return stored(t)
                values, parts = [], []
                for p in range(PLANES):
                    left = source[m, cell(t, p), :] - step * images[(k - 1) % 2][m, cell(t, p), :]
                    if not last:
                        target[m, cell(t, p), :] = left
                    parts.append(left * left)
                    value = left + ratio * directions[k - 1][m, cell(t, p), :]
                    directions[k][m, cell(t, p), :] = value
                    values.append(value)
                squares.append(tree_sum(parts))
                if len(squares) == 2:
                    squares[:] = [squares[0] + squares[1]]
                return values

            before, here = fetch(TILES - 1), fetch(0)
            total = spread = None
            for t in range(TILES):
                after = fetch(t + 1) if t < TILES - 2 else stored((t + 1) % TILES)
                applied = operator(t, before, here, after)
                if not last:
                    for p in range(PLANES):
                        images[k % 2][m, cell(t, p), :] = applied[p]
                    part = tree_sum([x * x for x in applied])
                    spread = part if spread is None else spread + part
                part = tree_sum([x * y for x, y in zip(here, applied)])
                total = part if total is None else total + part
                before, here = here, after
                yield
            put_sum(sums, 1, m, total)
            if not last:
                put_sum(sums, 2, m, spread)
            if k > 0:
                put_sum(sums, 0, m, squares[0])
            yield

        side_by_side(0, used, stencil)
        norm, product, square = (
            jnp.broadcast_to(jnp.sum(sums[kind], axis=1, keepdims=True), sums.shape[1:])
            for kind in range(3)
        )
        step = norm / product
        steps[k] = step
        if not last:
            ratios[...] = jnp.maximum(step * step * square - norm, 0.0) / norm


def run_slots(used, nears, fars, shift_of, left_of, right_of, near_to, far_to, held, scratch):
    pads, shifted, sums, steps, ratios, *boxes = scratch
    residuals, images, directions = boxes[:2], boxes[2:4], boxes[4:]

    def box(row, t):
        return blocks(held[row, t].astype(jnp.float32))

    def load(m, side):
        pad = pads.at[side]
        left, right = left_of(m), right_of(m)
        for t in range(TILES):
            for p, block in enumerate(box(right, t)):
                put_padded(pad, t, p, block)
            yield
        total = None
        for t, moved in displaced(pad, shift_of(m)):
            squares = []
            for p, value in enumerate(box(left, t)):
                shifted[m, cell(t, p), :] = moved[p]
                density = moved[p] * value
                directions[0][m, cell(t, p), :] = density
                squares.append(density * density)
            part = tree_sum(squares)
            total = part if total is None else total + part
            yield
        put_sum(sums, 0, m, total)
        yield

    side_by_side(0, used, load)
    solve(used, directions, residuals, images, sums, steps, ratios)

    def unload(near, far):
        def one(m, side):
            pad = pads.at[side]
            left = left_of(m)
            weights = [
                jnp.broadcast_to(steps[k, pl.ds(m, 1), :], (SUB, LANES)) for k in range(ITERS)
            ]
            put_near = near_to(m) if near else None
            put_far = far_to(m) if far else None
            for t in range(TILES):
                solved = [
                    tree_sum([w * d[m, cell(t, p), :] for w, d in zip(weights, directions)])
                    for p in range(PLANES)
                ]
                if near:
                    terms = [v * shifted[m, cell(t, p), :] for p, v in enumerate(solved)]
                    put_near(t, jnp.concatenate(terms, axis=0))
                if far:
                    for p, value in enumerate(box(left, t)):
                        put_padded(pad, t, p, solved[p] * value)
                yield
            if far:
                for t, moved in displaced(pad, [-s for s in shift_of(m)]):
                    put_far(t, jnp.concatenate(moved, axis=0))
                    yield

        return one

    if nears is fars:
        side_by_side(*nears, unload(True, True))
    else:
        side_by_side(*nears, unload(True, False))
        side_by_side(*fars, unload(False, True))


def slot_scratch(batch):
    row = pltpu.VMEM((batch, LANES), jnp.float32)
    box = pltpu.VMEM((batch, CELLS * SUB, LANES), jnp.float32)
    return [
        pltpu.SMEM((batch * FIELDS,), jnp.int32),
        pltpu.VMEM((2, CELLS * CELL + SUB, LANES), jnp.float32),
        box,
        pltpu.VMEM((3, batch, LANES), jnp.float32),
        pltpu.VMEM((ITERS, batch, LANES), jnp.float32),
        row,
    ] + [box] * (4 + ITERS)


def clear(ref):
    for n in range(ref.shape[0]):
        for t in range(TILES):
            ref[n, t] = jnp.zeros((B, LANES), ref.dtype)


def append(listed, used, values):
    for i, value in enumerate(values):
        listed[used * FIELDS + i] = value


def adding(ref, row):
    def put(t, value):
        ref[row, t] += value

    return put


def piece_copies(pieces, index, held, slot, sem):
    part = pieces[0].shape[0]
    for h, piece in enumerate(pieces):

        @pl.when((index >= h * part) & (index < (h + 1) * part))
        def _(h=h, piece=piece):
            pltpu.make_async_copy(piece.at[index - h * part], held.at[slot], sem).start()


def wait_box(pieces, held, slot, sem):
    pltpu.make_async_copy(pieces[0].at[0], held.at[slot], sem).wait()


def read_tables(meta, orbs, me, count, index_ref):
    free = LANES - USED
    lines = orbs // free
    bits = count.bit_length() - 1
    row = lax.broadcasted_iota(jnp.int32, (B, LANES), 0)
    lane = lanes_of((B, LANES)) - USED

    def digits(value, length):
        value = value.astype(jnp.int32)
        for _ in range(length):
            rest = value >> bits if count == 1 << bits else lax.div(value, count)
            yield value - rest * count
            value = rest

    weight = jnp.zeros((B, LANES), jnp.float32)
    for place, kind in enumerate((0, 2, 3)):
        chosen = (row - kind * lines) * free + lane == me
        chosen = chosen & (lane >= 0)
        weight = jnp.where(chosen, float(count**place), weight)
    for k in range(orbs):
        source = jnp.bitwise_xor(me, k)
        total = jnp.sum(meta[k].astype(jnp.float32) * weight)
        for kind, value in enumerate(digits(total, 3)):
            index_ref[kind * orbs + source] = value
    weight = jnp.zeros((B, LANES), jnp.float32)
    for place in range(free):
        weight = jnp.where(lane == place, float(count**place), weight)
    arrived = meta[orbs].astype(jnp.float32) * weight
    for line in range(lines):
        total = jnp.sum(jnp.where(row == lines + line, arrived, 0.0))
        for place, value in enumerate(digits(total, free)):
            index_ref[3 * orbs + line * free + place] = value


def forward_body(orbs, count, grid_cells, where_ref, offset_ref, *refs):
    pieces = [refs[2 * k : 2 * k + 2] for k in range(orbs)]
    incoming = refs[2 * orbs]
    near_ref, far_ref, index_ref, meta, held, far_sum, meta_sem, box_sem, listed = refs[
        2 * orbs + 1 : 2 * orbs + 10
    ]
    scratch = refs[2 * orbs + 10 :]
    batch = listed.shape[0] // FIELDS
    me = where_ref[2]
    first_left, first_right = where_ref[0], where_ref[1]

    tables = [
        pltpu.make_async_copy(source[0].at[0, 0], meta.at[k], meta_sem.at[k])
        for k, source in enumerate(pieces + [[incoming]])
    ]
    for copy in tables:
        copy.start()
    rights = [
        pltpu.make_async_copy(
            incoming.at[n], held.at[orbs + n], box_sem.at[orbs + n]
        )
        for n in range(count)
    ]
    for copy in rights:
        copy.start()
    scratch[0][...] = jnp.zeros(scratch[0].shape, jnp.float32)
    clear(far_sum)
    for copy in tables:
        copy.wait()
    read_tables(meta, orbs, me, count, index_ref)
    for k in range(orbs):
        source = jnp.bitwise_xor(me, k)
        piece_copies(pieces[k], index_ref[2 * orbs + source], held, source, box_sem.at[k])

    def run(i, carry):
        def gather(j, used):
            slot = i * batch + j
            left, right = slot * count + index_ref[2 * orbs + slot], index_ref[3 * orbs + slot]
            shift, live = geometry(
                offset_ref, first_left + left, first_right + right, grid_cells
            )

            @pl.when(live == 1)
            def _():
                append(listed, used, [slot, orbs + right, *shift])

            @pl.when(live == 0)
            def _():
                for t in range(TILES):
                    near_ref[slot, t] = jnp.zeros((B, LANES), near_ref.dtype)

            return used + live

        used = lax.fori_loop(0, batch, gather, jnp.int32(0))

        @pl.when(i == 0)
        def _():
            for k in range(orbs):
                wait_box(pieces[k], held, jnp.bitwise_xor(me, k), box_sem.at[k])
            for copy in rights:
                copy.wait()

        def shift_of(m):
            return [listed[m * FIELDS + 2 + axis] for axis in range(3)]

        def near_to(m):
            row = listed[m * FIELDS]

            def put(t, value):
                near_ref[row, t] = value.astype(near_ref.dtype)

            return put

        def far_to(m):
            return adding(far_sum, listed[m * FIELDS + 1] - orbs)

        every = (0, used)
        run_slots(
            used, every, every, shift_of,
            lambda m: listed[m * FIELDS], lambda m: listed[m * FIELDS + 1],
            near_to, far_to, held, scratch,
        )
        return carry

    lax.fori_loop(0, orbs // batch, run, 0)
    for n in range(count):
        for t in range(TILES):
            far_ref[n, t] = far_sum[n, t].astype(far_ref.dtype)


def forward_pairs(where, offsets, pieces, incoming, count, grid_cells):
    orbs = len(pieces)
    vmem, smem, left = (pl.BlockSpec(memory_space=m) for m in (pltpu.VMEM, pltpu.SMEM, pl.ANY))
    shape = (TILES, B, LANES)
    return pl.pallas_call(
        functools.partial(forward_body, orbs, count, grid_cells),
        out_shape=(
            jax.ShapeDtypeStruct((orbs,) + shape, jnp.bfloat16),
            jax.ShapeDtypeStruct((count,) + shape, jnp.bfloat16),
            jax.ShapeDtypeStruct((4 * orbs,), jnp.int32),
        ),
        in_specs=[smem] * 2 + [left] * (2 * orbs + 1),
        out_specs=(vmem, vmem, smem),
        scratch_shapes=[
            pltpu.VMEM((orbs + 1, B, LANES), jnp.bfloat16),
            pltpu.VMEM((orbs + count,) + shape, jnp.bfloat16),
            pltpu.VMEM((count,) + shape, jnp.float32),
            pltpu.SemaphoreType.DMA((orbs + 1,)),
            pltpu.SemaphoreType.DMA((orbs + count,)),
        ] + slot_scratch(8),
        compiler_params=pltpu.CompilerParams(vmem_limit_bytes=VMEM_BYTES),
        name="forward_pairs",
    )(where, offsets, *[half for piece in pieces for half in piece], incoming)


def group_body(orbs, count, grid_cells, where_ref, offset_ref, mine_ref, sent_ref, index_ref, *refs):
    pieces = [refs[2 * k : 2 * k + 2] for k in range(orbs)]
    field, held, sem, listed = refs[2 * orbs : 2 * orbs + 4]
    scratch = refs[2 * orbs + 4 :]
    half = listed.shape[0] // FIELDS // 2
    part = count // 2
    first, me = where_ref[0], where_ref[2]
    mine = me * count
    own = 2 * orbs

    for k in range(orbs):
        source = jnp.bitwise_xor(me, k)
        piece_copies(pieces[k], index_ref[source], held, source, sem.at[k])
        piece_copies(pieces[k], index_ref[orbs + source], held, orbs + source, sem.at[orbs + k])
    owned = [
        pltpu.make_async_copy(pieces[0][n // part].at[n % part], held.at[own + n], sem.at[own + n])
        for n in range(count)
    ]
    for copy in owned:
        copy.start()
    scratch[0][...] = jnp.zeros(scratch[0].shape, jnp.float32)
    clear(field)

    def run(i, carry):
        def listing(near):
            def gather(j, used):
                slot = i * half + ((me + 1 + j) & (half - 1))
                if near:
                    left, right = mine + mine_ref[slot], slot * count + index_ref[slot]
                    boxes = [own + mine_ref[slot], slot]
                else:
                    left, right = slot * count + index_ref[orbs + slot], mine + sent_ref[slot]
                    boxes = [orbs + slot, own + sent_ref[slot]]
                shift, live = geometry(offset_ref, first + left, first + right, grid_cells)
                if not near:
                    live = jnp.where(slot == me, 0, live)
                else:
                    boxes[1] = jnp.where(slot == me, own + index_ref[slot], boxes[1])

                @pl.when(live == 1)
                def _():
                    append(listed, used, boxes + [*shift])

                return used + live

            return gather

        near_count = lax.fori_loop(0, half, listing(True), jnp.int32(0))
        used = lax.fori_loop(0, half, listing(False), near_count)
        left, right = mine + mine_ref[me], mine + index_ref[me]
        inside = geometry(offset_ref, first + left, first + right, grid_cells)[1]
        inside = jnp.where((me >= i * half) & (me < (i + 1) * half), inside, 0)

        @pl.when(i == 0)
        def _():
            for k in range(orbs):
                source = jnp.bitwise_xor(me, k)
                wait_box(pieces[k], held, source, sem.at[k])
                wait_box(pieces[k], held, orbs + source, sem.at[orbs + k])
            for copy in owned:
                copy.wait()

        def shift_of(m):
            return [listed[m * FIELDS + 2 + axis] for axis in range(3)]

        def near_to(m):
            return adding(field, listed[m * FIELDS] - own)

        def far_to(m):
            return adding(field, listed[m * FIELDS + 1] - own)

        run_slots(
            used, (0, near_count), (near_count - inside, used), shift_of,
            lambda m: listed[m * FIELDS], lambda m: listed[m * FIELDS + 1],
            near_to, far_to, held, scratch,
        )
        return carry

    lax.fori_loop(0, orbs // half, run, 0)


def group_pairs(where, offsets, mine, sent, index, pieces, count, grid_cells):
    orbs = len(pieces)
    vmem, smem, left = (pl.BlockSpec(memory_space=m) for m in (pltpu.VMEM, pltpu.SMEM, pl.ANY))
    shape = (TILES, B, LANES)
    return pl.pallas_call(
        functools.partial(group_body, orbs, count, grid_cells),
        out_shape=jax.ShapeDtypeStruct((count,) + shape, jnp.float32),
        in_specs=[smem] * 5 + [left] * (2 * orbs),
        out_specs=vmem,
        scratch_shapes=[
            pltpu.VMEM((2 * orbs + count,) + shape, jnp.bfloat16),
            pltpu.SemaphoreType.DMA((2 * orbs + count,)),
        ] + slot_scratch(16),
        compiler_params=pltpu.CompilerParams(vmem_limit_bytes=VMEM_BYTES),
        name="group_pairs",
    )(where, offsets, mine, sent, index, *[half for piece in pieces for half in piece])


def along_space(block, distance):
    size = lax.axis_size("space")
    return lax.ppermute(block, "space", [((i - distance) % size, i) for i in range(size)])


def group_exchange(packed, orbs):
    bits = [1 << i for i in range(orbs.bit_length() - 1)]
    orders = (bits[1:] + bits[:1], bits[:0:-1] + bits[:1])
    halves = []
    for block, order in zip(packed, orders):
        known = {0: block}
        for bit in order:
            route = [(i, i ^ bit) for i in range(orbs)]
            for k in list(known):
                known[k ^ bit] = lax.ppermute(known[k], "orb", route)
        halves.append(known)
    return [[known[k] for known in halves] for k in range(orbs)]


def per_device(orbitals, box_offset, send_index, pair_left):
    count = orbitals.shape[0]
    spaces, orbs = lax.axis_size("space"), lax.axis_size("orb")
    grid_cells = spaces * HALF
    space, orb = lax.axis_index("space"), lax.axis_index("orb")
    group_first = space * orbs * count
    offsets = box_offset.reshape(-1)

    free = LANES - USED
    entries = jnp.concatenate([send_index[0].reshape(-1), pair_left[0].reshape(-1)])
    lines = 4 * orbs // free
    table = jnp.pad(
        entries.astype(jnp.float32).reshape(lines, free), ((0, B - lines), (USED, 0))
    )
    whole, *packed = pack(orbitals, table)

    incoming = along_space(whole, -1)
    pieces = group_exchange(packed, orbs)
    where = jnp.stack([group_first, ((space + 1) % spaces * orbs + orb) * count, orb])
    near, far, index = forward_pairs(where, offsets, pieces, incoming, count, grid_cells)
    near = lax.all_to_all(near, "orb", split_axis=0, concat_axis=0, tiled=True)
    far = along_space(far, 1)
    field = group_pairs(
        where, offsets, pair_left[0, 0], send_index[0, 0], index, pieces, count, grid_cells
    )
    return finish(field, near, far, pair_left[0, 1])


def solution(mesh):
    split = P(("space", "orb"), None, None)
    return jax.shard_map(
        per_device, mesh=mesh, in_specs=(split, P(), split, split), out_specs=split,
        check_vma=False,
    )
```
